32 devices in a mesh: ctx: 16 (over z, y, x), tp: 2 (over core).
Axes of the slice: x: 2, y: 2, z: 4, core: 2. Of those that a mesh axis runs over, the one named last changes fastest.
Arguments:
- layer_cotangent: bfloat16 [4096, 5376], P('ctx', 'tp'), may hold values from -6 to 6
- out_weight: bfloat16 [2048, 5376], P(None, 'tp'), may hold values from -0.078125 to 0.078125
- queries: bfloat16 [4096, 2048], P('ctx', 'tp'), may hold values from -38 to 38
- keys: bfloat16 [4096, 1024], P('ctx', 'tp'), may hold values from -13 to 13
- values: bfloat16 [4096, 1024], P('ctx', 'tp'), may hold values from -6 to 6
Outputs:
- query_grads: bfloat16 [4096, 2048], P('ctx', 'tp')
- key_gradients: bfloat16 [4096, 1024], P('ctx', 'tp')
- value_gradients: bfloat16 [4096, 1024], P('ctx', 'tp')
The draws below stay inside these ranges and needn't reach their ends.
All inputs are finite; a program needn't handle non-finite values.
Results may differ from the reference program's by a relative error of at most 0.03.
Values may be sent and summed in bfloat16 or wider, within the bound.
No kernel may reach another device: no remote copies, remote signals or barrier semaphores. Data moves between devices by JAX's collectives and lax.ppermute only.
A program may use at most 128 MiB of HBM per device.

```python
import jax
import jax.numpy as jnp
from jax import lax

D = 5376
QUERY_HEAD_COUNT = 16
KEY_VALUE_HEADS = 8
HEAD_SIZE = 128
WINDOW_LENGTH = 1024
T_DEV = 256
TOKEN_COUNT = 4096
N_TP = 2


def shared_fields(key):
    key_row_block = jax.random.normal(jax.random.fold_in(key, 11), (TOKEN_COUNT, KEY_VALUE_HEADS, HEAD_SIZE), jnp.float32)
    key_row_block = jnp.clip(key_row_block, -4.0, 4.0)
    key_scale = jnp.exp(jax.random.uniform(jax.random.fold_in(key, 12), (TOKEN_COUNT, 1, 1), jnp.float32, -1.15, 1.15))
    key_row_block = key_row_block * key_scale
    query_rows = jax.random.normal(jax.random.fold_in(key, 13), (TOKEN_COUNT, QUERY_HEAD_COUNT, HEAD_SIZE), jnp.float32)
    query_rows = jnp.clip(query_rows, -4.0, 4.0)
    query_scale = jnp.exp(jax.random.uniform(jax.random.fold_in(key, 14), (TOKEN_COUNT, 1, 1), jnp.float32, -1.15, 1.15))
    query_rows = query_rows * query_scale
    return (query_rows, key_row_block)


def draw_queries(key, part):
    query_rows, key_row_block = shared_fields(key)
    return query_rows.reshape(TOKEN_COUNT, QUERY_HEAD_COUNT * HEAD_SIZE).astype(jnp.bfloat16)


def draw_keys(key, part):
    query_rows, key_row_block = shared_fields(key)
    return key_row_block.reshape(TOKEN_COUNT, KEY_VALUE_HEADS * HEAD_SIZE).astype(jnp.bfloat16)


def block_levels(own_key, dims, pieces, low, largest):
    gain, own = 1.0, jax.random.fold_in(own_key, 6)
    for dim, blocks in pieces:
        draws = jnp.exp(jax.random.uniform(jax.random.fold_in(own, dim), (blocks,), jnp.float32, low / len(pieces), largest / len(pieces)))
        gain = gain * jnp.repeat(draws, dims[dim] // blocks).reshape([-1 if axis == dim else 1 for axis in range(len(dims))])
    return gain


def bell_draw(key, shape, width, bound, split=(), kind=jnp.bfloat16):
    loudness = block_levels(key, shape, split, -0.22, 0.18) if split else 1.0
    values = jax.random.normal(key, shape, jnp.float32) * width * loudness
    return jnp.minimum(jnp.maximum(values, -bound), bound).astype(kind)


def setup_inputs(seed: int = 0) -> dict:
    splits = jax.random.split(jax.random.key(seed), 6)
    return {
        "layer_cotangent": bell_draw(splits[0], (TOKEN_COUNT, D), 1.0, 6.0, ((0, 16), (1, 2))),
        "out_weight": bell_draw(splits[1], (QUERY_HEAD_COUNT * HEAD_SIZE, D), D ** -0.5, 0.078125, ((1, 2),)),
        "queries": draw_queries(jax.random.fold_in(splits[5], 71), 0),
        "keys": draw_keys(jax.random.fold_in(splits[5], 71), 0),
        "values": bell_draw(splits[4], (TOKEN_COUNT, KEY_VALUE_HEADS * HEAD_SIZE), 1.0, 6.0, ((0, 16), (1, 2))),
    }


score_scale = 168.0 ** -0.5


def rounded(term):
    return lax.optimization_barrier(term.astype(jnp.bfloat16)).astype(jnp.float32)


def reference(layer_cotangent, out_weight, queries, keys, values):
    parts = D // N_TP
    query_group = QUERY_HEAD_COUNT // KEY_VALUE_HEADS
    cot_parts = layer_cotangent.reshape(TOKEN_COUNT, N_TP, parts).transpose(1, 0, 2)
    weight_parts = out_weight.reshape(QUERY_HEAD_COUNT * HEAD_SIZE, N_TP, parts).transpose(1, 0, 2)

    def add_part(total, pair):
        term = lax.dot_general(pair[0], pair[1], (((1,), (1,)), ((), ())), preferred_element_type=jnp.float32)
        term = lax.optimization_barrier(term.astype(jnp.bfloat16))
        return total + term.astype(jnp.float32), None

    head_total, unused = lax.scan(add_part, jnp.zeros((TOKEN_COUNT, QUERY_HEAD_COUNT * HEAD_SIZE), jnp.float32), (cot_parts, weight_parts))
    head_gradients = head_total.astype(jnp.bfloat16)

    block = T_DEV
    nblocks = TOKEN_COUNT // block
    query_quad = queries.reshape(TOKEN_COUNT, KEY_VALUE_HEADS, query_group, HEAD_SIZE)
    gradient_quad = head_gradients.reshape(TOKEN_COUNT, KEY_VALUE_HEADS, query_group, HEAD_SIZE)
    padding_rows = jnp.zeros((WINDOW_LENGTH, KEY_VALUE_HEADS, HEAD_SIZE), jnp.bfloat16)
    key_padding = jnp.concatenate([padding_rows, keys.reshape(TOKEN_COUNT, KEY_VALUE_HEADS, HEAD_SIZE)], axis=0)
    value_padding = jnp.concatenate([padding_rows, values.reshape(TOKEN_COUNT, KEY_VALUE_HEADS, HEAD_SIZE)], axis=0)

    def one_block(carry, index):
        key_total, value_total = carry
        start = (index * block).astype(jnp.int32)
        query_blk = lax.dynamic_slice_in_dim(query_quad, start, block, 0).astype(jnp.float32)
        grad_blk = lax.dynamic_slice_in_dim(gradient_quad, start, block, 0).astype(jnp.float32)
        key_blk = lax.dynamic_slice_in_dim(key_padding, start, block + WINDOW_LENGTH, 0).astype(jnp.float32)
        value_blk = lax.dynamic_slice_in_dim(value_padding, start, block + WINDOW_LENGTH, 0).astype(jnp.float32)
        query_pos = start + jnp.arange(block, dtype=jnp.int32)
        key_pos = start - WINDOW_LENGTH + jnp.arange(block + WINDOW_LENGTH, dtype=jnp.int32)
        apart = query_pos[:, None] - key_pos[None, :]
        visible = (apart >= 0) & (apart <= WINDOW_LENGTH - 1) & (key_pos[None, :] >= 0)
        scores = jnp.einsum('qhgd,khd->hgqk', query_blk, key_blk) * score_scale
        scores = jnp.where(visible, scores, -jnp.inf)
        top = jnp.max(scores, axis=-1, keepdims=True)
        expo = jnp.exp(scores - top)
        probs = expo / jnp.sum(expo, axis=-1, keepdims=True)
        probs_low = probs.astype(jnp.bfloat16)
        dprobs = jnp.einsum('qhgd,khd->hgqk', grad_blk, value_blk)
        delta = jnp.sum(probs * dprobs, axis=-1, keepdims=True)
        dscores = (probs * (dprobs - delta) * score_scale).astype(jnp.bfloat16)
        query_part = jnp.einsum('hgqk,khd->qhgd', dscores.astype(jnp.float32), key_blk)
        key_part = jnp.einsum('hgqk,qhgd->khd', dscores.astype(jnp.float32), query_blk)
        value_part = jnp.einsum('hgqk,qhgd->khd', probs_low.astype(jnp.float32), grad_blk)
        key_part = jnp.concatenate([rounded(key_part[:WINDOW_LENGTH]), key_part[WINDOW_LENGTH:]], axis=0)
        value_part = jnp.concatenate([rounded(value_part[:WINDOW_LENGTH]), value_part[WINDOW_LENGTH:]], axis=0)
        key_total = lax.dynamic_update_slice_in_dim(key_total, lax.dynamic_slice_in_dim(key_total, start, block + WINDOW_LENGTH, 0) + key_part, start, 0)
        value_total = lax.dynamic_update_slice_in_dim(value_total, lax.dynamic_slice_in_dim(value_total, start, block + WINDOW_LENGTH, 0) + value_part, start, 0)
        return (key_total, value_total), query_part.astype(jnp.bfloat16)

    zero_padding = jnp.zeros((TOKEN_COUNT + WINDOW_LENGTH, KEY_VALUE_HEADS, HEAD_SIZE), jnp.float32)
    running_totals, query_blocks = lax.scan(one_block, (zero_padding, zero_padding), jnp.arange(nblocks, dtype=jnp.int32))
    query_grads = query_blocks.reshape(TOKEN_COUNT, QUERY_HEAD_COUNT * HEAD_SIZE)
    key_gradients = running_totals[0][WINDOW_LENGTH:].reshape(TOKEN_COUNT, KEY_VALUE_HEADS * HEAD_SIZE).astype(jnp.bfloat16)
    value_gradients = running_totals[1][WINDOW_LENGTH:].reshape(TOKEN_COUNT, KEY_VALUE_HEADS * HEAD_SIZE).astype(jnp.bfloat16)
    return (query_grads, key_gradients, value_gradients)
```

```python
import functools

import jax
import jax.numpy as jnp
from jax import lax
from jax.experimental import pallas as pl
from jax.experimental.pallas import tpu as pltpu
from jax.sharding import PartitionSpec as P

HEAD_SIZE = 128
WINDOW_LENGTH = 1024
LOG2_E = 1.4426950408889634

score_scale = 168.0 ** (-0.5)

VMEM = pl.BlockSpec(memory_space=pltpu.VMEM)
SMEM = pl.BlockSpec(memory_space=pltpu.SMEM)
NT = (((1,), (1,)), ((), ()))
NN = (((1,), (0,)), ((), ()))


def shifted(value, axis, steps):
    count = lax.axis_size(axis)
    leading, last = (max(0, -steps), min(count, count - steps))
    return lax.ppermute(value, axis, [(source, source + steps) for source in range(leading, last)])


def swapped(value, axis, bits):
    count = lax.axis_size(axis)
    return lax.ppermute(value, axis, [(source, source ^ bits) for source in range(count)])


def call(body, outs, scratch=(), flops=0, count=0, exps=0):
    def run(*args):
        moved = sum(a.size * a.dtype.itemsize for a in args)
        moved += sum(o.size * o.dtype.itemsize for o in outs)
        return pl.pallas_call(
            body,
            out_shape=tuple(outs),
            in_specs=[SMEM] + [VMEM] * (len(args) - 1),
            out_specs=tuple(VMEM for _ in outs),
            scratch_shapes=list(scratch),
            compiler_params=pltpu.CompilerParams(vmem_limit_bytes=48 * 1024 * 1024),
            cost_estimate=pl.CostEstimate(flops=flops, bytes_accessed=moved, transcendentals=exps),
        )(*args)

    return run


def lanes(index, width):
    return pl.ds(pl.multiple_of(index * width, width), width)


def pack_inputs(group, ids, keys, values, queries):
    tokens = keys.shape[0]
    kv_width, query_width = keys.shape[1] // group, queries.shape[1] // group

    def body(ids_ref, k_ref, v_ref, q_ref, *out_refs):
        for r in range(group):
            member = ids_ref[0] ^ r
            out_refs[r][:, :kv_width] = k_ref[:, lanes(member, kv_width)]
            out_refs[r][:, kv_width : 2 * kv_width] = v_ref[:, lanes(member, kv_width)]
            out_refs[r][:, 2 * kv_width :] = q_ref[:, lanes(member, query_width)]

    outs = [jax.ShapeDtypeStruct((tokens, 2 * kv_width + query_width), jnp.bfloat16)] * group
    return call(body, outs)(ids, keys, values, queries)


def order_inputs(group, ids, pieces, kv_width):
    tokens, width = pieces[0].shape

    def body(ids_ref, *refs):
        kv_ref, q_ref = refs[group:]
        for r in range(group):
            member = ids_ref[0] ^ r
            kv_ref[member] = refs[r][:, : 2 * kv_width]
            q_ref[member] = refs[r][:, 2 * kv_width :]

    outs = [
        jax.ShapeDtypeStruct((group, tokens, 2 * kv_width), jnp.bfloat16),
        jax.ShapeDtypeStruct((group, tokens, width - 2 * kv_width), jnp.bfloat16),
    ]
    return call(body, outs)(ids, *pieces)


def head_product(start, rows, out_weight, layer_cotangent):
    tokens, depth = layer_cotangent.shape
    tile = min(rows, 256)
    steps = rows // tile

    def body(start_ref, w_ref, c_ref, o_ref):
        o_ref[...] = lax.dot_general(
            w_ref[...], c_ref[...], NT, preferred_element_type=jnp.float32
        ).astype(jnp.bfloat16)

    return pl.pallas_call(
        body,
        out_shape=jax.ShapeDtypeStruct((rows, tokens), jnp.bfloat16),
        grid_spec=pltpu.PrefetchScalarGridSpec(
            num_scalar_prefetch=1,
            grid=(steps,),
            in_specs=[
                pl.BlockSpec((tile, depth), lambda i, s: (s[0] * steps + i, 0)),
                pl.BlockSpec((tokens, depth), lambda i, s: (0, 0)),
            ],
            out_specs=pl.BlockSpec((tile, tokens), lambda i, s: (i, 0)),
        ),
        compiler_params=pltpu.CompilerParams(vmem_limit_bytes=48 * 1024 * 1024),
        cost_estimate=pl.CostEstimate(
            flops=2 * rows * tokens * depth,
            bytes_accessed=2 * (rows * depth + tokens * depth + rows * tokens),
            transcendentals=0,
        ),
    )(start, out_weight, layer_cotangent)


def pack_grads(group, ids, terms):
    rows, tokens = terms[0].shape
    rows //= group

    def body(ids_ref, *refs):
        for r in range(group):
            there = lanes(ids_ref[0] ^ r, rows)
            total = refs[0][there, :]
            if len(terms) > 1:
                total = total.astype(jnp.float32)
                for term in refs[1 : len(terms)]:
                    total = total + term[there, :].astype(jnp.float32)
            refs[len(terms) + r][...] = total.astype(jnp.bfloat16)

    outs = [jax.ShapeDtypeStruct((rows, tokens), jnp.bfloat16)] * group
    return call(body, outs)(ids, *terms)


def attention(group, heads, per_head, ids, kv_own, kv_earlier, queries, grads):
    back = len(kv_earlier) * group
    tokens = kv_own.shape[1]
    span = back + 1
    total = back + group
    wide = per_head * tokens
    kv_width = heads * HEAD_SIZE
    factor = score_scale * LOG2_E

    def body(ids_ref, *refs):
        own_ref = refs[0]
        earlier_refs = refs[1 : 1 + len(kv_earlier)]
        q_ref = refs[1 + len(kv_earlier)]
        grad_refs = refs[2 + len(kv_earlier) : 2 + len(kv_earlier) + group]
        refs = refs[2 + len(kv_earlier) + group :]
        dq_refs, dkv_own, dkv_earlier = refs[:group], refs[group], refs[group + 1 : group + 1 + len(kv_earlier)]
        k_all, kt_all, v_all, g_all, q_all, dq_all, dk_all, dv_all, s_all, dp_all = refs[
            group + 1 + len(kv_earlier) :
        ]
        place, first = ids_ref[0], ids_ref[1]
        key_id = lax.broadcasted_iota(jnp.int32, (tokens, wide), 0)
        query_id = lax.broadcasted_iota(jnp.int32, (tokens, wide), 1) & (tokens - 1)

        for head in range(heads):
            at_k = slice(head * HEAD_SIZE, (head + 1) * HEAD_SIZE)
            at_v = slice(kv_width + head * HEAD_SIZE, kv_width + (head + 1) * HEAD_SIZE)
            for number in range(total):
                if number < back:
                    source = earlier_refs[number // group].at[number % group]
                else:
                    source = own_ref.at[number - back]
                k_all[number] = source[:, at_k]
                kt_all[number] = source[:, at_k].T
                v_all[number] = source[:, at_v]
            for r in range(group):
                for j in range(per_head):
                    lower = (head * per_head + j) * HEAD_SIZE
                    g_all[place ^ r, :, j * tokens : (j + 1) * tokens] = grad_refs[r][
                        lower : lower + HEAD_SIZE, :
                    ]
                    q_all[r, j * tokens : (j + 1) * tokens, :] = q_ref[r, :, lower : lower + HEAD_SIZE]
            dk_all[...] = jnp.zeros_like(dk_all)
            dv_all[...] = jnp.zeros_like(dv_all)

            @pl.loop(0, group)
            def _(b):
                q = q_all[b]
                g = g_all[b]
                top = None
                for c in range(span):
                    s = lax.dot_general(k_all[b + c], q, NT, preferred_element_type=jnp.float32) * factor
                    if c == 0:
                        s = jnp.where(key_id > query_id, s, -jnp.inf)
                    if c < back:
                        s = s + jnp.where(first + b + c >= back, 0.0, -jnp.inf)
                    else:
                        s = jnp.where(key_id <= query_id, s, -jnp.inf)
                    s_all[c] = s
                    here = jnp.max(s, axis=0, keepdims=True)
                    top = here if top is None else jnp.maximum(top, here)
                norm = jnp.zeros((1, wide), jnp.float32)
                delta = jnp.zeros((1, wide), jnp.float32)
                for c in range(span):
                    e = jnp.exp2(s_all[c] - top)
                    dp = lax.dot_general(v_all[b + c], g, NN, preferred_element_type=jnp.float32)
                    norm = norm + jnp.sum(e, axis=0, keepdims=True)
                    delta = delta + jnp.sum(e * dp, axis=0, keepdims=True)
                    s_all[c] = e
                    dp_all[c] = dp
                inverse = 1.0 / norm
                delta = delta * inverse
                dqt = jnp.zeros((HEAD_SIZE, wide), jnp.float32)
                for c in range(span):
                    p = s_all[c] * inverse
                    ds = (p * (dp_all[c] - delta) * score_scale).astype(jnp.bfloat16)
                    p = p.astype(jnp.bfloat16)
                    dv_all[b + c] += lax.dot_general(p, g, NT, preferred_element_type=jnp.float32)
                    dk_all[b + c] += lax.dot_general(ds, q, NN, preferred_element_type=jnp.float32)
                    dqt = dqt + lax.dot_general(kt_all[b + c], ds, NN, preferred_element_type=jnp.float32)
                for j in range(per_head):
                    lower = (head * per_head + j) * HEAD_SIZE
                    dq_all[b, :, lower : lower + HEAD_SIZE] = (
                        dqt[:, j * tokens : (j + 1) * tokens].T.astype(jnp.bfloat16)
                    )

            for number in range(back):
                target = dkv_earlier[number // group].at[number % group]
                target[:, at_k] = dk_all[number].astype(jnp.bfloat16)
                target[:, at_v] = dv_all[number].astype(jnp.bfloat16)
            dkv_own[:, :, at_k] = dk_all[back:]
            dkv_own[:, :, at_v] = dv_all[back:]
        for r in range(group):
            dq_refs[r][...] = dq_all[place ^ r]

    width = heads * per_head * HEAD_SIZE
    outs = [jax.ShapeDtypeStruct((tokens, width), jnp.bfloat16)] * group
    outs += [jax.ShapeDtypeStruct((group, tokens, 2 * kv_width), jnp.float32)]
    outs += [jax.ShapeDtypeStruct((group, tokens, 2 * kv_width), jnp.bfloat16)] * len(kv_earlier)
    scratch = [
        pltpu.VMEM((total, tokens, HEAD_SIZE), jnp.bfloat16),
        pltpu.VMEM((total, HEAD_SIZE, tokens), jnp.bfloat16),
        pltpu.VMEM((total, tokens, HEAD_SIZE), jnp.bfloat16),
        pltpu.VMEM((group, HEAD_SIZE, wide), jnp.bfloat16),
        pltpu.VMEM((group, wide, HEAD_SIZE), jnp.bfloat16),
        pltpu.VMEM((group, tokens, width), jnp.bfloat16),
        pltpu.VMEM((total, tokens, HEAD_SIZE), jnp.float32),
        pltpu.VMEM((total, tokens, HEAD_SIZE), jnp.float32),
        pltpu.VMEM((span, tokens, wide), jnp.float32),
        pltpu.VMEM((span, tokens, wide), jnp.float32),
    ]
    entries = group * heads * wide * span * tokens
    results = call(body, outs, scratch, flops=10 * entries * HEAD_SIZE, exps=entries)(
        ids, kv_own, *kv_earlier, queries, *grads
    )
    return results[:group], results[group], results[group + 1 :]


def pack_kv_grads(group, ids, own, arrived):
    shape = own.shape[1:]

    def body(ids_ref, *refs):
        for r in range(group):
            member = ids_ref[0] ^ r
            total = refs[0][member]
            for term in refs[1 : 1 + len(arrived)]:
                total = total + term[member].astype(jnp.float32)
            refs[1 + len(arrived) + r][...] = total.astype(jnp.bfloat16)

    outs = [jax.ShapeDtypeStruct(shape, jnp.bfloat16)] * group
    return call(body, outs)(ids, own, *arrived)


def unpack(group, ids, pieces, widths):
    tokens = pieces[0].shape[0]

    def body(ids_ref, *refs):
        for r in range(group):
            lower = 0
            for number, width in enumerate(widths):
                refs[group + number][:, lanes(ids_ref[0] ^ r, width)] = refs[r][:, lower : lower + width]
                lower += width

    outs = [jax.ShapeDtypeStruct((tokens, group * width), jnp.bfloat16) for width in widths]
    return call(body, outs)(ids, *pieces)


def local(layer_cotangent, out_weight, queries, keys, values):
    tokens = queries.shape[0]
    kv_heads = keys.shape[1] // HEAD_SIZE
    per_head = queries.shape[1] // keys.shape[1]
    count, tp_count = lax.axis_size("ctx"), lax.axis_size("tp")
    group = 1
    while (
        kv_heads % (2 * group) == 0
        and count % (2 * group) == 0
        and WINDOW_LENGTH % (2 * group * tokens) == 0
    ):
        group *= 2
    heads = kv_heads // group
    kv_width = heads * HEAD_SIZE
    back_groups = WINDOW_LENGTH // (group * tokens)
    index = lax.axis_index("ctx")
    place = index % group
    ids = jnp.stack([place, index - place]).astype(jnp.int32)
    rows = out_weight.shape[0] // tp_count

    sent = pack_inputs(group, ids, keys, values, queries)
    pieces = [sent[0]] + [swapped(sent[r], "ctx", r) for r in range(1, group)]
    if tp_count == 2:
        mine = lax.axis_index("tp").reshape(1)
        other = head_product(1 - mine, rows, out_weight, layer_cotangent)
        terms = [swapped(other, "tp", 1)]
        terms = [head_product(mine, rows, out_weight, layer_cotangent)] + terms
    else:
        product = head_product(jnp.zeros(1, jnp.int32), rows * tp_count, out_weight, layer_cotangent)
        terms = [lax.psum_scatter(product, "tp", scatter_dimension=0, tiled=True)]
    kv_own, query_all = order_inputs(group, ids, pieces, kv_width)
    kv_earlier = [shifted(kv_own, "ctx", group * step) for step in range(back_groups, 0, -1)]
    sent = pack_grads(group, ids, terms)
    grads = [sent[0]] + [swapped(sent[r], "ctx", r) for r in range(1, group)]
    dq, dkv_own, dkv_earlier = attention(
        group, heads, per_head, ids, kv_own, kv_earlier, query_all, grads
    )
    arrived = [
        shifted(dkv_earlier[number], "ctx", -group * (back_groups - number))
        for number in range(back_groups)
    ]
    dq = [dq[0]] + [swapped(dq[r], "ctx", r) for r in range(1, group)]
    sent = pack_kv_grads(group, ids, dkv_own, arrived)
    dkv = [sent[0]] + [swapped(sent[r], "ctx", r) for r in range(1, group)]
    (query_grads,) = unpack(group, ids, dq, [dq[0].shape[1]])
    key_gradients, value_gradients = unpack(group, ids, dkv, [kv_width, kv_width])
    return (query_grads, key_gradients, value_gradients)


def solution(mesh):
    in_specs = (P("ctx", "tp"), P(None, "tp"), P("ctx", "tp"), P("ctx", "tp"), P("ctx", "tp"))
    out_specs = (P("ctx", "tp"), P("ctx", "tp"), P("ctx", "tp"))
    return jax.shard_map(local, mesh=mesh, in_specs=in_specs, out_specs=out_specs, check_vma=False)
```

```python
import functools

import jax
import jax.numpy as jnp
from jax import lax
from jax.experimental import pallas as pl
from jax.experimental.pallas import tpu as pltpu
from jax.sharding import PartitionSpec as P

HEAD_SIZE = 128
WINDOW_LENGTH = 1024
LOG2_E = 1.4426950408889634

score_scale = 168.0 ** (-0.5)

VMEM = pl.BlockSpec(memory_space=pltpu.VMEM)
SMEM = pl.BlockSpec(memory_space=pltpu.SMEM)
NT = (((1,), (1,)), ((), ()))
NN = (((1,), (0,)), ((), ()))


def shifted(value, axis, steps):
    count = lax.axis_size(axis)
    leading, last = (max(0, -steps), min(count, count - steps))
    return lax.ppermute(value, axis, [(source, source + steps) for source in range(leading, last)])


def swapped(value, axis, bits):
    count = lax.axis_size(axis)
    return lax.ppermute(value, axis, [(source, source ^ bits) for source in range(count)])


def traded(value, axis, group):
    if group == 1:
        return value
    count = lax.axis_size(axis)
    groups = [list(range(first, first + group)) for first in range(0, count, group)]
    return lax.all_to_all(value, axis, 0, 0, axis_index_groups=groups, tiled=True)


def call(body, outs, scratch=(), flops=0, count=0, exps=0):
    def run(*args):
        moved = sum(a.size * a.dtype.itemsize for a in args)
        moved += sum(o.size * o.dtype.itemsize for o in outs)
        return pl.pallas_call(
            body,
            out_shape=tuple(outs),
            in_specs=[SMEM if a.dtype == jnp.int32 else VMEM for a in args],
            out_specs=tuple(VMEM for _ in outs),
            scratch_shapes=list(scratch),
            compiler_params=pltpu.CompilerParams(vmem_limit_bytes=48 * 1024 * 1024),
            cost_estimate=pl.CostEstimate(flops=flops, bytes_accessed=moved, transcendentals=exps),
        )(*args)

    return run


def split_heads(group, arrays):
    tokens = arrays[0].shape[0]
    widths = [array.shape[1] // group for array in arrays]

    def body(*refs):
        out_ref, sems = refs[-2:]
        copies = []
        for member in range(group):
            lower = 0
            for number, width in enumerate(widths):
                copies.append(
                    pltpu.make_async_copy(
                        refs[number].at[:, member * width : (member + 1) * width],
                        out_ref.at[member, :, lower : lower + width],
                        sems.at[len(copies)],
                    )
                )
                lower += width
        for copy in copies:
            copy.start()
        for copy in copies:
            copy.wait()

    moved = 2 * sum(array.size * array.dtype.itemsize for array in arrays)
    return pl.pallas_call(
        body,
        out_shape=jax.ShapeDtypeStruct((group, tokens, sum(widths)), jnp.bfloat16),
        in_specs=[pl.BlockSpec(memory_space=pltpu.HBM)] * len(arrays),
        out_specs=VMEM,
        scratch_shapes=[pltpu.SemaphoreType.DMA((group * len(arrays),))],
        cost_estimate=pl.CostEstimate(flops=0, bytes_accessed=moved, transcendentals=0),
    )(*arrays)


def head_product(start, rows, out_weight, layer_cotangent):
    tokens, depth = layer_cotangent.shape
    chunk = next((depth // parts for parts in range(3, depth) if depth % (parts * 128) == 0), depth)
    steps = depth // chunk

    def body(start_ref, w_ref, c_ref, o_ref, total):
        step = pl.program_id(0)
        term = lax.dot_general(w_ref[...], c_ref[...], NT, preferred_element_type=jnp.float32)

        if steps == 1:
            o_ref[...] = term.astype(jnp.bfloat16)
            return

        @pl.when(step == 0)
        def _():
            total[...] = term

        @pl.when((step > 0) & (step < steps - 1))
        def _():
            total[...] += term

        @pl.when(step == steps - 1)
        def _():
            o_ref[...] = (total[...] + term).astype(jnp.bfloat16)

    return pl.pallas_call(
        body,
        out_shape=jax.ShapeDtypeStruct((rows, tokens), jnp.bfloat16),
        grid_spec=pltpu.PrefetchScalarGridSpec(
            num_scalar_prefetch=1,
            grid=(steps,),
            in_specs=[
                pl.BlockSpec((rows, chunk), lambda i, s: (s[0], i)),
                pl.BlockSpec((tokens, chunk), lambda i, s: (0, i)),
            ],
            out_specs=pl.BlockSpec((rows, tokens), lambda i, s: (0, 0)),
            scratch_shapes=[pltpu.VMEM((rows, tokens), jnp.float32)],
        ),
        compiler_params=pltpu.CompilerParams(vmem_limit_bytes=48 * 1024 * 1024),
        cost_estimate=pl.CostEstimate(
            flops=2 * rows * tokens * depth,
            bytes_accessed=2 * (rows * depth + tokens * depth + rows * tokens),
            transcendentals=0,
        ),
    )(start, out_weight, layer_cotangent)


def add_grads(terms):
    def body(*refs):
        total = refs[0][...].astype(jnp.float32)
        for term in refs[1:-1]:
            total = total + term[...].astype(jnp.float32)
        refs[-1][...] = total.astype(jnp.bfloat16)

    return call(body, [jax.ShapeDtypeStruct(terms[0].shape, jnp.bfloat16)])(*terms)[0]


def attention(group, heads, per_head, ids, kv_own, kv_earlier, queries, grads):
    back = len(kv_earlier) * group
    tokens = kv_own.shape[1]
    span = back + 1
    total = back + group
    wide = per_head * tokens
    kv_width = heads * HEAD_SIZE
    factor = score_scale * LOG2_E

    def body(ids_ref, *refs):
        own_ref = refs[0]
        earlier_refs = refs[1 : 1 + len(kv_earlier)]
        q_ref = refs[1 + len(kv_earlier)]
        grad_ref = refs[2 + len(kv_earlier)]
        refs = refs[3 + len(kv_earlier) :]
        dq_ref, dkv_own, dkv_earlier = refs[0], refs[1], refs[2 : 2 + len(kv_earlier)]
        k_all, kt_all, v_all, g_all, q_all, dk_all, dv_all, s_all, dp_all = refs[2 + len(kv_earlier) :]
        first = ids_ref[0]
        key_id = lax.broadcasted_iota(jnp.int32, (tokens, wide), 0)
        query_id = lax.broadcasted_iota(jnp.int32, (tokens, wide), 1) & (tokens - 1)

        for head in range(heads):
            at_k = slice(head * HEAD_SIZE, (head + 1) * HEAD_SIZE)
            at_v = slice(kv_width + head * HEAD_SIZE, kv_width + (head + 1) * HEAD_SIZE)
            for number in range(total):
                if number < back:
                    source = earlier_refs[number // group].at[number % group]
                else:
                    source = own_ref.at[number - back]
                k_all[number] = source[:, at_k]
                kt_all[number] = source[:, at_k].T
                v_all[number] = source[:, at_v]
            for r in range(group):
                for j in range(per_head):
                    lower = (head * per_head + j) * HEAD_SIZE
                    g_all[r, :, j * tokens : (j + 1) * tokens] = grad_ref[r, lower : lower + HEAD_SIZE, :]
                    q_all[r, j * tokens : (j + 1) * tokens, :] = q_ref[r, :, lower : lower + HEAD_SIZE]
            dk_all[...] = jnp.zeros_like(dk_all)
            dv_all[...] = jnp.zeros_like(dv_all)

            @pl.loop(0, group)
            def _(b):
                q = q_all[b]
                g = g_all[b]
                top = None
                for c in range(span):
                    s = lax.dot_general(k_all[b + c], q, NT, preferred_element_type=jnp.float32) * factor
                    if c == 0:
                        s = jnp.where(key_id > query_id, s, -jnp.inf)
                    if c < back:
                        s = s + jnp.where(first + b + c >= back, 0.0, -jnp.inf)
                    else:
                        s = jnp.where(key_id <= query_id, s, -jnp.inf)
                    s_all[c] = s
                    here = jnp.max(s, axis=0, keepdims=True)
                    top = here if top is None else jnp.maximum(top, here)
                norm = jnp.zeros((1, wide), jnp.float32)
                delta = jnp.zeros((1, wide), jnp.float32)
                for c in range(span):
                    e = jnp.exp2(s_all[c] - top)
                    dp = lax.dot_general(v_all[b + c], g, NN, preferred_element_type=jnp.float32)
                    norm = norm + jnp.sum(e, axis=0, keepdims=True)
                    delta = delta + jnp.sum(e * dp, axis=0, keepdims=True)
                    s_all[c] = e
                    dp_all[c] = dp
                inverse = 1.0 / norm
                delta = delta * inverse
                dqt = jnp.zeros((HEAD_SIZE, wide), jnp.float32)
                for c in range(span):
                    p = s_all[c] * inverse
                    ds = (p * (dp_all[c] - delta) * score_scale).astype(jnp.bfloat16)
                    p = p.astype(jnp.bfloat16)
                    dv_all[b + c] += lax.dot_general(p, g, NT, preferred_element_type=jnp.float32)
                    dk_all[b + c] += lax.dot_general(ds, q, NN, preferred_element_type=jnp.float32)
                    dqt = dqt + lax.dot_general(kt_all[b + c], ds, NN, preferred_element_type=jnp.float32)
                for j in range(per_head):
                    lower = (head * per_head + j) * HEAD_SIZE
                    dq_ref[b, :, lower : lower + HEAD_SIZE] = (
                        dqt[:, j * tokens : (j + 1) * tokens].T.astype(jnp.bfloat16)
                    )

            for number in range(back):
                target = dkv_earlier[number // group].at[number % group]
                target[:, at_k] = dk_all[number].astype(jnp.bfloat16)
                target[:, at_v] = dv_all[number].astype(jnp.bfloat16)
            dkv_own[:, :, at_k] = dk_all[back:]
            dkv_own[:, :, at_v] = dv_all[back:]

    width = heads * per_head * HEAD_SIZE
    outs = [jax.ShapeDtypeStruct((group, tokens, width), jnp.bfloat16)]
    outs += [jax.ShapeDtypeStruct((group, tokens, 2 * kv_width), jnp.float32)]
    outs += [jax.ShapeDtypeStruct((group, tokens, 2 * kv_width), jnp.bfloat16)] * len(kv_earlier)
    scratch = [
        pltpu.VMEM((total, tokens, HEAD_SIZE), jnp.bfloat16),
        pltpu.VMEM((total, HEAD_SIZE, tokens), jnp.bfloat16),
        pltpu.VMEM((total, tokens, HEAD_SIZE), jnp.bfloat16),
        pltpu.VMEM((group, HEAD_SIZE, wide), jnp.bfloat16),
        pltpu.VMEM((group, wide, HEAD_SIZE), jnp.bfloat16),
        pltpu.VMEM((total, tokens, HEAD_SIZE), jnp.float32),
        pltpu.VMEM((total, tokens, HEAD_SIZE), jnp.float32),
        pltpu.VMEM((span, tokens, wide), jnp.float32),
        pltpu.VMEM((span, tokens, wide), jnp.float32),
    ]
    entries = group * heads * wide * span * tokens
    results = call(body, outs, scratch, flops=10 * entries * HEAD_SIZE, exps=entries)(
        ids, kv_own, *kv_earlier, queries, grads
    )
    return results[0], results[1], results[2:]


def join_heads(group, pieces, widths):
    tokens = pieces.shape[1]

    def body(in_ref, *out_refs):
        for member in range(group):
            lower = 0
            for out_ref, width in zip(out_refs, widths):
                out_ref[:, member * width : (member + 1) * width] = in_ref[member, :, lower : lower + width]
                lower += width

    outs = [jax.ShapeDtypeStruct((tokens, group * width), jnp.bfloat16) for width in widths]
    return call(body, outs)(pieces)


def local(layer_cotangent, out_weight, queries, keys, values):
    tokens = queries.shape[0]
    kv_heads = keys.shape[1] // HEAD_SIZE
    per_head = queries.shape[1] // keys.shape[1]
    count, tp_count = lax.axis_size("ctx"), lax.axis_size("tp")
    group = 1
    while (
        kv_heads % (2 * group) == 0
        and count % (2 * group) == 0
        and WINDOW_LENGTH % (2 * group * tokens) == 0
    ):
        group *= 2
    heads = kv_heads // group
    kv_width = heads * HEAD_SIZE
    back_groups = WINDOW_LENGTH // (group * tokens)
    index = lax.axis_index("ctx")
    ids = (index - index % group).astype(jnp.int32).reshape(1)
    rows = out_weight.shape[0] // tp_count

    kv_own = traded(split_heads(group, [keys, values]), "ctx", group)
    query_all = traded(split_heads(group, [queries]), "ctx", group)
    if tp_count == 2:
        mine = lax.axis_index("tp").astype(jnp.int32).reshape(1)
        other = head_product(1 - mine, rows, out_weight, layer_cotangent)
        terms = [swapped(other, "tp", 1)]
        terms = [head_product(mine, rows, out_weight, layer_cotangent)] + terms
        grads = add_grads(terms)
    else:
        product = head_product(jnp.zeros(1, jnp.int32), rows * tp_count, out_weight, layer_cotangent)
        grads = lax.psum_scatter(product, "tp", scatter_dimension=0, tiled=True)
    kv_earlier = [shifted(kv_own, "ctx", group * step) for step in range(back_groups, 0, -1)]
    grads = traded(grads.reshape(group, rows // group, tokens), "ctx", group)
    dq, dkv_own, dkv_earlier = attention(
        group, heads, per_head, ids, kv_own, kv_earlier, query_all, grads
    )
    arrived = [
        shifted(dkv_earlier[number], "ctx", -group * (back_groups - number))
        for number in range(back_groups)
    ]
    dq = traded(dq, "ctx", group)
    dkv = traded(add_grads([dkv_own] + arrived), "ctx", group)
    (query_grads,) = join_heads(group, dq, [dq.shape[2]])
    key_gradients, value_gradients = join_heads(group, dkv, [kv_width, kv_width])
    return (query_grads, key_gradients, value_gradients)


def solution(mesh):
    in_specs = (P("ctx", "tp"), P(None, "tp"), P("ctx", "tp"), P("ctx", "tp"), P("ctx", "tp"))
    out_specs = (P("ctx", "tp"), P("ctx", "tp"), P("ctx", "tp"))
    return jax.shard_map(local, mesh=mesh, in_specs=in_specs, out_specs=out_specs, check_vma=False)
```

```python
import functools

import jax
import jax.numpy as jnp
from jax import lax
from jax.experimental import pallas as pl
from jax.experimental.pallas import tpu as pltpu
from jax.sharding import PartitionSpec as P

HEAD_SIZE = 128
WINDOW_LENGTH = 1024
LOG2_E = 1.4426950408889634

score_scale = 168.0 ** (-0.5)

VMEM = pl.BlockSpec(memory_space=pltpu.VMEM)
HBM = pl.BlockSpec(memory_space=pltpu.HBM)
SMEM = pl.BlockSpec(memory_space=pltpu.SMEM)
NT = (((1,), (1,)), ((), ()))
NN = (((1,), (0,)), ((), ()))


def shifted(value, axis, steps):
    count = lax.axis_size(axis)
    leading, last = (max(0, -steps), min(count, count - steps))
    return lax.ppermute(value, axis, [(source, source + steps) for source in range(leading, last)])


def swapped(value, axis, bits):
    count = lax.axis_size(axis)
    return lax.ppermute(value, axis, [(source, source ^ bits) for source in range(count)])


def call(body, outs, scratch=(), flops=0, exps=0, specs=None, vmem=32):
    def run(*args):
        moved = sum(a.size * a.dtype.itemsize for a in args)
        moved += sum(o.size * o.dtype.itemsize for o in outs)
        return pl.pallas_call(
            body,
            out_shape=tuple(outs),
            in_specs=specs or [SMEM if a.dtype == jnp.int32 else VMEM for a in args],
            out_specs=tuple(VMEM for _ in outs),
            scratch_shapes=list(scratch),
            compiler_params=pltpu.CompilerParams(vmem_limit_bytes=vmem * 1024 * 1024),
            cost_estimate=pl.CostEstimate(flops=flops, bytes_accessed=moved, transcendentals=exps),
        )(*args)

    return run


def lanes(index, width):
    return pl.ds(pl.multiple_of(index * width, width), width)


def fetch_all(refs, held, sems):
    copies = [pltpu.make_async_copy(ref, to, sems.at[i]) for i, (ref, to) in enumerate(zip(refs, held))]
    for copy in copies:
        copy.start()
    for copy in copies:
        copy.wait()


def pack_kv(group, ids, keys, values):
    tokens, width = keys.shape[0], keys.shape[1] // group

    def body(ids_ref, k_in, v_in, *refs):
        k_ref, v_ref, sems = refs[group:]
        fetch_all((k_in, v_in), (k_ref, v_ref), sems)
        for r in range(group):
            member = ids_ref[0] ^ r
            refs[r][:, :width] = k_ref[:, lanes(member, width)]
            refs[r][:, width:] = v_ref[:, lanes(member, width)]

    outs = [jax.ShapeDtypeStruct((tokens, 2 * width), jnp.bfloat16)] * group
    scratch = [pltpu.VMEM(keys.shape, jnp.bfloat16)] * 2 + [pltpu.SemaphoreType.DMA((2,))]
    return call(body, outs, scratch, specs=[SMEM, HBM, HBM], vmem=62)(ids, keys, values)


def pack_queries(group, ids, queries):
    tokens, width = queries.shape[0], queries.shape[1] // group

    def body(ids_ref, q_ref, *out_refs):
        for r in range(group):
            out_refs[r][...] = q_ref[:, lanes(ids_ref[0] ^ r, width)]

    outs = [jax.ShapeDtypeStruct((tokens, width), jnp.bfloat16)] * group
    return call(body, outs)(ids, queries)


def order_pieces(group, ids, pieces):
    def body(ids_ref, *refs):
        for r in range(group):
            refs[group][ids_ref[0] ^ r] = refs[r][...]

    outs = [jax.ShapeDtypeStruct((group,) + pieces[0].shape, jnp.bfloat16)]
    return call(body, outs)(ids, *pieces)[0]


def head_product(start, rows, out_weight, layer_cotangent):
    tokens, depth = layer_cotangent.shape
    cuts = 3 if depth % (3 * 128) == 0 else 1
    chunk = depth // cuts
    strips = 4

    def body(start_ref, w_in, c_in, o_ref, w_ref, c_ref, total, w_sems, c_sems):
        first = start_ref[0] * rows
        copies = []
        for cut in range(cuts):
            columns = slice(cut * chunk, (cut + 1) * chunk)
            here = [pltpu.make_async_copy(c_in.at[:, columns], c_ref.at[:, columns], c_sems.at[cut])]
            for strip in range(strips):
                height = rows // strips
                there = pl.ds(pl.multiple_of(first + strip * height, height), height)
                here.append(
                    pltpu.make_async_copy(
                        w_in.at[there, columns],
                        w_ref.at[strip * height : (strip + 1) * height, columns],
                        w_sems.at[cut, strip],
                    )
                )
            copies.append(here)
        for here in copies:
            for copy in here:
                copy.start()
        for cut in range(cuts):
            columns = slice(cut * chunk, (cut + 1) * chunk)
            for copy in copies[cut]:
                copy.wait()
            term = lax.dot_general(
                w_ref[:, columns], c_ref[:, columns], NT, preferred_element_type=jnp.float32
            )
            if cut > 0:
                term = total[...] + term
            if cut < cuts - 1:
                total[...] = term
            else:
                o_ref[...] = term.astype(jnp.bfloat16)

    outs = [jax.ShapeDtypeStruct((rows, tokens), jnp.bfloat16)]
    scratch = [
        pltpu.VMEM((rows, depth), jnp.bfloat16),
        pltpu.VMEM((tokens, depth), jnp.bfloat16),
        pltpu.VMEM((rows, tokens), jnp.float32),
        pltpu.SemaphoreType.DMA((cuts, strips)),
        pltpu.SemaphoreType.DMA((cuts,)),
    ]
    run = call(body, outs, scratch, flops=2 * rows * tokens * depth, specs=[SMEM, HBM, HBM], vmem=54)
    return run(start, out_weight, layer_cotangent)[0]


def pack_grads(group, ids, terms):
    rows, tokens = terms[0].shape
    rows //= group

    def body(ids_ref, *refs):
        for r in range(group):
            there = lanes(ids_ref[0] ^ r, rows)
            total = refs[0][there, :]
            if len(terms) > 1:
                total = total.astype(jnp.float32)
                for term in refs[1 : len(terms)]:
                    total = total + term[there, :].astype(jnp.float32)
            refs[len(terms) + r][...] = total.astype(jnp.bfloat16)

    outs = [jax.ShapeDtypeStruct((rows, tokens), jnp.bfloat16)] * group
    return call(body, outs)(ids, *terms)


class Shape:
    def __init__(self, group, steps, heads, per_head, tokens):
        self.group, self.steps, self.heads, self.per_head, self.tokens = group, steps, heads, per_head, tokens
        self.back = steps * group
        self.span = self.back + 1
        self.total = self.back + group
        self.wide = per_head * tokens
        self.width = heads * per_head * HEAD_SIZE
        self.kv_width = heads * HEAD_SIZE
        self.entries = group * heads * self.wide * self.span * tokens

    def block(self, own_ref, earlier_refs, number):
        if number < self.back:
            return earlier_refs[number // self.group].at[number % self.group]
        return own_ref.at[number - self.back]


def softmax(z, ids, kv_own, kv_earlier, queries):
    factor = score_scale * LOG2_E

    def body(ids_ref, *refs):
        own_ref, earlier_refs, q_refs = refs[0], refs[1 : 1 + z.steps], refs[1 + z.steps : 1 + z.steps + z.group]
        e_ref, inverse_ref, qt_ref, k_all, s_all = refs[1 + z.steps + z.group :]
        place, first = ids_ref[0], ids_ref[1]
        key_id = lax.broadcasted_iota(jnp.int32, (z.tokens, z.wide), 0)
        query_id = lax.broadcasted_iota(jnp.int32, (z.tokens, z.wide), 1) & (z.tokens - 1)
        for head in range(z.heads):
            at_k = slice(head * HEAD_SIZE, (head + 1) * HEAD_SIZE)
            for number in range(z.total):
                k_all[number] = z.block(own_ref, earlier_refs, number)[:, at_k]
            for r in range(z.group):
                for j in range(z.per_head):
                    lower = (head * z.per_head + j) * HEAD_SIZE
                    qt_ref[head, place ^ r, :, j * z.tokens : (j + 1) * z.tokens] = q_refs[r][
                        :, lower : lower + HEAD_SIZE
                    ].T

            @pl.loop(0, z.group)
            def _(b):
                qt = qt_ref[head, b]
                top = None
                for c in range(z.span):
                    s = lax.dot_general(k_all[b + c], qt, NN, preferred_element_type=jnp.float32)
                    if c == 0:
                        s = jnp.where(key_id > query_id, s, -jnp.inf)
                    if c == z.back:
                        s = jnp.where(key_id <= query_id, s, -jnp.inf)
                    s_all[c] = s
                    here = jnp.max(s, axis=0, keepdims=True)
                    if c < z.back:
                        here = jnp.where(first + b + c >= z.back, here, -jnp.inf)
                    top = here if top is None else jnp.maximum(top, here)
                norm = jnp.zeros((1, z.wide), jnp.float32)
                for c in range(z.span):
                    base = top
                    if c < z.back:
                        base = jnp.where(first + b + c >= z.back, top, jnp.inf)
                    e = jnp.exp2((s_all[c] - base) * factor)
                    norm = norm + jnp.sum(e, axis=0, keepdims=True)
                    e_ref[head, b, c] = e.astype(jnp.bfloat16)
                inverse_ref[head, b] = 1.0 / norm

    outs = [
        jax.ShapeDtypeStruct((z.heads, z.group, z.span, z.tokens, z.wide), jnp.bfloat16),
        jax.ShapeDtypeStruct((z.heads, z.group, 1, z.wide), jnp.float32),
        jax.ShapeDtypeStruct((z.heads, z.group, HEAD_SIZE, z.wide), jnp.bfloat16),
    ]
    scratch = [
        pltpu.VMEM((z.total, z.tokens, HEAD_SIZE), jnp.bfloat16),
        pltpu.VMEM((z.span, z.tokens, z.wide), jnp.float32),
    ]
    return call(body, outs, scratch, flops=2 * z.entries * HEAD_SIZE, exps=z.entries)(
        ids, kv_own, *kv_earlier, *queries
    )


def value_terms(z, ids, e, inverse, grads):
    def body(ids_ref, e_ref, inverse_ref, *refs):
        g_refs, (g_ref, own_ref), earlier_refs = (
            refs[: z.group],
            refs[z.group : z.group + 2],
            refs[z.group + 2 : z.group + 2 + z.steps],
        )
        dv_all = refs[-1]
        place = ids_ref[0]
        for head in range(z.heads):
            at = slice(head * HEAD_SIZE, (head + 1) * HEAD_SIZE)
            for r in range(z.group):
                for j in range(z.per_head):
                    lower = (head * z.per_head + j) * HEAD_SIZE
                    g_ref[head, place ^ r, :, j * z.tokens : (j + 1) * z.tokens] = g_refs[r][
                        lower : lower + HEAD_SIZE, :
                    ]
            dv_all[...] = jnp.zeros_like(dv_all)

            @pl.loop(0, z.group)
            def _(b):
                g = (g_ref[head, b].astype(jnp.float32) * inverse_ref[head, b]).astype(jnp.bfloat16)
                for c in range(z.span):
                    dv_all[b + c] += lax.dot_general(
                        e_ref[head, b, c], g, NT, preferred_element_type=jnp.float32
                    )

            for number in range(z.total):
                part = dv_all[number]
                z.block(own_ref, earlier_refs, number)[:, at] = part.astype(own_ref.dtype if number >= z.back else jnp.bfloat16)

    outs = [
        jax.ShapeDtypeStruct((z.heads, z.group, HEAD_SIZE, z.wide), jnp.bfloat16),
        jax.ShapeDtypeStruct((z.group, z.tokens, z.kv_width), jnp.float32),
    ]
    outs += [jax.ShapeDtypeStruct((z.group, z.tokens, z.kv_width), jnp.bfloat16)] * z.steps
    scratch = [pltpu.VMEM((z.total, z.tokens, HEAD_SIZE), jnp.float32)]
    results = call(body, outs, scratch, flops=2 * z.entries * HEAD_SIZE)(ids, e, inverse, *grads)
    return results[0], results[1], results[2:]


def score_terms(z, ids, e, inverse, qt, g, kv_own, kv_earlier):
    def body(ids_ref, e_ref, inverse_ref, qt_ref, g_ref, own_ref, *refs):
        earlier_refs, dq_refs = refs[: z.steps], refs[z.steps : z.steps + z.group]
        dk_own, dk_earlier = refs[z.steps + z.group], refs[z.steps + z.group + 1 : 2 * z.steps + z.group + 1]
        kt_all, v_all, dq_all, dk_all, dp_all = refs[2 * z.steps + z.group + 1 :]
        place = ids_ref[0]
        for head in range(z.heads):
            at = slice(head * HEAD_SIZE, (head + 1) * HEAD_SIZE)
            at_v = slice(z.kv_width + head * HEAD_SIZE, z.kv_width + (head + 1) * HEAD_SIZE)
            for number in range(z.total):
                source = z.block(own_ref, earlier_refs, number)
                kt_all[number] = source[:, at].T
                v_all[number] = source[:, at_v]
            dk_all[...] = jnp.zeros_like(dk_all)

            @pl.loop(0, z.group)
            def _(b):
                g = g_ref[head, b]
                inverse = inverse_ref[head, b]
                delta = jnp.zeros((1, z.wide), jnp.float32)
                for c in range(z.span):
                    dp = lax.dot_general(v_all[b + c], g, NN, preferred_element_type=jnp.float32)
                    delta = delta + jnp.sum(e_ref[head, b, c].astype(jnp.float32) * dp, axis=0, keepdims=True)
                    dp_all[c] = dp
                delta = delta * inverse
                q = (qt_ref[head, b].astype(jnp.float32) * inverse).astype(jnp.bfloat16)
                dqt = jnp.zeros((HEAD_SIZE, z.wide), jnp.float32)
                for c in range(z.span):
                    ds = (e_ref[head, b, c].astype(jnp.float32) * (dp_all[c] - delta)).astype(jnp.bfloat16)
                    dk_all[b + c] += lax.dot_general(ds, q, NT, preferred_element_type=jnp.float32)
                    dqt = dqt + lax.dot_general(kt_all[b + c], ds, NN, preferred_element_type=jnp.float32)
                dqt = dqt * (inverse * score_scale)
                for j in range(z.per_head):
                    lower = (head * z.per_head + j) * HEAD_SIZE
                    dq_all[b, :, lower : lower + HEAD_SIZE] = (
                        dqt[:, j * z.tokens : (j + 1) * z.tokens].T.astype(jnp.bfloat16)
                    )

            for number in range(z.total):
                part = dk_all[number] * score_scale
                z.block(dk_own, dk_earlier, number)[:, at] = part.astype(dk_own.dtype if number >= z.back else jnp.bfloat16)
        for r in range(z.group):
            dq_refs[r][...] = dq_all[place ^ r]

    outs = [jax.ShapeDtypeStruct((z.tokens, z.width), jnp.bfloat16)] * z.group
    outs += [jax.ShapeDtypeStruct((z.group, z.tokens, z.kv_width), jnp.float32)]
    outs += [jax.ShapeDtypeStruct((z.group, z.tokens, z.kv_width), jnp.bfloat16)] * z.steps
    scratch = [
        pltpu.VMEM((z.total, HEAD_SIZE, z.tokens), jnp.bfloat16),
        pltpu.VMEM((z.total, z.tokens, HEAD_SIZE), jnp.bfloat16),
        pltpu.VMEM((z.group, z.tokens, z.width), jnp.bfloat16),
        pltpu.VMEM((z.total, z.tokens, HEAD_SIZE), jnp.float32),
        pltpu.VMEM((z.span, z.tokens, z.wide), jnp.float32),
    ]
    results = call(body, outs, scratch, flops=6 * z.entries * HEAD_SIZE)(
        ids, e, inverse, qt, g, kv_own, *kv_earlier
    )
    return results[: z.group], results[z.group], results[z.group + 1 :]


def pack_terms(group, ids, own, arrived):
    shape = own.shape[1:]

    def body(ids_ref, *refs):
        for r in range(group):
            member = ids_ref[0] ^ r
            total = refs[0][member]
            for term in refs[1 : 1 + len(arrived)]:
                total = total + term[member].astype(jnp.float32)
            refs[1 + len(arrived) + r][...] = total.astype(jnp.bfloat16)

    outs = [jax.ShapeDtypeStruct(shape, jnp.bfloat16)] * group
    return call(body, outs)(ids, own, *arrived)


def unpack(group, ids, pieces):
    tokens, width = pieces[0].shape

    def body(ids_ref, *refs):
        for r in range(group):
            refs[group][:, lanes(ids_ref[0] ^ r, width)] = refs[r][...]

    return call(body, [jax.ShapeDtypeStruct((tokens, group * width), jnp.bfloat16)])(ids, *pieces)[0]


def local(layer_cotangent, out_weight, queries, keys, values):
    tokens = queries.shape[0]
    kv_heads = keys.shape[1] // HEAD_SIZE
    per_head = queries.shape[1] // keys.shape[1]
    count, tp_count = lax.axis_size("ctx"), lax.axis_size("tp")
    group = 1
    while (
        kv_heads % (2 * group) == 0
        and count % (2 * group) == 0
        and WINDOW_LENGTH % (2 * group * tokens) == 0
    ):
        group *= 2
    heads = kv_heads // group
    kv_width = heads * HEAD_SIZE
    back_groups = WINDOW_LENGTH // (group * tokens)
    index = lax.axis_index("ctx")
    place = index % group
    ids = jnp.stack([place, index - place]).astype(jnp.int32)
    rows = out_weight.shape[0] // tp_count

    def trade(sent):
        return [sent[0]] + [swapped(sent[r], "ctx", r) for r in range(1, group)]

    def returned(own, earlier):
        arrived = [
            shifted(earlier[number], "ctx", -group * (back_groups - number)) for number in range(back_groups)
        ]
        return unpack(group, ids, trade(pack_terms(group, ids, own, arrived)))

    kv_own = order_pieces(group, ids, trade(pack_kv(group, ids, keys, values)))
    kv_earlier = [shifted(kv_own, "ctx", group * step) for step in range(back_groups, 0, -1)]
    query_pieces = trade(pack_queries(group, ids, queries))
    if tp_count == 2:
        mine = lax.axis_index("tp").astype(jnp.int32).reshape(1)
        other = head_product(1 - mine, rows, out_weight, layer_cotangent)
        terms = [swapped(other, "tp", 1)]
        terms = [head_product(mine, rows, out_weight, layer_cotangent)] + terms
    else:
        product = head_product(jnp.zeros(1, jnp.int32), rows * tp_count, out_weight, layer_cotangent)
        terms = [lax.psum_scatter(product, "tp", scatter_dimension=0, tiled=True)]
    grads = trade(pack_grads(group, ids, terms))
    z = Shape(group, back_groups, heads, per_head, tokens)
    e, inverse, qt = softmax(z, ids, kv_own, kv_earlier, query_pieces)
    g, dv_own, dv_earlier = value_terms(z, ids, e, inverse, grads)
    dq, dk_own, dk_earlier = score_terms(z, ids, e, inverse, qt, g, kv_own, kv_earlier)
    value_gradients = returned(dv_own, dv_earlier)
    query_grads = unpack(group, ids, trade(dq))
    key_gradients = returned(dk_own, dk_earlier)
    return (query_grads, key_gradients, value_gradients)


def solution(mesh):
    in_specs = (P("ctx", "tp"), P(None, "tp"), P("ctx", "tp"), P("ctx", "tp"), P("ctx", "tp"))
    out_specs = (P("ctx", "tp"), P("ctx", "tp"), P("ctx", "tp"))
    return jax.shard_map(local, mesh=mesh, in_specs=in_specs, out_specs=out_specs, check_vma=False)
```

```python
import functools

import jax
import jax.numpy as jnp
from jax import lax
from jax.experimental import pallas as pl
from jax.experimental.pallas import tpu as pltpu
from jax.sharding import PartitionSpec as P

HEAD_SIZE = 128
WINDOW_LENGTH = 1024
LOG2_E = 1.4426950408889634
AHEAD = 10**10

score_scale = 168.0 ** (-0.5)

VMEM = pl.BlockSpec(memory_space=pltpu.VMEM)
ANY = pl.BlockSpec(memory_space=pl.ANY)
SMEM = pl.BlockSpec(memory_space=pltpu.SMEM)
NT = (((1,), (1,)), ((), ()))
NN = (((1,), (0,)), ((), ()))


def shifted(value, axis, steps):
    count = lax.axis_size(axis)
    leading, last = (max(0, -steps), min(count, count - steps))
    return lax.ppermute(value, axis, [(source, source + steps) for source in range(leading, last)])


def swapped(value, axis, bits):
    count = lax.axis_size(axis)
    return lax.ppermute(value, axis, [(source, source ^ bits) for source in range(count)])


def call(body, outs, scratch=(), flops=0, exps=0, specs=None, vmem=32):
    def run(*args):
        moved = sum(a.size * a.dtype.itemsize for a in args)
        moved += sum(o.size * o.dtype.itemsize for o in outs)
        return pl.pallas_call(
            body,
            out_shape=tuple(outs),
            in_specs=specs or [SMEM if a.dtype == jnp.int32 else VMEM for a in args],
            out_specs=tuple(VMEM for _ in outs),
            scratch_shapes=list(scratch),
            compiler_params=pltpu.CompilerParams(vmem_limit_bytes=vmem * 1024 * 1024),
            cost_estimate=pl.CostEstimate(flops=flops, bytes_accessed=moved, transcendentals=exps),
        )(*args)

    return run


def spot(group):
    index = lax.axis_index("ctx")
    place = lax.rem(index, group)
    return place, index - place


def lanes(index, width):
    return pl.ds(pl.multiple_of(index * width, width), width)


def pack_kv(group, keys, values):
    tokens, width = keys.shape[0], keys.shape[1] // group

    def body(k_ref, v_ref, *refs):
        for r in range(group):
            member = spot(group)[0] ^ r
            refs[r][:, :width] = k_ref[:, lanes(member, width)]
            refs[r][:, width:] = v_ref[:, lanes(member, width)]

    outs = [jax.ShapeDtypeStruct((tokens, 2 * width), jnp.bfloat16)] * group
    return call(body, outs, flops=AHEAD)(keys, values)


def pack_queries(group, queries, before):
    tokens, width = queries.shape[0], queries.shape[1] // group

    def body(q_ref, before_ref, *out_refs):
        for r in range(group):
            out_refs[r][...] = q_ref[:, lanes(spot(group)[0] ^ r, width)]

    outs = [jax.ShapeDtypeStruct((tokens, width), jnp.bfloat16)] * group
    return call(body, outs, specs=[VMEM, ANY])(queries, before)


def order_pieces(group, pieces):
    def body(*refs):
        for r in range(group):
            refs[group][spot(group)[0] ^ r] = refs[r][...]

    outs = [jax.ShapeDtypeStruct((group,) + pieces[0].shape, jnp.bfloat16)]
    return call(body, outs)(*pieces)[0]


def head_product(parts, part, out_weight, layer_cotangent, before):
    tokens, depth = layer_cotangent.shape
    rows = out_weight.shape[0] // parts
    tile = min(rows, 512)

    def body(w_ref, c_ref, *refs):
        first = (lax.axis_index("tp") ^ part) * rows if parts > 1 else 0

        @pl.loop(0, rows // tile)
        def _(i):
            here = pl.ds(pl.multiple_of(i * tile, tile), tile)
            there = pl.ds(pl.multiple_of(first + i * tile, tile), tile)
            refs[-1][here, :] = lax.dot_general(
                w_ref[there, :], c_ref[...], NT, preferred_element_type=jnp.float32
            ).astype(jnp.bfloat16)

    outs = [jax.ShapeDtypeStruct((rows, tokens), jnp.bfloat16)]
    specs = [VMEM, VMEM] + [ANY] * len(before)
    return call(body, outs, flops=2 * rows * tokens * depth, specs=specs, vmem=16)(
        out_weight, layer_cotangent, *before
    )[0]


def pack_grads(group, terms):
    rows, tokens = terms[0].shape
    rows //= group

    def body(*refs):
        for r in range(group):
            there = lanes(spot(group)[0] ^ r, rows)
            total = refs[0][there, :]
            if len(terms) > 1:
                total = total.astype(jnp.float32)
                for term in refs[1 : len(terms)]:
                    total = total + term[there, :].astype(jnp.float32)
            refs[len(terms) + r][...] = total.astype(jnp.bfloat16)

    outs = [jax.ShapeDtypeStruct((rows, tokens), jnp.bfloat16)] * group
    return call(body, outs)(*terms)


class Shape:
    def __init__(self, group, steps, heads, per_head, tokens):
        self.group, self.steps, self.heads, self.per_head, self.tokens = group, steps, heads, per_head, tokens
        self.back = steps * group
        self.span = self.back + 1
        self.total = self.back + group
        self.wide = per_head * tokens
        self.width = heads * per_head * HEAD_SIZE
        self.kv_width = heads * HEAD_SIZE
        self.entries = group * heads * self.wide * self.span * tokens

    def block(self, own_ref, earlier_refs, number):
        if number < self.back:
            return earlier_refs[number // self.group].at[number % self.group]
        return own_ref.at[number - self.back]


def turn_queries(z, pieces):
    def body(*refs):
        for head in range(z.heads):
            for r in range(z.group):
                for j in range(z.per_head):
                    lower = (head * z.per_head + j) * HEAD_SIZE
                    refs[z.group][head, spot(z.group)[0] ^ r, :, j * z.tokens : (j + 1) * z.tokens] = refs[r][
                        :, lower : lower + HEAD_SIZE
                    ].T

    outs = [jax.ShapeDtypeStruct((z.heads, z.group, HEAD_SIZE, z.wide), jnp.bfloat16)]
    return call(body, outs)(*pieces)[0]


def softmax(z, kv_own, kv_earlier, qt):
    factor = score_scale * LOG2_E

    def body(*refs):
        own_ref, earlier_refs = refs[0], refs[1 : 1 + z.steps]
        qt_ref, e_ref, inverse_ref, k_all, s_all = refs[1 + z.steps :]
        first = spot(z.group)[1]
        key_id = lax.broadcasted_iota(jnp.int32, (z.tokens, z.wide), 0)
        query_id = lax.broadcasted_iota(jnp.int32, (z.tokens, z.wide), 1) & (z.tokens - 1)
        for head in range(z.heads):
            at_k = slice(head * HEAD_SIZE, (head + 1) * HEAD_SIZE)
            for number in range(z.total):
                k_all[number] = z.block(own_ref, earlier_refs, number)[:, at_k]

            @pl.loop(0, z.group)
            def _(b):
                qt = qt_ref[head, b]
                top = None
                for c in range(z.span):
                    s = lax.dot_general(k_all[b + c], qt, NN, preferred_element_type=jnp.float32)
                    if c == 0:
                        s = jnp.where(key_id > query_id, s, -jnp.inf)
                    if c == z.back:
                        s = jnp.where(key_id <= query_id, s, -jnp.inf)
                    s_all[c] = s
                    here = jnp.max(s, axis=0, keepdims=True)
                    if c < z.back:
                        here = jnp.where(first + b + c >= z.back, here, -jnp.inf)
                    top = here if top is None else jnp.maximum(top, here)
                norm = jnp.zeros((1, z.wide), jnp.float32)
                for c in range(z.span):
                    base = top
                    if c < z.back:
                        base = jnp.where(first + b + c >= z.back, top, jnp.inf)
                    e = jnp.exp2((s_all[c] - base) * factor)
                    norm = norm + jnp.sum(e, axis=0, keepdims=True)
                    e_ref[head, b, c] = e.astype(jnp.bfloat16)
                inverse_ref[head, b] = 1.0 / norm

    outs = [
        jax.ShapeDtypeStruct((z.heads, z.group, z.span, z.tokens, z.wide), jnp.bfloat16),
        jax.ShapeDtypeStruct((z.heads, z.group, 1, z.wide), jnp.float32),
    ]
    scratch = [
        pltpu.VMEM((z.total, z.tokens, HEAD_SIZE), jnp.bfloat16),
        pltpu.VMEM((z.span, z.tokens, z.wide), jnp.float32),
    ]
    return call(body, outs, scratch, flops=2 * z.entries * HEAD_SIZE, exps=z.entries)(
        kv_own, *kv_earlier, qt
    )


def value_terms(z, e, inverse, grads):
    def body(e_ref, inverse_ref, *refs):
        g_refs, (g_ref, own_ref), earlier_refs = (
            refs[: z.group],
            refs[z.group : z.group + 2],
            refs[z.group + 2 : z.group + 2 + z.steps],
        )
        dv_all = refs[-1]
        place = spot(z.group)[0]
        for head in range(z.heads):
            at = slice(head * HEAD_SIZE, (head + 1) * HEAD_SIZE)
            for r in range(z.group):
                for j in range(z.per_head):
                    lower = (head * z.per_head + j) * HEAD_SIZE
                    g_ref[head, place ^ r, :, j * z.tokens : (j + 1) * z.tokens] = g_refs[r][
                        lower : lower + HEAD_SIZE, :
                    ]
            dv_all[...] = jnp.zeros_like(dv_all)

            @pl.loop(0, z.group)
            def _(b):
                g = (g_ref[head, b].astype(jnp.float32) * inverse_ref[head, b]).astype(jnp.bfloat16)
                for c in range(z.span):
                    dv_all[b + c] += lax.dot_general(
                        e_ref[head, b, c], g, NT, preferred_element_type=jnp.float32
                    )

            for number in range(z.total):
                part = dv_all[number]
                z.block(own_ref, earlier_refs, number)[:, at] = part.astype(own_ref.dtype if number >= z.back else jnp.bfloat16)

    outs = [
        jax.ShapeDtypeStruct((z.heads, z.group, HEAD_SIZE, z.wide), jnp.bfloat16),
        jax.ShapeDtypeStruct((z.group, z.tokens, z.kv_width), jnp.float32),
    ]
    outs += [jax.ShapeDtypeStruct((z.group, z.tokens, z.kv_width), jnp.bfloat16)] * z.steps
    scratch = [pltpu.VMEM((z.total, z.tokens, HEAD_SIZE), jnp.float32)]
    results = call(body, outs, scratch, flops=2 * z.entries * HEAD_SIZE)(e, inverse, *grads)
    return results[0], results[1], results[2:]


def key_terms(z, e, inverse, qt, g, kv_own, kv_earlier):
    def body(e_ref, inverse_ref, qt_ref, g_ref, own_ref, *refs):
        earlier_refs, ds_ref = refs[: z.steps], refs[z.steps]
        dk_own, dk_earlier = refs[z.steps + 1], refs[z.steps + 2 : 2 * z.steps + 2]
        v_all, dk_all, dp_all = refs[2 * z.steps + 2 :]
        for head in range(z.heads):
            at = slice(head * HEAD_SIZE, (head + 1) * HEAD_SIZE)
            at_v = slice(z.kv_width + head * HEAD_SIZE, z.kv_width + (head + 1) * HEAD_SIZE)
            for number in range(z.total):
                v_all[number] = z.block(own_ref, earlier_refs, number)[:, at_v]
            dk_all[...] = jnp.zeros_like(dk_all)

            @pl.loop(0, z.group)
            def _(b):
                g = g_ref[head, b]
                inverse = inverse_ref[head, b]
                delta = jnp.zeros((1, z.wide), jnp.float32)
                for c in range(z.span):
                    dp = lax.dot_general(v_all[b + c], g, NN, preferred_element_type=jnp.float32)
                    delta = delta + jnp.sum(e_ref[head, b, c].astype(jnp.float32) * dp, axis=0, keepdims=True)
                    dp_all[c] = dp
                delta = delta * inverse
                q = (qt_ref[head, b].astype(jnp.float32) * inverse).astype(jnp.bfloat16)
                for c in range(z.span):
                    ds = (e_ref[head, b, c].astype(jnp.float32) * (dp_all[c] - delta)).astype(jnp.bfloat16)
                    ds_ref[head, b, c] = ds
                    dk_all[b + c] += lax.dot_general(ds, q, NT, preferred_element_type=jnp.float32)

            for number in range(z.total):
                part = dk_all[number] * score_scale
                z.block(dk_own, dk_earlier, number)[:, at] = part.astype(
                    dk_own.dtype if number >= z.back else jnp.bfloat16
                )

    outs = [jax.ShapeDtypeStruct(e.shape, jnp.bfloat16)]
    outs += [jax.ShapeDtypeStruct((z.group, z.tokens, z.kv_width), jnp.float32)]
    outs += [jax.ShapeDtypeStruct((z.group, z.tokens, z.kv_width), jnp.bfloat16)] * z.steps
    scratch = [
        pltpu.VMEM((z.total, z.tokens, HEAD_SIZE), jnp.bfloat16),
        pltpu.VMEM((z.total, z.tokens, HEAD_SIZE), jnp.float32),
        pltpu.VMEM((z.span, z.tokens, z.wide), jnp.float32),
    ]
    results = call(body, outs, scratch, flops=4 * z.entries * HEAD_SIZE)(
        e, inverse, qt, g, kv_own, *kv_earlier
    )
    return results[0], results[1], results[2:]


def query_terms(z, ds, inverse, kv_own, kv_earlier, dv_terms):
    def body(ds_ref, inverse_ref, own_ref, *refs):
        earlier_refs, term_refs, dv_ref = refs[: z.steps], refs[z.steps : 2 * z.steps + 1], refs[2 * z.steps + 1]
        dq_refs = refs[2 * z.steps + 2 : 2 * z.steps + 2 + z.group]
        kt_all, dq_all = refs[2 * z.steps + 2 + z.group :]
        dv = term_refs[0][...]
        for term in term_refs[1:]:
            dv = dv + term[...].astype(jnp.float32)
        dv_ref[...] = dv.astype(jnp.bfloat16)
        for head in range(z.heads):
            at = slice(head * HEAD_SIZE, (head + 1) * HEAD_SIZE)
            for number in range(z.total):
                kt_all[number] = z.block(own_ref, earlier_refs, number)[:, at].T

            @pl.loop(0, z.group)
            def _(b):
                dqt = jnp.zeros((HEAD_SIZE, z.wide), jnp.float32)
                for c in range(z.span):
                    dqt = dqt + lax.dot_general(
                        kt_all[b + c], ds_ref[head, b, c], NN, preferred_element_type=jnp.float32
                    )
                dqt = dqt * (inverse_ref[head, b] * score_scale)
                for j in range(z.per_head):
                    lower = (head * z.per_head + j) * HEAD_SIZE
                    dq_all[b, :, lower : lower + HEAD_SIZE] = (
                        dqt[:, j * z.tokens : (j + 1) * z.tokens].T.astype(jnp.bfloat16)
                    )

        for r in range(z.group):
            dq_refs[r][...] = dq_all[spot(z.group)[0] ^ r]

    outs = [jax.ShapeDtypeStruct((z.group, z.tokens, z.kv_width), jnp.bfloat16)]
    outs += [jax.ShapeDtypeStruct((z.tokens, z.width), jnp.bfloat16)] * z.group
    scratch = [
        pltpu.VMEM((z.total, HEAD_SIZE, z.tokens), jnp.bfloat16),
        pltpu.VMEM((z.group, z.tokens, z.width), jnp.bfloat16),
    ]
    results = call(body, outs, scratch, flops=2 * z.entries * HEAD_SIZE)(
        ds, inverse, kv_own, *kv_earlier, *dv_terms
    )
    return results[0], results[1:]


def pack_terms(group, sums):
    tokens, width = sums[0][0].shape[1:]
    flat = [term for terms in sums for term in terms]

    def body(*refs):
        for r in range(group):
            member = spot(group)[0] ^ r
            number = 0
            for column, terms in enumerate(sums):
                total = refs[number][member].astype(jnp.float32)
                for term in refs[number + 1 : number + len(terms)]:
                    total = total + term[member].astype(jnp.float32)
                refs[len(flat) + r][:, column * width : (column + 1) * width] = total.astype(jnp.bfloat16)
                number += len(terms)

    outs = [jax.ShapeDtypeStruct((tokens, len(sums) * width), jnp.bfloat16)] * group
    return call(body, outs)(*flat)


def unpack(group, pieces, widths):
    tokens = pieces[0].shape[0]

    def body(*refs):
        for r in range(group):
            lower = 0
            for number, width in enumerate(widths):
                refs[group + number][:, lanes(spot(group)[0] ^ r, width)] = refs[r][:, lower : lower + width]
                lower += width

    outs = [jax.ShapeDtypeStruct((tokens, group * width), jnp.bfloat16) for width in widths]
    return call(body, outs)(*pieces)


def local(layer_cotangent, out_weight, queries, keys, values):
    tokens = queries.shape[0]
    kv_heads = keys.shape[1] // HEAD_SIZE
    per_head = queries.shape[1] // keys.shape[1]
    count, tp_count = lax.axis_size("ctx"), lax.axis_size("tp")
    group = 1
    while (
        kv_heads % (2 * group) == 0
        and count % (2 * group) == 0
        and WINDOW_LENGTH % (2 * group * tokens) == 0
    ):
        group *= 2
    heads = kv_heads // group
    kv_width = heads * HEAD_SIZE
    back_groups = WINDOW_LENGTH // (group * tokens)
    def trade(sent):
        return [sent[0]] + [swapped(sent[r], "ctx", r) for r in range(1, group)]

    def returned(earlier):
        return [
            shifted(earlier[number], "ctx", -group * (back_groups - number)) for number in range(back_groups)
        ]

    sent = pack_kv(group, keys, values)
    kv_own = order_pieces(group, trade(sent))
    kv_earlier = [shifted(kv_own, "ctx", group * step) for step in range(back_groups, 0, -1)]
    z = Shape(group, back_groups, heads, per_head, tokens)
    query_sent = pack_queries(group, queries, sent[0])
    qt = turn_queries(z, trade(query_sent))
    if tp_count == 2:
        other = head_product(2, 1, out_weight, layer_cotangent, [query_sent[0]])
        terms = [head_product(2, 0, out_weight, layer_cotangent, [kv_own, other]), swapped(other, "tp", 1)]
    else:
        product = head_product(1, 0, out_weight, layer_cotangent, [query_sent[0]])
        terms = [lax.psum_scatter(product, "tp", scatter_dimension=0, tiled=True)]
    grads = trade(pack_grads(group, terms))
    e, inverse = softmax(z, kv_own, kv_earlier, qt)
    g, dv_own, dv_earlier = value_terms(z, e, inverse, grads)
    dv_terms = [dv_own] + returned(dv_earlier)
    ds, dk_own, dk_earlier = key_terms(z, e, inverse, qt, g, kv_own, kv_earlier)
    dk_terms = [dk_own] + returned(dk_earlier)
    dv, dq = query_terms(z, ds, inverse, kv_own, kv_earlier, dv_terms)
    dq = trade(dq)
    dkv = trade(pack_terms(group, [dk_terms, [dv]]))
    (query_grads,) = unpack(group, dq, [dq[0].shape[1]])
    key_gradients, value_gradients = unpack(group, dkv, [kv_width, kv_width])
    return (query_grads, key_gradients, value_gradients)


def solution(mesh):
    in_specs = (P("ctx", "tp"), P(None, "tp"), P("ctx", "tp"), P("ctx", "tp"), P("ctx", "tp"))
    out_specs = (P("ctx", "tp"), P("ctx", "tp"), P("ctx", "tp"))
    return jax.shard_map(local, mesh=mesh, in_specs=in_specs, out_specs=out_specs, check_vma=False)
```

```python
import functools

import jax
import jax.numpy as jnp
from jax import lax
from jax.experimental import pallas as pl
from jax.experimental.pallas import tpu as pltpu
from jax.sharding import PartitionSpec as P

HEAD_SIZE = 128
WINDOW_LENGTH = 1024
LOG2_E = 1.4426950408889634
AHEAD = 10**10

score_scale = 168.0 ** (-0.5)

VMEM = pl.BlockSpec(memory_space=pltpu.VMEM)
ANY = pl.BlockSpec(memory_space=pl.ANY)
SMEM = pl.BlockSpec(memory_space=pltpu.SMEM)
NT = (((1,), (1,)), ((), ()))
NN = (((1,), (0,)), ((), ()))


def shifted(value, axis, steps):
    count = lax.axis_size(axis)
    leading, last = (max(0, -steps), min(count, count - steps))
    return lax.ppermute(value, axis, [(source, source + steps) for source in range(leading, last)])


def swapped(value, axis, bits):
    count = lax.axis_size(axis)
    return lax.ppermute(value, axis, [(source, source ^ bits) for source in range(count)])


def call(body, outs, scratch=(), flops=0, exps=0, specs=None, vmem=32):
    def run(*args):
        moved = sum(a.size * a.dtype.itemsize for a in args)
        moved += sum(o.size * o.dtype.itemsize for o in outs)
        return pl.pallas_call(
            body,
            out_shape=tuple(outs),
            in_specs=specs or [SMEM if a.dtype == jnp.int32 else VMEM for a in args],
            out_specs=tuple(VMEM for _ in outs),
            scratch_shapes=list(scratch),
            compiler_params=pltpu.CompilerParams(vmem_limit_bytes=vmem * 1024 * 1024),
            cost_estimate=pl.CostEstimate(flops=flops, bytes_accessed=moved, transcendentals=exps),
        )(*args)

    return run


def spot(group):
    index = lax.axis_index("ctx")
    place = lax.rem(index, group)
    return place, index - place


def lanes(index, width):
    return pl.ds(pl.multiple_of(index * width, width), width)


def begin():
    def body(out_ref):
        out_ref[...] = jnp.zeros_like(out_ref)

    return call(body, [jax.ShapeDtypeStruct((8, 128), jnp.float32)], flops=AHEAD)()[0]


def pack_kv(group, keys, values, before):
    tokens, width = keys.shape[0], keys.shape[1] // group

    def body(k_ref, v_ref, before_ref, *refs):
        for r in range(group):
            member = spot(group)[0] ^ r
            refs[r][:, :width] = k_ref[:, lanes(member, width)]
            refs[r][:, width:] = v_ref[:, lanes(member, width)]

    outs = [jax.ShapeDtypeStruct((tokens, 2 * width), jnp.bfloat16)] * group
    return call(body, outs, flops=AHEAD, specs=[VMEM, VMEM, ANY])(keys, values, before)


def pack_queries(group, queries, before):
    tokens, width = queries.shape[0], queries.shape[1] // group

    def body(q_ref, before_ref, *out_refs):
        for r in range(group):
            out_refs[r][...] = q_ref[:, lanes(spot(group)[0] ^ r, width)]

    outs = [jax.ShapeDtypeStruct((tokens, width), jnp.bfloat16)] * group
    return call(body, outs, specs=[VMEM, ANY])(queries, before)


def order_pieces(group, pieces, before):
    def body(*refs):
        for r in range(group):
            refs[-1][spot(group)[0] ^ r] = refs[r][...]

    outs = [jax.ShapeDtypeStruct((group,) + pieces[0].shape, jnp.bfloat16)]
    return call(body, outs, specs=[VMEM] * group + [ANY])(*pieces, before)[0]


def head_product(parts, part, out_weight, layer_cotangent, before):
    tokens, depth = layer_cotangent.shape
    rows = out_weight.shape[0] // parts
    tile = min(rows, 512)

    def body(w_ref, c_ref, *refs):
        first = (lax.axis_index("tp") ^ part) * rows if parts > 1 else 0

        @pl.loop(0, rows // tile)
        def _(i):
            here = pl.ds(pl.multiple_of(i * tile, tile), tile)
            there = pl.ds(pl.multiple_of(first + i * tile, tile), tile)
            refs[-1][here, :] = lax.dot_general(
                w_ref[there, :], c_ref[...], NT, preferred_element_type=jnp.float32
            ).astype(jnp.bfloat16)

    outs = [jax.ShapeDtypeStruct((rows, tokens), jnp.bfloat16)]
    specs = [VMEM, VMEM] + [ANY] * len(before)
    return call(body, outs, flops=2 * rows * tokens * depth, specs=specs, vmem=16)(
        out_weight, layer_cotangent, *before
    )[0]


def pack_grads(group, terms):
    rows, tokens = terms[0].shape
    rows //= group

    def body(*refs):
        for r in range(group):
            there = lanes(spot(group)[0] ^ r, rows)
            total = refs[0][there, :]
            if len(terms) > 1:
                total = total.astype(jnp.float32)
                for term in refs[1 : len(terms)]:
                    total = total + term[there, :].astype(jnp.float32)
            refs[len(terms) + r][...] = total.astype(jnp.bfloat16)

    outs = [jax.ShapeDtypeStruct((rows, tokens), jnp.bfloat16)] * group
    return call(body, outs)(*terms)


class Shape:
    def __init__(self, group, steps, heads, per_head, tokens):
        self.group, self.steps, self.heads, self.per_head, self.tokens = group, steps, heads, per_head, tokens
        self.back = steps * group
        self.span = self.back + 1
        self.total = self.back + group
        self.wide = per_head * tokens
        self.width = heads * per_head * HEAD_SIZE
        self.kv_width = heads * HEAD_SIZE
        self.entries = group * heads * self.wide * self.span * tokens

    def block(self, own_ref, earlier_refs, number):
        if number < self.back:
            return earlier_refs[number // self.group].at[number % self.group]
        return own_ref.at[number - self.back]


def turn_queries(z, pieces):
    def body(*refs):
        for head in range(z.heads):
            for r in range(z.group):
                for j in range(z.per_head):
                    lower = (head * z.per_head + j) * HEAD_SIZE
                    refs[z.group][head, spot(z.group)[0] ^ r, :, j * z.tokens : (j + 1) * z.tokens] = refs[r][
                        :, lower : lower + HEAD_SIZE
                    ].T

    outs = [jax.ShapeDtypeStruct((z.heads, z.group, HEAD_SIZE, z.wide), jnp.bfloat16)]
    return call(body, outs)(*pieces)[0]


def softmax(z, kv_own, kv_earlier, qt):
    factor = score_scale * LOG2_E

    def body(*refs):
        own_ref, earlier_refs = refs[0], refs[1 : 1 + z.steps]
        qt_ref, e_ref, inverse_ref, k_all, s_all, tops = refs[1 + z.steps :]
        first = spot(z.group)[1]
        key_id = lax.broadcasted_iota(jnp.int32, (z.tokens, z.wide), 0)
        query_id = lax.broadcasted_iota(jnp.int32, (z.tokens, z.wide), 1) & (z.tokens - 1)
        for head in range(z.heads):
            at_k = slice(head * HEAD_SIZE, (head + 1) * HEAD_SIZE)
            for number in range(z.total):
                k_all[number] = z.block(own_ref, earlier_refs, number)[:, at_k]

            def score(b, slot, c, top):
                s = lax.dot_general(k_all[b + c], qt_ref[head, b], NN, preferred_element_type=jnp.float32)
                if c == 0:
                    s = jnp.where(key_id > query_id, s, -jnp.inf)
                if c == z.back:
                    s = jnp.where(key_id <= query_id, s, -jnp.inf)
                s_all[slot, c] = s
                here = jnp.max(s, axis=0, keepdims=True)
                if c < z.back:
                    here = jnp.where(first + b + c >= z.back, here, -jnp.inf)
                return here if top is None else jnp.maximum(top, here)

            def expo(b, slot, c, norm):
                base = tops[slot]
                if c < z.back:
                    base = jnp.where(first + b + c >= z.back, base, jnp.inf)
                e = jnp.exp2((s_all[slot, c] - base) * factor)
                e_ref[head, b, c] = e.astype(jnp.bfloat16)
                here = jnp.sum(e, axis=0, keepdims=True)
                return here if norm is None else norm + here

            def both(b, slot, ahead):
                top = norm = None
                for c in range(z.span):
                    if ahead:
                        top = score(b + 1, 1 - slot, c, top)
                    norm = expo(b, slot, c, norm)
                if ahead:
                    tops[1 - slot] = top
                inverse_ref[head, b] = 1.0 / norm

            top = None
            for c in range(z.span):
                top = score(0, 0, c, top)
            tops[0] = top
            if z.group > 1:

                @pl.loop(0, z.group - 1)
                def _(b):
                    both(b, b & 1, True)

            both(z.group - 1, (z.group - 1) & 1, False)

    outs = [
        jax.ShapeDtypeStruct((z.heads, z.group, z.span, z.tokens, z.wide), jnp.bfloat16),
        jax.ShapeDtypeStruct((z.heads, z.group, 1, z.wide), jnp.float32),
    ]
    scratch = [
        pltpu.VMEM((z.total, z.tokens, HEAD_SIZE), jnp.bfloat16),
        pltpu.VMEM((2, z.span, z.tokens, z.wide), jnp.float32),
        pltpu.VMEM((2, 1, z.wide), jnp.float32),
    ]
    return call(body, outs, scratch, flops=2 * z.entries * HEAD_SIZE, exps=z.entries)(
        kv_own, *kv_earlier, qt
    )


def value_terms(z, e, inverse, grads):
    def body(e_ref, inverse_ref, *refs):
        g_refs, (g_ref, own_ref), earlier_refs = (
            refs[: z.group],
            refs[z.group : z.group + 2],
            refs[z.group + 2 : z.group + 2 + z.steps],
        )
        dv_all = refs[-1]
        place = spot(z.group)[0]
        for head in range(z.heads):
            at = slice(head * HEAD_SIZE, (head + 1) * HEAD_SIZE)
            for r in range(z.group):
                for j in range(z.per_head):
                    lower = (head * z.per_head + j) * HEAD_SIZE
                    g_ref[head, place ^ r, :, j * z.tokens : (j + 1) * z.tokens] = g_refs[r][
                        lower : lower + HEAD_SIZE, :
                    ]
            dv_all[...] = jnp.zeros_like(dv_all)

            @pl.loop(0, z.group)
            def _(b):
                g = (g_ref[head, b].astype(jnp.float32) * inverse_ref[head, b]).astype(jnp.bfloat16)
                window = pl.ds(pl.multiple_of(b * z.tokens, z.tokens), z.span * z.tokens)
                dv_all[window, :] += lax.dot_general(
                    e_ref[head, b].reshape(z.span * z.tokens, z.wide), g, NT, preferred_element_type=jnp.float32
                )

            for number in range(z.total):
                part = dv_all[number * z.tokens : (number + 1) * z.tokens, :]
                z.block(own_ref, earlier_refs, number)[:, at] = part.astype(own_ref.dtype if number >= z.back else jnp.bfloat16)

    outs = [
        jax.ShapeDtypeStruct((z.heads, z.group, HEAD_SIZE, z.wide), jnp.bfloat16),
        jax.ShapeDtypeStruct((z.group, z.tokens, z.kv_width), jnp.float32),
    ]
    outs += [jax.ShapeDtypeStruct((z.group, z.tokens, z.kv_width), jnp.bfloat16)] * z.steps
    scratch = [pltpu.VMEM((z.total * z.tokens, HEAD_SIZE), jnp.float32)]
    results = call(body, outs, scratch, flops=2 * z.entries * HEAD_SIZE)(e, inverse, *grads)
    return results[0], results[1], results[2:]


def key_terms(z, e, inverse, qt, g, kv_own, kv_earlier):
    def body(e_ref, inverse_ref, qt_ref, g_ref, own_ref, *refs):
        earlier_refs, ds_ref = refs[: z.steps], refs[z.steps]
        dk_own, dk_earlier = refs[z.steps + 1], refs[z.steps + 2 : 2 * z.steps + 2]
        v_all, dk_all, dp_all, deltas = refs[2 * z.steps + 2 :]
        for head in range(z.heads):
            at = slice(head * HEAD_SIZE, (head + 1) * HEAD_SIZE)
            at_v = slice(z.kv_width + head * HEAD_SIZE, z.kv_width + (head + 1) * HEAD_SIZE)
            for number in range(z.total):
                v_all[number] = z.block(own_ref, earlier_refs, number)[:, at_v]
            dk_all[...] = jnp.zeros_like(dk_all)

            def product(b, slot, c, delta):
                dp = lax.dot_general(v_all[b + c], g_ref[head, b], NN, preferred_element_type=jnp.float32)
                dp_all[slot, c] = dp
                here = jnp.sum(e_ref[head, b, c].astype(jnp.float32) * dp, axis=0, keepdims=True)
                return here if delta is None else delta + here

            def both(b, slot, ahead):
                delta = None
                q = (qt_ref[head, b].astype(jnp.float32) * inverse_ref[head, b]).astype(jnp.bfloat16)
                for c in range(z.span):
                    if ahead:
                        delta = product(b + 1, 1 - slot, c, delta)
                    ds = (e_ref[head, b, c].astype(jnp.float32) * (dp_all[slot, c] - deltas[slot])).astype(
                        jnp.bfloat16
                    )
                    ds_ref[head, b, c] = ds
                    dk_all[b + c] += lax.dot_general(ds, q, NT, preferred_element_type=jnp.float32)
                if ahead:
                    deltas[1 - slot] = delta * inverse_ref[head, b + 1]

            delta = None
            for c in range(z.span):
                delta = product(0, 0, c, delta)
            deltas[0] = delta * inverse_ref[head, 0]
            if z.group > 1:

                @pl.loop(0, z.group - 1)
                def _(b):
                    both(b, b & 1, True)

            both(z.group - 1, (z.group - 1) & 1, False)

            for number in range(z.total):
                part = dk_all[number] * score_scale
                z.block(dk_own, dk_earlier, number)[:, at] = part.astype(
                    dk_own.dtype if number >= z.back else jnp.bfloat16
                )

    outs = [jax.ShapeDtypeStruct(e.shape, jnp.bfloat16)]
    outs += [jax.ShapeDtypeStruct((z.group, z.tokens, z.kv_width), jnp.float32)]
    outs += [jax.ShapeDtypeStruct((z.group, z.tokens, z.kv_width), jnp.bfloat16)] * z.steps
    scratch = [
        pltpu.VMEM((z.total, z.tokens, HEAD_SIZE), jnp.bfloat16),
        pltpu.VMEM((z.total, z.tokens, HEAD_SIZE), jnp.float32),
        pltpu.VMEM((2, z.span, z.tokens, z.wide), jnp.float32),
        pltpu.VMEM((2, 1, z.wide), jnp.float32),
    ]
    results = call(body, outs, scratch, flops=4 * z.entries * HEAD_SIZE)(
        e, inverse, qt, g, kv_own, *kv_earlier
    )
    return results[0], results[1], results[2:]


def query_terms(z, ds, inverse, kv_own, kv_earlier, dv_terms):
    def body(ds_ref, inverse_ref, own_ref, *refs):
        earlier_refs, term_refs, dv_ref = refs[: z.steps], refs[z.steps : 2 * z.steps + 1], refs[2 * z.steps + 1]
        dq_refs = refs[2 * z.steps + 2 : 2 * z.steps + 2 + z.group]
        kt_all, dq_all = refs[2 * z.steps + 2 + z.group :]
        dv = term_refs[0][...]
        for term in term_refs[1:]:
            dv = dv + term[...].astype(jnp.float32)
        dv_ref[...] = dv.astype(jnp.bfloat16)
        for head in range(z.heads):
            at = slice(head * HEAD_SIZE, (head + 1) * HEAD_SIZE)
            for number in range(z.total):
                kt_all[number] = z.block(own_ref, earlier_refs, number)[:, at].T

            @pl.loop(0, z.group)
            def _(b):
                dqt = jnp.zeros((HEAD_SIZE, z.wide), jnp.float32)
                for c in range(z.span):
                    dqt = dqt + lax.dot_general(
                        kt_all[b + c], ds_ref[head, b, c], NN, preferred_element_type=jnp.float32
                    )
                dqt = dqt * (inverse_ref[head, b] * score_scale)
                for j in range(z.per_head):
                    lower = (head * z.per_head + j) * HEAD_SIZE
                    dq_all[b, :, lower : lower + HEAD_SIZE] = (
                        dqt[:, j * z.tokens : (j + 1) * z.tokens].T.astype(jnp.bfloat16)
                    )

        for r in range(z.group):
            dq_refs[r][...] = dq_all[spot(z.group)[0] ^ r]

    outs = [jax.ShapeDtypeStruct((z.group, z.tokens, z.kv_width), jnp.bfloat16)]
    outs += [jax.ShapeDtypeStruct((z.tokens, z.width), jnp.bfloat16)] * z.group
    scratch = [
        pltpu.VMEM((z.total, HEAD_SIZE, z.tokens), jnp.bfloat16),
        pltpu.VMEM((z.group, z.tokens, z.width), jnp.bfloat16),
    ]
    results = call(body, outs, scratch, flops=2 * z.entries * HEAD_SIZE)(
        ds, inverse, kv_own, *kv_earlier, *dv_terms
    )
    return results[0], results[1:]


def pack_terms(group, sums):
    tokens, width = sums[0][0].shape[1:]
    flat = [term for terms in sums for term in terms]

    def body(*refs):
        for r in range(group):
            member = spot(group)[0] ^ r
            number = 0
            for column, terms in enumerate(sums):
                total = refs[number][member].astype(jnp.float32)
                for term in refs[number + 1 : number + len(terms)]:
                    total = total + term[member].astype(jnp.float32)
                refs[len(flat) + r][:, column * width : (column + 1) * width] = total.astype(jnp.bfloat16)
                number += len(terms)

    outs = [jax.ShapeDtypeStruct((tokens, len(sums) * width), jnp.bfloat16)] * group
    return call(body, outs)(*flat)


def unpack(group, pieces, widths):
    tokens = pieces[0].shape[0]

    def body(*refs):
        for r in range(group):
            lower = 0
            for number, width in enumerate(widths):
                refs[group + number][:, lanes(spot(group)[0] ^ r, width)] = refs[r][:, lower : lower + width]
                lower += width

    outs = [jax.ShapeDtypeStruct((tokens, group * width), jnp.bfloat16) for width in widths]
    return call(body, outs)(*pieces)


def local(layer_cotangent, out_weight, queries, keys, values):
    tokens = queries.shape[0]
    kv_heads = keys.shape[1] // HEAD_SIZE
    per_head = queries.shape[1] // keys.shape[1]
    count, tp_count = lax.axis_size("ctx"), lax.axis_size("tp")
    group = 1
    while (
        kv_heads % (2 * group) == 0
        and count % (2 * group) == 0
        and WINDOW_LENGTH % (2 * group * tokens) == 0
    ):
        group *= 2
    heads = kv_heads // group
    kv_width = heads * HEAD_SIZE
    back_groups = WINDOW_LENGTH // (group * tokens)
    def trade(sent):
        return [sent[0]] + [swapped(sent[r], "ctx", r) for r in range(1, group)]

    def returned(earlier):
        return [
            shifted(earlier[number], "ctx", -group * (back_groups - number)) for number in range(back_groups)
        ]

    sent = pack_kv(group, keys, values, begin())
    kv_pieces = trade(sent)
    z = Shape(group, back_groups, heads, per_head, tokens)
    query_sent = pack_queries(group, queries, sent[0])
    if tp_count == 2:
        other = head_product(2, 1, out_weight, layer_cotangent, [query_sent[0]])
        mine = head_product(2, 0, out_weight, layer_cotangent, [other])
        terms = [mine, swapped(other, "tp", 1)]
    else:
        mine = head_product(1, 0, out_weight, layer_cotangent, [query_sent[0]])
        terms = [lax.psum_scatter(mine, "tp", scatter_dimension=0, tiled=True)]
    kv_own = order_pieces(group, kv_pieces, mine)
    kv_earlier = [shifted(kv_own, "ctx", group * step) for step in range(back_groups, 0, -1)]
    qt = turn_queries(z, trade(query_sent))
    grads = trade(pack_grads(group, terms))
    e, inverse = softmax(z, kv_own, kv_earlier, qt)
    g, dv_own, dv_earlier = value_terms(z, e, inverse, grads)
    dv_terms = [dv_own] + returned(dv_earlier)
    ds, dk_own, dk_earlier = key_terms(z, e, inverse, qt, g, kv_own, kv_earlier)
    dk_terms = [dk_own] + returned(dk_earlier)
    dv, dq = query_terms(z, ds, inverse, kv_own, kv_earlier, dv_terms)
    dq = trade(dq)
    dkv = trade(pack_terms(group, [dk_terms, [dv]]))
    (query_grads,) = unpack(group, dq, [dq[0].shape[1]])
    key_gradients, value_gradients = unpack(group, dkv, [kv_width, kv_width])
    return (query_grads, key_gradients, value_gradients)


def solution(mesh):
    in_specs = (P("ctx", "tp"), P(None, "tp"), P("ctx", "tp"), P("ctx", "tp"), P("ctx", "tp"))
    out_specs = (P("ctx", "tp"), P("ctx", "tp"), P("ctx", "tp"))
    return jax.shard_map(local, mesh=mesh, in_specs=in_specs, out_specs=out_specs, check_vma=False)
```

```python
import functools

import jax
import jax.numpy as jnp
from jax import lax
from jax.experimental import pallas as pl
from jax.experimental.pallas import tpu as pltpu
from jax.sharding import PartitionSpec as P

HEAD_SIZE = 128
WINDOW_LENGTH = 1024
LOG2_E = 1.4426950408889634
AHEAD = 10**10
ONES = 16

score_scale = 168.0 ** (-0.5)

VMEM = pl.BlockSpec(memory_space=pltpu.VMEM)
ANY = pl.BlockSpec(memory_space=pl.ANY)
SMEM = pl.BlockSpec(memory_space=pltpu.SMEM)
NT = (((1,), (1,)), ((), ()))
NN = (((1,), (0,)), ((), ()))


def shifted(value, axis, steps):
    count = lax.axis_size(axis)
    leading, last = (max(0, -steps), min(count, count - steps))
    return lax.ppermute(value, axis, [(source, source + steps) for source in range(leading, last)])


def swapped(value, axis, bits):
    count = lax.axis_size(axis)
    return lax.ppermute(value, axis, [(source, source ^ bits) for source in range(count)])


def call(body, outs, scratch=(), flops=0, exps=0, specs=None, vmem=32):
    def run(*args):
        moved = sum(a.size * a.dtype.itemsize for a in args)
        moved += sum(o.size * o.dtype.itemsize for o in outs)
        return pl.pallas_call(
            body,
            out_shape=tuple(outs),
            in_specs=specs or [SMEM if a.dtype == jnp.int32 else VMEM for a in args],
            out_specs=tuple(VMEM for _ in outs),
            scratch_shapes=list(scratch),
            compiler_params=pltpu.CompilerParams(vmem_limit_bytes=vmem * 1024 * 1024),
            cost_estimate=pl.CostEstimate(flops=flops, bytes_accessed=moved, transcendentals=exps),
        )(*args)

    return run


def spot(group):
    index = lax.axis_index("ctx")
    place = lax.rem(index, group)
    return place, index - place


def lanes(index, width):
    return pl.ds(pl.multiple_of(index * width, width), width)


def begin():
    def body(out_ref):
        out_ref[...] = jnp.zeros_like(out_ref)

    return call(body, [jax.ShapeDtypeStruct((8, 128), jnp.float32)], flops=AHEAD)()[0]


def pack_kv(group, keys, values, before):
    tokens, width = keys.shape[0], keys.shape[1] // group

    def body(k_ref, v_ref, before_ref, *refs):
        for r in range(group):
            member = spot(group)[0] ^ r
            refs[r][:, :width] = k_ref[:, lanes(member, width)]
            refs[r][:, width:] = v_ref[:, lanes(member, width)]

    outs = [jax.ShapeDtypeStruct((tokens, 2 * width), jnp.bfloat16)] * group
    return call(body, outs, flops=AHEAD, specs=[VMEM, VMEM, ANY])(keys, values, before)


def pack_queries(group, queries, before):
    tokens, width = queries.shape[0], queries.shape[1] // group

    def body(q_ref, before_ref, *out_refs):
        for r in range(group):
            out_refs[r][...] = q_ref[:, lanes(spot(group)[0] ^ r, width)]

    outs = [jax.ShapeDtypeStruct((tokens, width), jnp.bfloat16)] * group
    return call(body, outs, specs=[VMEM, ANY])(queries, before)


def order_kv(group, pieces, before):
    tokens, width = pieces[0].shape
    width //= 2

    def body(*refs):
        for r in range(group):
            member = spot(group)[0] ^ r
            refs[-2][member] = refs[r][:, :width]
            refs[-1][member] = refs[r][:, width:]

    outs = [jax.ShapeDtypeStruct((group, tokens, width), jnp.bfloat16)] * 2
    return call(body, outs, flops=AHEAD, specs=[VMEM] * group + [ANY])(*pieces, before)


def head_product(parts, part, out_weight, layer_cotangent, before):
    tokens, depth = layer_cotangent.shape
    rows = out_weight.shape[0] // parts
    tile = min(rows, 512)

    def body(w_ref, c_ref, *refs):
        first = (lax.axis_index("tp") ^ part) * rows if parts > 1 else 0

        @pl.loop(0, rows // tile)
        def _(i):
            here = pl.ds(pl.multiple_of(i * tile, tile), tile)
            there = pl.ds(pl.multiple_of(first + i * tile, tile), tile)
            refs[-1][here, :] = lax.dot_general(
                w_ref[there, :], c_ref[...], NT, preferred_element_type=jnp.float32
            ).astype(jnp.bfloat16)

    outs = [jax.ShapeDtypeStruct((rows, tokens), jnp.bfloat16)]
    specs = [VMEM, VMEM] + [ANY] * len(before)
    return call(body, outs, flops=2 * rows * tokens * depth, specs=specs, vmem=16)(
        out_weight, layer_cotangent, *before
    )[0]


def pack_grads(group, terms, before):
    rows, tokens = terms[0].shape
    rows //= group

    def body(*refs):
        for r in range(group):
            there = lanes(spot(group)[0] ^ r, rows)
            total = refs[0][there, :]
            if len(terms) > 1:
                total = total.astype(jnp.float32)
                for term in refs[1 : len(terms)]:
                    total = total + term[there, :].astype(jnp.float32)
            refs[len(terms) + 1 + r][...] = total.astype(jnp.bfloat16)

    outs = [jax.ShapeDtypeStruct((rows, tokens), jnp.bfloat16)] * group
    return call(body, outs, specs=[VMEM] * len(terms) + [ANY])(*terms, before)


class Shape:
    def __init__(self, group, steps, heads, per_head, tokens):
        self.group, self.steps, self.heads, self.per_head, self.tokens = group, steps, heads, per_head, tokens
        self.back = steps * group
        self.span = self.back + 1
        self.total = self.back + group
        self.wide = per_head * tokens
        self.width = heads * per_head * HEAD_SIZE
        self.kv_width = heads * HEAD_SIZE
        self.entries = group * heads * self.wide * self.span * tokens

    def block(self, own_ref, earlier_refs, number):
        if number < self.back:
            return earlier_refs[number // self.group].at[number % self.group]
        return own_ref.at[number - self.back]


def turn_queries(z, pieces):
    def body(*refs):
        for head in range(z.heads):
            for r in range(z.group):
                for j in range(z.per_head):
                    lower = (head * z.per_head + j) * HEAD_SIZE
                    refs[z.group][head, spot(z.group)[0] ^ r, :, j * z.tokens : (j + 1) * z.tokens] = refs[r][
                        :, lower : lower + HEAD_SIZE
                    ].T

    outs = [jax.ShapeDtypeStruct((z.heads, z.group, HEAD_SIZE, z.wide), jnp.bfloat16)]
    return call(body, outs)(*pieces)[0]


def softmax(z, k_own, k_earlier, qt):
    factor = score_scale * LOG2_E

    def body(own_ref, *refs):
        earlier_refs = refs[: z.steps]
        qt_ref, e_ref, k_all, s_all = refs[z.steps :]
        first = spot(z.group)[1]
        key_id = lax.broadcasted_iota(jnp.int32, (z.tokens, z.wide), 0)
        query_id = lax.broadcasted_iota(jnp.int32, (z.tokens, z.wide), 1) & (z.tokens - 1)
        for head in range(z.heads):
            at = slice(head * HEAD_SIZE, (head + 1) * HEAD_SIZE)
            for number in range(z.total):
                k_all[number] = z.block(own_ref, earlier_refs, number)[:, at]

            @pl.loop(0, z.group)
            def _(b):
                qt = qt_ref[head, b]
                top = None
                for c in range(z.span):
                    s = lax.dot_general(k_all[b + c], qt, NN, preferred_element_type=jnp.float32)
                    if c == 0:
                        s = jnp.where(key_id > query_id, s, -jnp.inf)
                    if c == z.back:
                        s = jnp.where(key_id <= query_id, s, -jnp.inf)
                    s_all[c] = s
                    here = jnp.max(s, axis=0, keepdims=True)
                    if c < z.back:
                        here = jnp.where(first + b + c >= z.back, here, -jnp.inf)
                    top = here if top is None else jnp.maximum(top, here)
                for c in range(z.span):
                    base = top
                    if c < z.back:
                        base = jnp.where(first + b + c >= z.back, top, jnp.inf)
                    e_ref[head, b, c] = jnp.exp2((s_all[c] - base) * factor).astype(jnp.bfloat16)

    outs = [jax.ShapeDtypeStruct((z.heads, z.group, z.span, z.tokens, z.wide), jnp.bfloat16)]
    scratch = [
        pltpu.VMEM((z.total, z.tokens, HEAD_SIZE), jnp.bfloat16),
        pltpu.VMEM((z.span, z.tokens, z.wide), jnp.float32),
    ]
    return call(body, outs, scratch, flops=2 * z.entries * HEAD_SIZE, exps=z.entries)(
        k_own, *k_earlier, qt
    )[0]


def value_terms(z, e, grads, v_own, v_earlier):
    def body(e_ref, own_ref, *refs):
        earlier_refs, g_refs = refs[: z.steps], refs[z.steps : z.steps + z.group]
        g_ref, inverse_ref, delta_ref, dv_own = refs[z.steps + z.group : z.steps + z.group + 4]
        dv_earlier, (vt_all, dv_all) = refs[z.steps + z.group + 4 : -2], refs[-2:]
        place = spot(z.group)[0]
        vt_all[:, HEAD_SIZE:, :] = jnp.ones((z.total, ONES, z.tokens), jnp.bfloat16)
        for head in range(z.heads):
            at = slice(head * HEAD_SIZE, (head + 1) * HEAD_SIZE)
            for number in range(z.total):
                vt_all[number, :HEAD_SIZE, :] = z.block(own_ref, earlier_refs, number)[:, at].T
            for r in range(z.group):
                for j in range(z.per_head):
                    lower = (head * z.per_head + j) * HEAD_SIZE
                    g_ref[head, place ^ r, :, j * z.tokens : (j + 1) * z.tokens] = g_refs[r][
                        lower : lower + HEAD_SIZE, :
                    ]
            dv_all[...] = jnp.zeros_like(dv_all)

            @pl.loop(0, z.group)
            def _(b):
                out = None
                for c in range(z.span):
                    term = lax.dot_general(vt_all[b + c], e_ref[head, b, c], NN, preferred_element_type=jnp.float32)
                    out = term if out is None else out + term
                inverse = 1.0 / out[HEAD_SIZE : HEAD_SIZE + 1, :]
                g = g_ref[head, b].astype(jnp.float32)
                inverse_ref[head, b] = inverse
                delta_ref[head, b] = jnp.sum(out[:HEAD_SIZE, :] * g, axis=0, keepdims=True) * inverse
                g = (g * inverse).astype(jnp.bfloat16)
                for c in range(z.span):
                    dv_all[b + c] += lax.dot_general(e_ref[head, b, c], g, NT, preferred_element_type=jnp.float32)

            for number in range(z.total):
                z.block(dv_own, dv_earlier, number)[:, at] = dv_all[number].astype(
                    dv_own.dtype if number >= z.back else jnp.bfloat16
                )

    outs = [
        jax.ShapeDtypeStruct((z.heads, z.group, HEAD_SIZE, z.wide), jnp.bfloat16),
        jax.ShapeDtypeStruct((z.heads, z.group, 1, z.wide), jnp.float32),
        jax.ShapeDtypeStruct((z.heads, z.group, 1, z.wide), jnp.float32),
        jax.ShapeDtypeStruct((z.group, z.tokens, z.kv_width), jnp.float32),
    ]
    outs += [jax.ShapeDtypeStruct((z.group, z.tokens, z.kv_width), jnp.bfloat16)] * z.steps
    scratch = [
        pltpu.VMEM((z.total, HEAD_SIZE + ONES, z.tokens), jnp.bfloat16),
        pltpu.VMEM((z.total, z.tokens, HEAD_SIZE), jnp.float32),
    ]
    results = call(body, outs, scratch, flops=4 * z.entries * HEAD_SIZE)(e, v_own, *v_earlier, *grads)
    return results[:3], results[3], results[4:]


def key_terms(z, e, inverse, delta, qt, g, v_own, v_earlier):
    def body(e_ref, inverse_ref, delta_ref, qt_ref, g_ref, own_ref, *refs):
        earlier_refs, ds_ref = refs[: z.steps], refs[z.steps]
        dk_own, dk_earlier = refs[z.steps + 1], refs[z.steps + 2 : 2 * z.steps + 2]
        v_all, dk_all = refs[2 * z.steps + 2 :]
        for head in range(z.heads):
            at = slice(head * HEAD_SIZE, (head + 1) * HEAD_SIZE)
            for number in range(z.total):
                v_all[number] = z.block(own_ref, earlier_refs, number)[:, at]
            dk_all[...] = jnp.zeros_like(dk_all)

            @pl.loop(0, z.group)
            def _(b):
                g = g_ref[head, b]
                q = (qt_ref[head, b].astype(jnp.float32) * inverse_ref[head, b]).astype(jnp.bfloat16)
                for c in range(z.span):
                    dp = lax.dot_general(v_all[b + c], g, NN, preferred_element_type=jnp.float32)
                    ds = e_ref[head, b, c] * (dp - delta_ref[head, b]).astype(jnp.bfloat16)
                    ds_ref[head, b, c] = ds
                    dk_all[b + c] += lax.dot_general(ds, q, NT, preferred_element_type=jnp.float32)

            for number in range(z.total):
                part = dk_all[number] * score_scale
                z.block(dk_own, dk_earlier, number)[:, at] = part.astype(
                    dk_own.dtype if number >= z.back else jnp.bfloat16
                )

    outs = [jax.ShapeDtypeStruct(e.shape, jnp.bfloat16)]
    outs += [jax.ShapeDtypeStruct((z.group, z.tokens, z.kv_width), jnp.float32)]
    outs += [jax.ShapeDtypeStruct((z.group, z.tokens, z.kv_width), jnp.bfloat16)] * z.steps
    scratch = [
        pltpu.VMEM((z.total, z.tokens, HEAD_SIZE), jnp.bfloat16),
        pltpu.VMEM((z.total, z.tokens, HEAD_SIZE), jnp.float32),
    ]
    results = call(body, outs, scratch, flops=4 * z.entries * HEAD_SIZE)(
        e, inverse, delta, qt, g, v_own, *v_earlier
    )
    return results[0], results[1], results[2:]


def query_terms(z, ds, inverse, k_own, k_earlier, dv_terms):
    def body(ds_ref, inverse_ref, own_ref, *refs):
        earlier_refs, term_refs, dv_ref = refs[: z.steps], refs[z.steps : 2 * z.steps + 1], refs[2 * z.steps + 1]
        dq_refs = refs[2 * z.steps + 2 : 2 * z.steps + 2 + z.group]
        kt_all, dq_all = refs[2 * z.steps + 2 + z.group :]
        dv = term_refs[0][...]
        for term in term_refs[1:]:
            dv = dv + term[...].astype(jnp.float32)
        dv_ref[...] = dv.astype(jnp.bfloat16)
        for head in range(z.heads):
            at = slice(head * HEAD_SIZE, (head + 1) * HEAD_SIZE)
            for number in range(z.total):
                kt_all[number] = z.block(own_ref, earlier_refs, number)[:, at].T

            @pl.loop(0, z.group)
            def _(b):
                dqt = jnp.zeros((HEAD_SIZE, z.wide), jnp.float32)
                for c in range(z.span):
                    dqt = dqt + lax.dot_general(
                        kt_all[b + c], ds_ref[head, b, c], NN, preferred_element_type=jnp.float32
                    )
                dqt = dqt * (inverse_ref[head, b] * score_scale)
                for j in range(z.per_head):
                    lower = (head * z.per_head + j) * HEAD_SIZE
                    dq_all[b, :, lower : lower + HEAD_SIZE] = (
                        dqt[:, j * z.tokens : (j + 1) * z.tokens].T.astype(jnp.bfloat16)
                    )

        for r in range(z.group):
            dq_refs[r][...] = dq_all[spot(z.group)[0] ^ r]

    outs = [jax.ShapeDtypeStruct((z.group, z.tokens, z.kv_width), jnp.bfloat16)]
    outs += [jax.ShapeDtypeStruct((z.tokens, z.width), jnp.bfloat16)] * z.group
    scratch = [
        pltpu.VMEM((z.total, HEAD_SIZE, z.tokens), jnp.bfloat16),
        pltpu.VMEM((z.group, z.tokens, z.width), jnp.bfloat16),
    ]
    results = call(body, outs, scratch, flops=2 * z.entries * HEAD_SIZE)(
        ds, inverse, k_own, *k_earlier, *dv_terms
    )
    return results[0], results[1:]


def pack_terms(group, sums):
    tokens, width = sums[0][0].shape[1:]
    flat = [term for terms in sums for term in terms]

    def body(*refs):
        for r in range(group):
            member = spot(group)[0] ^ r
            number = 0
            for column, terms in enumerate(sums):
                total = refs[number][member].astype(jnp.float32)
                for term in refs[number + 1 : number + len(terms)]:
                    total = total + term[member].astype(jnp.float32)
                refs[len(flat) + r][:, column * width : (column + 1) * width] = total.astype(jnp.bfloat16)
                number += len(terms)

    outs = [jax.ShapeDtypeStruct((tokens, len(sums) * width), jnp.bfloat16)] * group
    return call(body, outs)(*flat)


def unpack(group, pieces, widths):
    tokens = pieces[0].shape[0]

    def body(*refs):
        for r in range(group):
            lower = 0
            for number, width in enumerate(widths):
                refs[group + number][:, lanes(spot(group)[0] ^ r, width)] = refs[r][:, lower : lower + width]
                lower += width

    outs = [jax.ShapeDtypeStruct((tokens, group * width), jnp.bfloat16) for width in widths]
    return call(body, outs)(*pieces)


def local(layer_cotangent, out_weight, queries, keys, values):
    tokens = queries.shape[0]
    kv_heads = keys.shape[1] // HEAD_SIZE
    per_head = queries.shape[1] // keys.shape[1]
    count, tp_count = lax.axis_size("ctx"), lax.axis_size("tp")
    group = 1
    while (
        kv_heads % (2 * group) == 0
        and count % (2 * group) == 0
        and WINDOW_LENGTH % (2 * group * tokens) == 0
    ):
        group *= 2
    heads = kv_heads // group
    kv_width = heads * HEAD_SIZE
    back_groups = WINDOW_LENGTH // (group * tokens)
    def trade(sent):
        return [sent[0]] + [swapped(sent[r], "ctx", r) for r in range(1, group)]

    def returned(earlier):
        return [
            shifted(earlier[number], "ctx", -group * (back_groups - number)) for number in range(back_groups)
        ]

    sent = pack_kv(group, keys, values, begin())
    kv_pieces = trade(sent)
    z = Shape(group, back_groups, heads, per_head, tokens)
    query_sent = pack_queries(group, queries, sent[0])
    query_pieces = trade(query_sent)
    if tp_count == 2:
        other = head_product(2, 1, out_weight, layer_cotangent, [query_sent[0]])
        mine = head_product(2, 0, out_weight, layer_cotangent, [other])
        terms = [mine, swapped(other, "tp", 1)]
    else:
        mine = head_product(1, 0, out_weight, layer_cotangent, [query_sent[0]])
        terms = [lax.psum_scatter(mine, "tp", scatter_dimension=0, tiled=True)]
    k_own, v_own = order_kv(group, kv_pieces, mine)
    k_earlier, v_earlier = (
        [shifted(own, "ctx", group * step) for step in range(back_groups, 0, -1)] for own in (k_own, v_own)
    )
    qt = turn_queries(z, query_pieces)
    grads = trade(pack_grads(group, terms, k_own))
    e = softmax(z, k_own, k_earlier, qt)
    (g, inverse, delta), dv_own, dv_earlier = value_terms(z, e, grads, v_own, v_earlier)
    dv_terms = [dv_own] + returned(dv_earlier)
    ds, dk_own, dk_earlier = key_terms(z, e, inverse, delta, qt, g, v_own, v_earlier)
    dk_terms = [dk_own] + returned(dk_earlier)
    dv, dq = query_terms(z, ds, inverse, k_own, k_earlier, dv_terms)
    dq = trade(dq)
    dkv = trade(pack_terms(group, [dk_terms, [dv]]))
    (query_grads,) = unpack(group, dq, [dq[0].shape[1]])
    key_gradients, value_gradients = unpack(group, dkv, [kv_width, kv_width])
    return (query_grads, key_gradients, value_gradients)


def solution(mesh):
    in_specs = (P("ctx", "tp"), P(None, "tp"), P("ctx", "tp"), P("ctx", "tp"), P("ctx", "tp"))
    out_specs = (P("ctx", "tp"), P("ctx", "tp"), P("ctx", "tp"))
    return jax.shard_map(local, mesh=mesh, in_specs=in_specs, out_specs=out_specs, check_vma=False)
```

```python
import functools

import jax
import jax.numpy as jnp
from jax import lax
from jax.experimental import pallas as pl
from jax.experimental.pallas import tpu as pltpu
from jax.sharding import PartitionSpec as P

HEAD_SIZE = 128
WINDOW_LENGTH = 1024
LOG2_E = 1.4426950408889634
AHEAD = 10**10

score_scale = 168.0 ** (-0.5)

VMEM = pl.BlockSpec(memory_space=pltpu.VMEM)
ANY = pl.BlockSpec(memory_space=pl.ANY)
SMEM = pl.BlockSpec(memory_space=pltpu.SMEM)
NT = (((1,), (1,)), ((), ()))
NN = (((1,), (0,)), ((), ()))


def shifted(value, axis, steps):
    count = lax.axis_size(axis)
    leading, last = (max(0, -steps), min(count, count - steps))
    return lax.ppermute(value, axis, [(source, source + steps) for source in range(leading, last)])


def swapped(value, axis, bits):
    count = lax.axis_size(axis)
    return lax.ppermute(value, axis, [(source, source ^ bits) for source in range(count)])


def call(body, outs, scratch=(), flops=0, exps=0, specs=None, vmem=32):
    def run(*args):
        moved = sum(a.size * a.dtype.itemsize for a in args)
        moved += sum(o.size * o.dtype.itemsize for o in outs)
        return pl.pallas_call(
            body,
            out_shape=tuple(outs),
            in_specs=specs or [SMEM if a.dtype == jnp.int32 else VMEM for a in args],
            out_specs=tuple(VMEM for _ in outs),
            scratch_shapes=list(scratch),
            compiler_params=pltpu.CompilerParams(vmem_limit_bytes=vmem * 1024 * 1024),
            cost_estimate=pl.CostEstimate(flops=flops, bytes_accessed=moved, transcendentals=exps),
        )(*args)

    return run


def spot(group):
    index = lax.axis_index("ctx")
    place = lax.rem(index, group)
    return place, index - place


def lanes(index, width):
    return pl.ds(pl.multiple_of(index * width, width), width)


def begin():
    def body(out_ref):
        out_ref[...] = jnp.zeros_like(out_ref)

    return call(body, [jax.ShapeDtypeStruct((8, 128), jnp.float32)], flops=AHEAD)()[0]


def pack_kv(group, keys, values, before):
    tokens, width = keys.shape[0], keys.shape[1] // group

    def body(k_ref, v_ref, before_ref, *refs):
        for r in range(group):
            member = spot(group)[0] ^ r
            refs[r][:, :width] = k_ref[:, lanes(member, width)]
            refs[r][:, width:] = v_ref[:, lanes(member, width)]

    outs = [jax.ShapeDtypeStruct((tokens, 2 * width), jnp.bfloat16)] * group
    return call(body, outs, flops=AHEAD, specs=[VMEM, VMEM, ANY])(keys, values, before)


def pack_queries(group, queries, before):
    tokens, width = queries.shape[0], queries.shape[1] // group

    def body(q_ref, before_ref, *out_refs):
        for r in range(group):
            out_refs[r][...] = q_ref[:, lanes(spot(group)[0] ^ r, width)]

    outs = [jax.ShapeDtypeStruct((tokens, width), jnp.bfloat16)] * group
    return call(body, outs, specs=[VMEM, ANY])(queries, before)


def order_kv(group, pieces, before):
    tokens, width = pieces[0].shape
    width //= 2

    def body(*refs):
        for r in range(group):
            member = spot(group)[0] ^ r
            refs[-2][member] = refs[r][:, :width]
            refs[-1][member] = refs[r][:, width:]

    outs = [jax.ShapeDtypeStruct((group, tokens, width), jnp.bfloat16)] * 2
    return call(body, outs, flops=AHEAD, specs=[VMEM] * group + [ANY])(*pieces, before)


def head_product(parts, part, out_weight, layer_cotangent, before):
    tokens, depth = layer_cotangent.shape
    rows = out_weight.shape[0] // parts
    tile = min(rows, 512)

    def body(w_ref, c_ref, *refs):
        first = (lax.axis_index("tp") ^ part) * rows if parts > 1 else 0

        @pl.loop(0, rows // tile)
        def _(i):
            here = pl.ds(pl.multiple_of(i * tile, tile), tile)
            there = pl.ds(pl.multiple_of(first + i * tile, tile), tile)
            refs[-1][here, :] = lax.dot_general(
                w_ref[there, :], c_ref[...], NT, preferred_element_type=jnp.float32
            ).astype(jnp.bfloat16)

    outs = [jax.ShapeDtypeStruct((rows, tokens), jnp.bfloat16)]
    specs = [VMEM, VMEM] + [ANY] * len(before)
    return call(body, outs, flops=2 * rows * tokens * depth, specs=specs, vmem=16)(
        out_weight, layer_cotangent, *before
    )[0]


def pack_grads(group, terms, before):
    rows, tokens = terms[0].shape
    rows //= group

    def body(*refs):
        for r in range(group):
            there = lanes(spot(group)[0] ^ r, rows)
            total = refs[0][there, :]
            if len(terms) > 1:
                total = total.astype(jnp.float32)
                for term in refs[1 : len(terms)]:
                    total = total + term[there, :].astype(jnp.float32)
            refs[len(terms) + 1 + r][...] = total.astype(jnp.bfloat16)

    outs = [jax.ShapeDtypeStruct((rows, tokens), jnp.bfloat16)] * group
    return call(body, outs, specs=[VMEM] * len(terms) + [ANY])(*terms, before)


class Shape:
    def __init__(self, group, steps, heads, per_head, tokens):
        self.group, self.steps, self.heads, self.per_head, self.tokens = group, steps, heads, per_head, tokens
        self.back = steps * group
        self.span = self.back + 1
        self.total = self.back + group
        self.wide = per_head * tokens
        self.width = heads * per_head * HEAD_SIZE
        self.kv_width = heads * HEAD_SIZE
        self.entries = group * heads * self.wide * self.span * tokens

    def block(self, own_ref, earlier_refs, number):
        if number < self.back:
            return earlier_refs[number // self.group].at[number % self.group]
        return own_ref.at[number - self.back]


def turn_queries(z, pieces):
    def body(*refs):
        for head in range(z.heads):
            for r in range(z.group):
                for j in range(z.per_head):
                    lower = (head * z.per_head + j) * HEAD_SIZE
                    refs[z.group][head, spot(z.group)[0] ^ r, :, j * z.tokens : (j + 1) * z.tokens] = refs[r][
                        :, lower : lower + HEAD_SIZE
                    ].T

    outs = [jax.ShapeDtypeStruct((z.heads, z.group, HEAD_SIZE, z.wide), jnp.bfloat16)]
    return call(body, outs)(*pieces)[0]


def softmax(z, k_own, k_earlier, qt):
    factor = score_scale * LOG2_E

    def body(own_ref, *refs):
        earlier_refs = refs[: z.steps]
        qt_ref, e_ref, inverse_ref, k_all, s_all = refs[z.steps :]
        first = spot(z.group)[1]
        key_id = lax.broadcasted_iota(jnp.int32, (z.tokens, z.wide), 0)
        query_id = lax.broadcasted_iota(jnp.int32, (z.tokens, z.wide), 1) & (z.tokens - 1)
        for head in range(z.heads):
            at = slice(head * HEAD_SIZE, (head + 1) * HEAD_SIZE)
            for number in range(z.total):
                k_all[number] = z.block(own_ref, earlier_refs, number)[:, at]

            @pl.loop(0, z.group)
            def _(b):
                qt = qt_ref[head, b]
                top = None
                for c in range(z.span):
                    s = lax.dot_general(k_all[b + c], qt, NN, preferred_element_type=jnp.float32)
                    if c == 0:
                        s = jnp.where(key_id > query_id, s, -jnp.inf)
                    if c == z.back:
                        s = jnp.where(key_id <= query_id, s, -jnp.inf)
                    s_all[c] = s
                    here = jnp.max(s, axis=0, keepdims=True)
                    if c < z.back:
                        here = jnp.where(first + b + c >= z.back, here, -jnp.inf)
                    top = here if top is None else jnp.maximum(top, here)
                norm = jnp.zeros((1, z.wide), jnp.float32)
                for c in range(z.span):
                    base = top
                    if c < z.back:
                        base = jnp.where(first + b + c >= z.back, top, jnp.inf)
                    e = jnp.exp2((s_all[c] - base) * factor)
                    norm = norm + jnp.sum(e, axis=0, keepdims=True)
                    e_ref[head, b, c] = e.astype(jnp.bfloat16)
                inverse_ref[head, b] = 1.0 / norm

    outs = [
        jax.ShapeDtypeStruct((z.heads, z.group, z.span, z.tokens, z.wide), jnp.bfloat16),
        jax.ShapeDtypeStruct((z.heads, z.group, 1, z.wide), jnp.float32),
    ]
    scratch = [
        pltpu.VMEM((z.total, z.tokens, HEAD_SIZE), jnp.bfloat16),
        pltpu.VMEM((z.span, z.tokens, z.wide), jnp.float32),
    ]
    return call(body, outs, scratch, flops=2 * z.entries * HEAD_SIZE, exps=z.entries)(
        k_own, *k_earlier, qt
    )


def value_terms(z, e, inverse, grads):
    def body(e_ref, inverse_ref, *refs):
        g_refs, (g_ref, own_ref), earlier_refs = (
            refs[: z.group],
            refs[z.group : z.group + 2],
            refs[z.group + 2 : z.group + 2 + z.steps],
        )
        dv_all = refs[-1]
        place = spot(z.group)[0]
        for head in range(z.heads):
            at = slice(head * HEAD_SIZE, (head + 1) * HEAD_SIZE)
            for r in range(z.group):
                for j in range(z.per_head):
                    lower = (head * z.per_head + j) * HEAD_SIZE
                    g_ref[head, place ^ r, :, j * z.tokens : (j + 1) * z.tokens] = g_refs[r][
                        lower : lower + HEAD_SIZE, :
                    ]
            dv_all[...] = jnp.zeros_like(dv_all)

            @pl.loop(0, z.group)
            def _(b):
                g = (g_ref[head, b].astype(jnp.float32) * inverse_ref[head, b]).astype(jnp.bfloat16)
                for c in range(z.span):
                    dv_all[b + c] += lax.dot_general(
                        e_ref[head, b, c], g, NT, preferred_element_type=jnp.float32
                    )

            for number in range(z.total):
                z.block(own_ref, earlier_refs, number)[:, at] = dv_all[number].astype(
                    own_ref.dtype if number >= z.back else jnp.bfloat16
                )

    outs = [
        jax.ShapeDtypeStruct((z.heads, z.group, HEAD_SIZE, z.wide), jnp.bfloat16),
        jax.ShapeDtypeStruct((z.group, z.tokens, z.kv_width), jnp.float32),
    ]
    outs += [jax.ShapeDtypeStruct((z.group, z.tokens, z.kv_width), jnp.bfloat16)] * z.steps
    scratch = [pltpu.VMEM((z.total, z.tokens, HEAD_SIZE), jnp.float32)]
    results = call(body, outs, scratch, flops=2 * z.entries * HEAD_SIZE)(e, inverse, *grads)
    return results[0], results[1], results[2:]


def key_terms(z, e, inverse, qt, g, v_own, v_earlier):
    def body(e_ref, inverse_ref, qt_ref, g_ref, own_ref, *refs):
        earlier_refs, ds_ref = refs[: z.steps], refs[z.steps]
        dk_own, dk_earlier = refs[z.steps + 1], refs[z.steps + 2 : 2 * z.steps + 2]
        v_all, dk_all, dp_all = refs[2 * z.steps + 2 :]
        for head in range(z.heads):
            at = slice(head * HEAD_SIZE, (head + 1) * HEAD_SIZE)
            for number in range(z.total):
                v_all[number] = z.block(own_ref, earlier_refs, number)[:, at]
            dk_all[...] = jnp.zeros_like(dk_all)

            @pl.loop(0, z.group)
            def _(b):
                g = g_ref[head, b]
                inverse = inverse_ref[head, b]
                delta = jnp.zeros((1, z.wide), jnp.float32)
                for c in range(z.span):
                    dp = lax.dot_general(v_all[b + c], g, NN, preferred_element_type=jnp.float32)
                    delta = delta + jnp.sum(e_ref[head, b, c].astype(jnp.float32) * dp, axis=0, keepdims=True)
                    dp_all[c] = dp
                delta = delta * inverse
                q = (qt_ref[head, b].astype(jnp.float32) * inverse).astype(jnp.bfloat16)
                for c in range(z.span):
                    ds = e_ref[head, b, c] * (dp_all[c] - delta).astype(jnp.bfloat16)
                    ds_ref[head, b, c] = ds
                    dk_all[b + c] += lax.dot_general(ds, q, NT, preferred_element_type=jnp.float32)

            for number in range(z.total):
                part = dk_all[number] * score_scale
                z.block(dk_own, dk_earlier, number)[:, at] = part.astype(
                    dk_own.dtype if number >= z.back else jnp.bfloat16
                )

    outs = [jax.ShapeDtypeStruct(e.shape, jnp.bfloat16)]
    outs += [jax.ShapeDtypeStruct((z.group, z.tokens, z.kv_width), jnp.float32)]
    outs += [jax.ShapeDtypeStruct((z.group, z.tokens, z.kv_width), jnp.bfloat16)] * z.steps
    scratch = [
        pltpu.VMEM((z.total, z.tokens, HEAD_SIZE), jnp.bfloat16),
        pltpu.VMEM((z.total, z.tokens, HEAD_SIZE), jnp.float32),
        pltpu.VMEM((z.span, z.tokens, z.wide), jnp.float32),
    ]
    results = call(body, outs, scratch, flops=4 * z.entries * HEAD_SIZE)(
        e, inverse, qt, g, v_own, *v_earlier
    )
    return results[0], results[1], results[2:]


def query_terms(z, ds, inverse, k_own, k_earlier, dv_terms):
    def body(ds_ref, inverse_ref, own_ref, *refs):
        earlier_refs, term_refs, dv_ref = refs[: z.steps], refs[z.steps : 2 * z.steps + 1], refs[2 * z.steps + 1]
        dq_refs = refs[2 * z.steps + 2 : 2 * z.steps + 2 + z.group]
        kt_all, dq_all = refs[2 * z.steps + 2 + z.group :]
        dv = term_refs[0][...]
        for term in term_refs[1:]:
            dv = dv + term[...].astype(jnp.float32)
        dv_ref[...] = dv.astype(jnp.bfloat16)
        for head in range(z.heads):
            at = slice(head * HEAD_SIZE, (head + 1) * HEAD_SIZE)
            for number in range(z.total):
                kt_all[number] = z.block(own_ref, earlier_refs, number)[:, at].T

            @pl.loop(0, z.group)
            def _(b):
                dqt = jnp.zeros((HEAD_SIZE, z.wide), jnp.float32)
                for c in range(z.span):
                    dqt = dqt + lax.dot_general(
                        kt_all[b + c], ds_ref[head, b, c], NN, preferred_element_type=jnp.float32
                    )
                dqt = dqt * (inverse_ref[head, b] * score_scale)
                for j in range(z.per_head):
                    lower = (head * z.per_head + j) * HEAD_SIZE
                    dq_all[b, :, lower : lower + HEAD_SIZE] = (
                        dqt[:, j * z.tokens : (j + 1) * z.tokens].T.astype(jnp.bfloat16)
                    )

        for r in range(z.group):
            dq_refs[r][...] = dq_all[spot(z.group)[0] ^ r]

    outs = [jax.ShapeDtypeStruct((z.group, z.tokens, z.kv_width), jnp.bfloat16)]
    outs += [jax.ShapeDtypeStruct((z.tokens, z.width), jnp.bfloat16)] * z.group
    scratch = [
        pltpu.VMEM((z.total, HEAD_SIZE, z.tokens), jnp.bfloat16),
        pltpu.VMEM((z.group, z.tokens, z.width), jnp.bfloat16),
    ]
    results = call(body, outs, scratch, flops=2 * z.entries * HEAD_SIZE)(
        ds, inverse, k_own, *k_earlier, *dv_terms
    )
    return results[0], results[1:]


def pack_terms(group, sums):
    tokens, width = sums[0][0].shape[1:]
    flat = [term for terms in sums for term in terms]

    def body(*refs):
        for r in range(group):
            member = spot(group)[0] ^ r
            number = 0
            for column, terms in enumerate(sums):
                total = refs[number][member].astype(jnp.float32)
                for term in refs[number + 1 : number + len(terms)]:
                    total = total + term[member].astype(jnp.float32)
                refs[len(flat) + r][:, column * width : (column + 1) * width] = total.astype(jnp.bfloat16)
                number += len(terms)

    outs = [jax.ShapeDtypeStruct((tokens, len(sums) * width), jnp.bfloat16)] * group
    return call(body, outs)(*flat)


def unpack(group, pieces, widths):
    tokens = pieces[0].shape[0]

    def body(*refs):
        for r in range(group):
            lower = 0
            for number, width in enumerate(widths):
                refs[group + number][:, lanes(spot(group)[0] ^ r, width)] = refs[r][:, lower : lower + width]
                lower += width

    outs = [jax.ShapeDtypeStruct((tokens, group * width), jnp.bfloat16) for width in widths]
    return call(body, outs)(*pieces)


def local(layer_cotangent, out_weight, queries, keys, values):
    tokens = queries.shape[0]
    kv_heads = keys.shape[1] // HEAD_SIZE
    per_head = queries.shape[1] // keys.shape[1]
    count, tp_count = lax.axis_size("ctx"), lax.axis_size("tp")
    group = 1
    while (
        kv_heads % (2 * group) == 0
        and count % (2 * group) == 0
        and WINDOW_LENGTH % (2 * group * tokens) == 0
    ):
        group *= 2
    heads = kv_heads // group
    kv_width = heads * HEAD_SIZE
    back_groups = WINDOW_LENGTH // (group * tokens)
    def trade(sent):
        return [sent[0]] + [swapped(sent[r], "ctx", r) for r in range(1, group)]

    def returned(earlier):
        return [
            shifted(earlier[number], "ctx", -group * (back_groups - number)) for number in range(back_groups)
        ]

    sent = pack_kv(group, keys, values, begin())
    kv_pieces = trade(sent)
    z = Shape(group, back_groups, heads, per_head, tokens)
    query_sent = pack_queries(group, queries, sent[0])
    query_pieces = trade(query_sent)
    qt = turn_queries(z, query_pieces)
    if tp_count == 2:
        other = head_product(2, 1, out_weight, layer_cotangent, [query_sent[0]])
        mine = head_product(2, 0, out_weight, layer_cotangent, [other, qt])
        terms = [mine, swapped(other, "tp", 1)]
    else:
        other = head_product(1, 0, out_weight, layer_cotangent, [query_sent[0]])
        terms = [lax.psum_scatter(other, "tp", scatter_dimension=0, tiled=True)]
    k_own, v_own = order_kv(group, kv_pieces, other)
    k_earlier, v_earlier = (
        [shifted(own, "ctx", group * step) for step in range(back_groups, 0, -1)] for own in (k_own, v_own)
    )
    grads = trade(pack_grads(group, terms, qt))
    e, inverse = softmax(z, k_own, k_earlier, qt)
    g, dv_own, dv_earlier = value_terms(z, e, inverse, grads)
    dv_terms = [dv_own] + returned(dv_earlier)
    ds, dk_own, dk_earlier = key_terms(z, e, inverse, qt, g, v_own, v_earlier)
    dk_terms = [dk_own] + returned(dk_earlier)
    dv, dq = query_terms(z, ds, inverse, k_own, k_earlier, dv_terms)
    dq = trade(dq)
    dkv = trade(pack_terms(group, [dk_terms, [dv]]))
    (query_grads,) = unpack(group, dq, [dq[0].shape[1]])
    key_gradients, value_gradients = unpack(group, dkv, [kv_width, kv_width])
    return (query_grads, key_gradients, value_gradients)


def solution(mesh):
    in_specs = (P("ctx", "tp"), P(None, "tp"), P("ctx", "tp"), P("ctx", "tp"), P("ctx", "tp"))
    out_specs = (P("ctx", "tp"), P("ctx", "tp"), P("ctx", "tp"))
    return jax.shard_map(local, mesh=mesh, in_specs=in_specs, out_specs=out_specs, check_vma=False)
```

```python
import functools

import jax
import jax.numpy as jnp
from jax import lax
from jax.experimental import pallas as pl
from jax.experimental.pallas import tpu as pltpu
from jax.sharding import PartitionSpec as P

HEAD_SIZE = 128
WINDOW_LENGTH = 1024
LOG2_E = 1.4426950408889634
AHEAD = 10**10

score_scale = 168.0 ** (-0.5)

VMEM = pl.BlockSpec(memory_space=pltpu.VMEM)
ANY = pl.BlockSpec(memory_space=pl.ANY)
SMEM = pl.BlockSpec(memory_space=pltpu.SMEM)
NT = (((1,), (1,)), ((), ()))
NN = (((1,), (0,)), ((), ()))


def shifted(value, axis, steps):
    count = lax.axis_size(axis)
    leading, last = (max(0, -steps), min(count, count - steps))
    return lax.ppermute(value, axis, [(source, source + steps) for source in range(leading, last)])


def swapped(value, axis, bits):
    count = lax.axis_size(axis)
    return lax.ppermute(value, axis, [(source, source ^ bits) for source in range(count)])


def call(body, outs, scratch=(), flops=0, exps=0, specs=None, vmem=32):
    def run(*args):
        moved = sum(a.size * a.dtype.itemsize for a in args)
        moved += sum(o.size * o.dtype.itemsize for o in outs)
        return pl.pallas_call(
            body,
            out_shape=tuple(outs),
            in_specs=specs or [SMEM if a.dtype == jnp.int32 else VMEM for a in args],
            out_specs=tuple(VMEM for _ in outs),
            scratch_shapes=list(scratch),
            compiler_params=pltpu.CompilerParams(vmem_limit_bytes=vmem * 1024 * 1024),
            cost_estimate=pl.CostEstimate(flops=flops, bytes_accessed=moved, transcendentals=exps),
        )(*args)

    return run


def spot(group):
    index = lax.axis_index("ctx")
    place = lax.rem(index, group)
    return place, index - place


def lanes(index, width):
    return pl.ds(pl.multiple_of(index * width, width), width)


def begin():
    def body(out_ref):
        out_ref[...] = jnp.zeros_like(out_ref)

    return call(body, [jax.ShapeDtypeStruct((8, 128), jnp.float32)], flops=AHEAD)()[0]


def pack_kv(group, keys, values, before):
    tokens, width = keys.shape[0], keys.shape[1] // group

    def body(k_ref, v_ref, before_ref, *refs):
        for r in range(group):
            member = spot(group)[0] ^ r
            refs[r][:, :width] = k_ref[:, lanes(member, width)]
            refs[r][:, width:] = v_ref[:, lanes(member, width)]

    outs = [jax.ShapeDtypeStruct((tokens, 2 * width), jnp.bfloat16)] * group
    return call(body, outs, flops=AHEAD, specs=[VMEM, VMEM, ANY])(keys, values, before)


def pack_queries(group, queries, before):
    tokens, width = queries.shape[0], queries.shape[1] // group

    def body(q_ref, before_ref, *out_refs):
        for r in range(group):
            out_refs[r][...] = q_ref[:, lanes(spot(group)[0] ^ r, width)]

    outs = [jax.ShapeDtypeStruct((tokens, width), jnp.bfloat16)] * group
    return call(body, outs, specs=[VMEM, ANY])(queries, before)


def order_pieces(group, pieces, before):
    def body(*refs):
        for r in range(group):
            refs[-1][spot(group)[0] ^ r] = refs[r][...]

    outs = [jax.ShapeDtypeStruct((group,) + pieces[0].shape, jnp.bfloat16)]
    return call(body, outs, specs=[VMEM] * group + [ANY])(*pieces, before)[0]


def head_product(parts, part, out_weight, layer_cotangent, before):
    tokens, depth = layer_cotangent.shape
    rows = out_weight.shape[0] // parts
    tile = min(rows, 512)

    def body(w_ref, c_ref, *refs):
        first = (lax.axis_index("tp") ^ part) * rows if parts > 1 else 0

        @pl.loop(0, rows // tile)
        def _(i):
            here = pl.ds(pl.multiple_of(i * tile, tile), tile)
            there = pl.ds(pl.multiple_of(first + i * tile, tile), tile)
            refs[-1][here, :] = lax.dot_general(
                w_ref[there, :], c_ref[...], NT, preferred_element_type=jnp.float32
            ).astype(jnp.bfloat16)

    outs = [jax.ShapeDtypeStruct((rows, tokens), jnp.bfloat16)]
    specs = [VMEM, VMEM] + [ANY] * len(before)
    return call(body, outs, flops=2 * rows * tokens * depth, specs=specs, vmem=16)(
        out_weight, layer_cotangent, *before
    )[0]


def pack_grads(group, terms):
    rows, tokens = terms[0].shape
    rows //= group

    def body(*refs):
        for r in range(group):
            there = lanes(spot(group)[0] ^ r, rows)
            total = refs[0][there, :]
            if len(terms) > 1:
                total = total.astype(jnp.float32)
                for term in refs[1 : len(terms)]:
                    total = total + term[there, :].astype(jnp.float32)
            refs[len(terms) + r][...] = total.astype(jnp.bfloat16)

    outs = [jax.ShapeDtypeStruct((rows, tokens), jnp.bfloat16)] * group
    return call(body, outs)(*terms)


class Shape:
    def __init__(self, group, steps, heads, per_head, tokens):
        self.group, self.steps, self.heads, self.per_head, self.tokens = group, steps, heads, per_head, tokens
        self.back = steps * group
        self.span = self.back + 1
        self.total = self.back + group
        self.wide = per_head * tokens
        self.width = heads * per_head * HEAD_SIZE
        self.kv_width = heads * HEAD_SIZE
        self.entries = group * heads * self.wide * self.span * tokens

    def block(self, own_ref, earlier_refs, number):
        if number < self.back:
            return earlier_refs[number // self.group].at[number % self.group]
        return own_ref.at[number - self.back]


def turn_queries(z, pieces):
    def body(*refs):
        for head in range(z.heads):
            for r in range(z.group):
                for j in range(z.per_head):
                    lower = (head * z.per_head + j) * HEAD_SIZE
                    refs[z.group][head, spot(z.group)[0] ^ r, :, j * z.tokens : (j + 1) * z.tokens] = refs[r][
                        :, lower : lower + HEAD_SIZE
                    ].T

    outs = [jax.ShapeDtypeStruct((z.heads, z.group, HEAD_SIZE, z.wide), jnp.bfloat16)]
    return call(body, outs)(*pieces)[0]


def softmax(z, kv_own, kv_earlier, qt):
    factor = score_scale * LOG2_E

    def body(*refs):
        own_ref, earlier_refs = refs[0], refs[1 : 1 + z.steps]
        qt_ref, e_ref, inverse_ref, k_all, s_all = refs[1 + z.steps :]
        first = spot(z.group)[1]
        key_id = lax.broadcasted_iota(jnp.int32, (z.tokens, z.wide), 0)
        query_id = lax.broadcasted_iota(jnp.int32, (z.tokens, z.wide), 1) & (z.tokens - 1)
        for head in range(z.heads):
            at_k = slice(head * HEAD_SIZE, (head + 1) * HEAD_SIZE)
            for number in range(z.total):
                k_all[number] = z.block(own_ref, earlier_refs, number)[:, at_k]

            @pl.loop(0, z.group)
            def _(b):
                qt = qt_ref[head, b]
                top = None
                for c in range(z.span):
                    s = lax.dot_general(k_all[b + c], qt, NN, preferred_element_type=jnp.float32)
                    if c == 0:
                        s = jnp.where(key_id > query_id, s, -jnp.inf)
                    if c == z.back:
                        s = jnp.where(key_id <= query_id, s, -jnp.inf)
                    s_all[c] = s
                    here = jnp.max(s, axis=0, keepdims=True)
                    if c < z.back:
                        here = jnp.where(first + b + c >= z.back, here, -jnp.inf)
                    top = here if top is None else jnp.maximum(top, here)
                norm = jnp.zeros((1, z.wide), jnp.float32)
                for c in range(z.span):
                    base = top
                    if c < z.back:
                        base = jnp.where(first + b + c >= z.back, top, jnp.inf)
                    e = jnp.exp2((s_all[c] - base) * factor)
                    norm = norm + jnp.sum(e, axis=0, keepdims=True)
                    e_ref[head, b, c] = e.astype(jnp.bfloat16)
                inverse_ref[head, b] = 1.0 / norm

    outs = [
        jax.ShapeDtypeStruct((z.heads, z.group, z.span, z.tokens, z.wide), jnp.bfloat16),
        jax.ShapeDtypeStruct((z.heads, z.group, 1, z.wide), jnp.float32),
    ]
    scratch = [
        pltpu.VMEM((z.total, z.tokens, HEAD_SIZE), jnp.bfloat16),
        pltpu.VMEM((z.span, z.tokens, z.wide), jnp.float32),
    ]
    return call(body, outs, scratch, flops=2 * z.entries * HEAD_SIZE, exps=z.entries)(
        kv_own, *kv_earlier, qt
    )


def value_terms(z, e, inverse, grads):
    def body(e_ref, inverse_ref, *refs):
        g_refs, (g_ref, own_ref), earlier_refs = (
            refs[: z.group],
            refs[z.group : z.group + 2],
            refs[z.group + 2 : z.group + 2 + z.steps],
        )
        dv_all = refs[-1]
        place = spot(z.group)[0]
        for head in range(z.heads):
            at = slice(head * HEAD_SIZE, (head + 1) * HEAD_SIZE)
            for r in range(z.group):
                for j in range(z.per_head):
                    lower = (head * z.per_head + j) * HEAD_SIZE
                    g_ref[head, place ^ r, :, j * z.tokens : (j + 1) * z.tokens] = g_refs[r][
                        lower : lower + HEAD_SIZE, :
                    ]
            dv_all[...] = jnp.zeros_like(dv_all)

            @pl.loop(0, z.group)
            def _(b):
                g = (g_ref[head, b].astype(jnp.float32) * inverse_ref[head, b]).astype(jnp.bfloat16)
                for c in range(z.span):
                    dv_all[b + c] += lax.dot_general(
                        e_ref[head, b, c], g, NT, preferred_element_type=jnp.float32
                    )

            for number in range(z.total):
                part = dv_all[number]
                z.block(own_ref, earlier_refs, number)[:, at] = part.astype(own_ref.dtype if number >= z.back else jnp.bfloat16)

    outs = [
        jax.ShapeDtypeStruct((z.heads, z.group, HEAD_SIZE, z.wide), jnp.bfloat16),
        jax.ShapeDtypeStruct((z.group, z.tokens, z.kv_width), jnp.float32),
    ]
    outs += [jax.ShapeDtypeStruct((z.group, z.tokens, z.kv_width), jnp.bfloat16)] * z.steps
    scratch = [pltpu.VMEM((z.total, z.tokens, HEAD_SIZE), jnp.float32)]
    results = call(body, outs, scratch, flops=2 * z.entries * HEAD_SIZE)(e, inverse, *grads)
    return results[0], results[1], results[2:]


def key_terms(z, e, inverse, qt, g, kv_own, kv_earlier):
    def body(e_ref, inverse_ref, qt_ref, g_ref, own_ref, *refs):
        earlier_refs, ds_ref = refs[: z.steps], refs[z.steps]
        dk_own, dk_earlier = refs[z.steps + 1], refs[z.steps + 2 : 2 * z.steps + 2]
        v_all, dk_all, dp_all = refs[2 * z.steps + 2 :]
        for head in range(z.heads):
            at = slice(head * HEAD_SIZE, (head + 1) * HEAD_SIZE)
            at_v = slice(z.kv_width + head * HEAD_SIZE, z.kv_width + (head + 1) * HEAD_SIZE)
            for number in range(z.total):
                v_all[number] = z.block(own_ref, earlier_refs, number)[:, at_v]
            dk_all[...] = jnp.zeros_like(dk_all)

            @pl.loop(0, z.group)
            def _(b):
                g = g_ref[head, b]
                inverse = inverse_ref[head, b]
                delta = jnp.zeros((1, z.wide), jnp.float32)
                for c in range(z.span):
                    dp = lax.dot_general(v_all[b + c], g, NN, preferred_element_type=jnp.float32)
                    delta = delta + jnp.sum(e_ref[head, b, c].astype(jnp.float32) * dp, axis=0, keepdims=True)
                    dp_all[c] = dp
                delta = delta * inverse
                q = (qt_ref[head, b].astype(jnp.float32) * inverse).astype(jnp.bfloat16)
                for c in range(z.span):
                    ds = e_ref[head, b, c] * (dp_all[c] - delta).astype(jnp.bfloat16)
                    ds_ref[head, b, c] = ds
                    dk_all[b + c] += lax.dot_general(ds, q, NT, preferred_element_type=jnp.float32)

            for number in range(z.total):
                part = dk_all[number] * score_scale
                z.block(dk_own, dk_earlier, number)[:, at] = part.astype(
                    dk_own.dtype if number >= z.back else jnp.bfloat16
                )

    outs = [jax.ShapeDtypeStruct(e.shape, jnp.bfloat16)]
    outs += [jax.ShapeDtypeStruct((z.group, z.tokens, z.kv_width), jnp.float32)]
    outs += [jax.ShapeDtypeStruct((z.group, z.tokens, z.kv_width), jnp.bfloat16)] * z.steps
    scratch = [
        pltpu.VMEM((z.total, z.tokens, HEAD_SIZE), jnp.bfloat16),
        pltpu.VMEM((z.total, z.tokens, HEAD_SIZE), jnp.float32),
        pltpu.VMEM((z.span, z.tokens, z.wide), jnp.float32),
    ]
    results = call(body, outs, scratch, flops=4 * z.entries * HEAD_SIZE)(
        e, inverse, qt, g, kv_own, *kv_earlier
    )
    return results[0], results[1], results[2:]


def query_terms(z, ds, inverse, kv_own, kv_earlier, dv_terms):
    def body(ds_ref, inverse_ref, own_ref, *refs):
        earlier_refs, term_refs, dv_ref = refs[: z.steps], refs[z.steps : 2 * z.steps + 1], refs[2 * z.steps + 1]
        dq_refs = refs[2 * z.steps + 2 : 2 * z.steps + 2 + z.group]
        kt_all, dq_all = refs[2 * z.steps + 2 + z.group :]
        dv = term_refs[0][...]
        for term in term_refs[1:]:
            dv = dv + term[...].astype(jnp.float32)
        dv_ref[...] = dv.astype(jnp.bfloat16)
        for head in range(z.heads):
            at = slice(head * HEAD_SIZE, (head + 1) * HEAD_SIZE)
            for number in range(z.total):
                kt_all[number] = z.block(own_ref, earlier_refs, number)[:, at].T

            @pl.loop(0, z.group)
            def _(b):
                dqt = jnp.zeros((HEAD_SIZE, z.wide), jnp.float32)
                for c in range(z.span):
                    dqt = dqt + lax.dot_general(
                        kt_all[b + c], ds_ref[head, b, c], NN, preferred_element_type=jnp.float32
                    )
                dqt = dqt * (inverse_ref[head, b] * score_scale)
                for j in range(z.per_head):
                    lower = (head * z.per_head + j) * HEAD_SIZE
                    dq_all[b, :, lower : lower + HEAD_SIZE] = (
                        dqt[:, j * z.tokens : (j + 1) * z.tokens].T.astype(jnp.bfloat16)
                    )

        for r in range(z.group):
            dq_refs[r][...] = dq_all[spot(z.group)[0] ^ r]

    outs = [jax.ShapeDtypeStruct((z.group, z.tokens, z.kv_width), jnp.bfloat16)]
    outs += [jax.ShapeDtypeStruct((z.tokens, z.width), jnp.bfloat16)] * z.group
    scratch = [
        pltpu.VMEM((z.total, HEAD_SIZE, z.tokens), jnp.bfloat16),
        pltpu.VMEM((z.group, z.tokens, z.width), jnp.bfloat16),
    ]
    results = call(body, outs, scratch, flops=2 * z.entries * HEAD_SIZE)(
        ds, inverse, kv_own, *kv_earlier, *dv_terms
    )
    return results[0], results[1:]


def pack_terms(group, sums):
    tokens, width = sums[0][0].shape[1:]
    flat = [term for terms in sums for term in terms]

    def body(*refs):
        for r in range(group):
            member = spot(group)[0] ^ r
            number = 0
            for column, terms in enumerate(sums):
                total = refs[number][member].astype(jnp.float32)
                for term in refs[number + 1 : number + len(terms)]:
                    total = total + term[member].astype(jnp.float32)
                refs[len(flat) + r][:, column * width : (column + 1) * width] = total.astype(jnp.bfloat16)
                number += len(terms)

    outs = [jax.ShapeDtypeStruct((tokens, len(sums) * width), jnp.bfloat16)] * group
    return call(body, outs)(*flat)


def unpack(group, pieces, widths):
    tokens = pieces[0].shape[0]

    def body(*refs):
        for r in range(group):
            lower = 0
            for number, width in enumerate(widths):
                refs[group + number][:, lanes(spot(group)[0] ^ r, width)] = refs[r][:, lower : lower + width]
                lower += width

    outs = [jax.ShapeDtypeStruct((tokens, group * width), jnp.bfloat16) for width in widths]
    return call(body, outs)(*pieces)


def local(layer_cotangent, out_weight, queries, keys, values):
    tokens = queries.shape[0]
    kv_heads = keys.shape[1] // HEAD_SIZE
    per_head = queries.shape[1] // keys.shape[1]
    count, tp_count = lax.axis_size("ctx"), lax.axis_size("tp")
    group = 1
    while (
        kv_heads % (2 * group) == 0
        and count % (2 * group) == 0
        and WINDOW_LENGTH % (2 * group * tokens) == 0
    ):
        group *= 2
    heads = kv_heads // group
    kv_width = heads * HEAD_SIZE
    back_groups = WINDOW_LENGTH // (group * tokens)
    def trade(sent):
        return [sent[0]] + [swapped(sent[r], "ctx", r) for r in range(1, group)]

    def returned(earlier):
        return [
            shifted(earlier[number], "ctx", -group * (back_groups - number)) for number in range(back_groups)
        ]

    sent = pack_kv(group, keys, values, begin())
    kv_pieces = trade(sent)
    z = Shape(group, back_groups, heads, per_head, tokens)
    query_sent = pack_queries(group, queries, sent[0])
    if tp_count == 2:
        other = head_product(2, 1, out_weight, layer_cotangent, [query_sent[0]])
        mine = head_product(2, 0, out_weight, layer_cotangent, [other])
        terms = [mine, swapped(other, "tp", 1)]
    else:
        mine = head_product(1, 0, out_weight, layer_cotangent, [query_sent[0]])
        terms = [lax.psum_scatter(mine, "tp", scatter_dimension=0, tiled=True)]
    kv_own = order_pieces(group, kv_pieces, mine)
    kv_earlier = [shifted(kv_own, "ctx", group * step) for step in range(back_groups, 0, -1)]
    qt = turn_queries(z, trade(query_sent))
    grads = trade(pack_grads(group, terms))
    e, inverse = softmax(z, kv_own, kv_earlier, qt)
    g, dv_own, dv_earlier = value_terms(z, e, inverse, grads)
    dv_terms = [dv_own] + returned(dv_earlier)
    ds, dk_own, dk_earlier = key_terms(z, e, inverse, qt, g, kv_own, kv_earlier)
    dk_terms = [dk_own] + returned(dk_earlier)
    dv, dq = query_terms(z, ds, inverse, kv_own, kv_earlier, dv_terms)
    dq = trade(dq)
    dkv = trade(pack_terms(group, [dk_terms, [dv]]))
    (query_grads,) = unpack(group, dq, [dq[0].shape[1]])
    key_gradients, value_gradients = unpack(group, dkv, [kv_width, kv_width])
    return (query_grads, key_gradients, value_gradients)


def solution(mesh):
    in_specs = (P("ctx", "tp"), P(None, "tp"), P("ctx", "tp"), P("ctx", "tp"), P("ctx", "tp"))
    out_specs = (P("ctx", "tp"), P("ctx", "tp"), P("ctx", "tp"))
    return jax.shard_map(local, mesh=mesh, in_specs=in_specs, out_specs=out_specs, check_vma=False)
```

```python
import functools

import jax
import jax.numpy as jnp
from jax import lax
from jax.experimental import pallas as pl
from jax.experimental.pallas import tpu as pltpu
from jax.sharding import PartitionSpec as P

HEAD_SIZE = 128
WINDOW_LENGTH = 1024
LOG2_E = 1.4426950408889634
AHEAD = 10**10

score_scale = 168.0 ** (-0.5)

VMEM = pl.BlockSpec(memory_space=pltpu.VMEM)
ANY = pl.BlockSpec(memory_space=pl.ANY)
SMEM = pl.BlockSpec(memory_space=pltpu.SMEM)
NT = (((1,), (1,)), ((), ()))
NN = (((1,), (0,)), ((), ()))


def shifted(value, axis, steps):
    count = lax.axis_size(axis)
    leading, last = (max(0, -steps), min(count, count - steps))
    return lax.ppermute(value, axis, [(source, source + steps) for source in range(leading, last)])


def swapped(value, axis, bits):
    count = lax.axis_size(axis)
    return lax.ppermute(value, axis, [(source, source ^ bits) for source in range(count)])


def call(body, outs, scratch=(), flops=0, exps=0, specs=None, vmem=32):
    def run(*args):
        moved = sum(a.size * a.dtype.itemsize for a in args)
        moved += sum(o.size * o.dtype.itemsize for o in outs)
        return pl.pallas_call(
            body,
            out_shape=tuple(outs),
            in_specs=specs or [SMEM if a.dtype == jnp.int32 else VMEM for a in args],
            out_specs=tuple(VMEM for _ in outs),
            scratch_shapes=list(scratch),
            compiler_params=pltpu.CompilerParams(vmem_limit_bytes=vmem * 1024 * 1024),
            cost_estimate=pl.CostEstimate(flops=flops, bytes_accessed=moved, transcendentals=exps),
        )(*args)

    return run


def spot(group):
    index = lax.axis_index("ctx")
    place = lax.rem(index, group)
    return place, index - place


def hop(group, r):
    return group - r if r else 0


def lanes(index, width):
    return pl.ds(pl.multiple_of(index * width, width), width)


def begin():
    def body(out_ref):
        out_ref[...] = jnp.zeros_like(out_ref)

    return call(body, [jax.ShapeDtypeStruct((8, 128), jnp.float32)], flops=AHEAD)()[0]


def pack_kv(group, keys, values, before):
    tokens, width = keys.shape[0], keys.shape[1] // group

    def body(k_ref, v_ref, before_ref, *refs):
        for r in range(group):
            member = spot(group)[0] ^ hop(group, r)
            refs[r][:, :width] = k_ref[:, lanes(member, width)]
            refs[r][:, width:] = v_ref[:, lanes(member, width)]

    outs = [jax.ShapeDtypeStruct((tokens, 2 * width), jnp.bfloat16)] * group
    return call(body, outs, flops=AHEAD, specs=[VMEM, VMEM, ANY])(keys, values, before)


def pack_queries(group, queries, before):
    tokens, width = queries.shape[0], queries.shape[1] // group

    def body(q_ref, before_ref, *out_refs):
        for r in range(group):
            out_refs[r][...] = q_ref[:, lanes(spot(group)[0] ^ hop(group, r), width)]

    outs = [jax.ShapeDtypeStruct((tokens, width), jnp.bfloat16)] * group
    return call(body, outs, specs=[VMEM, ANY])(queries, before)


def order_pieces(group, pieces, before):
    def body(*refs):
        for r in range(group):
            refs[-1][spot(group)[0] ^ hop(group, r)] = refs[r][...]

    outs = [jax.ShapeDtypeStruct((group,) + pieces[0].shape, jnp.bfloat16)]
    return call(body, outs, specs=[VMEM] * group + [ANY])(*pieces, before)[0]


def head_product(parts, part, out_weight, layer_cotangent, before):
    tokens, depth = layer_cotangent.shape
    rows = out_weight.shape[0] // parts
    tile = min(rows, 512)

    def body(w_ref, c_ref, *refs):
        first = (lax.axis_index("tp") ^ part) * rows if parts > 1 else 0

        @pl.loop(0, rows // tile)
        def _(i):
            here = pl.ds(pl.multiple_of(i * tile, tile), tile)
            there = pl.ds(pl.multiple_of(first + i * tile, tile), tile)
            refs[-1][here, :] = lax.dot_general(
                w_ref[there, :], c_ref[...], NT, preferred_element_type=jnp.float32
            ).astype(jnp.bfloat16)

    outs = [jax.ShapeDtypeStruct((rows, tokens), jnp.bfloat16)]
    specs = [VMEM, VMEM] + [ANY] * len(before)
    return call(body, outs, flops=2 * rows * tokens * depth, specs=specs, vmem=16)(
        out_weight, layer_cotangent, *before
    )[0]


def pack_grads(group, terms, before):
    rows, tokens = terms[0].shape
    rows //= group

    def body(*refs):
        for r in range(group):
            there = lanes(spot(group)[0] ^ hop(group, r), rows)
            total = refs[0][there, :]
            if len(terms) > 1:
                total = total.astype(jnp.float32)
                for term in refs[1 : len(terms)]:
                    total = total + term[there, :].astype(jnp.float32)
            refs[len(terms) + 1 + r][...] = total.astype(jnp.bfloat16)

    outs = [jax.ShapeDtypeStruct((rows, tokens), jnp.bfloat16)] * group
    return call(body, outs, specs=[VMEM] * len(terms) + [ANY])(*terms, before)


class Shape:
    def __init__(self, group, steps, heads, per_head, tokens):
        self.group, self.steps, self.heads, self.per_head, self.tokens = group, steps, heads, per_head, tokens
        self.back = steps * group
        self.span = self.back + 1
        self.total = self.back + group
        self.wide = per_head * tokens
        self.width = heads * per_head * HEAD_SIZE
        self.kv_width = heads * HEAD_SIZE
        self.entries = group * heads * self.wide * self.span * tokens

    def block(self, own_ref, earlier_refs, number):
        if number < self.back:
            return earlier_refs[number // self.group].at[number % self.group]
        return own_ref.at[number - self.back]


def turn_queries(z, pieces):
    def body(*refs):
        for head in range(z.heads):
            for r in range(z.group):
                for j in range(z.per_head):
                    lower = (head * z.per_head + j) * HEAD_SIZE
                    refs[z.group][head, spot(z.group)[0] ^ hop(z.group, r), :, j * z.tokens : (j + 1) * z.tokens] = refs[r][
                        :, lower : lower + HEAD_SIZE
                    ].T

    outs = [jax.ShapeDtypeStruct((z.heads, z.group, HEAD_SIZE, z.wide), jnp.bfloat16)]
    return call(body, outs)(*pieces)[0]


def softmax(z, kv_own, kv_earlier, qt):
    factor = score_scale * LOG2_E

    def body(*refs):
        own_ref, earlier_refs = refs[0], refs[1 : 1 + z.steps]
        qt_ref, e_ref, inverse_ref, k_all, s_all = refs[1 + z.steps :]
        first = spot(z.group)[1]
        key_id = lax.broadcasted_iota(jnp.int32, (z.tokens, z.wide), 0)
        query_id = lax.broadcasted_iota(jnp.int32, (z.tokens, z.wide), 1) & (z.tokens - 1)
        for head in range(z.heads):
            at_k = slice(head * HEAD_SIZE, (head + 1) * HEAD_SIZE)
            for number in range(z.total):
                k_all[number] = z.block(own_ref, earlier_refs, number)[:, at_k]

            @pl.loop(0, z.group)
            def _(b):
                qt = qt_ref[head, b]
                top = None
                for c in range(z.span):
                    s = lax.dot_general(k_all[b + c], qt, NN, preferred_element_type=jnp.float32)
                    if c == 0:
                        s = jnp.where(key_id > query_id, s, -jnp.inf)
                    if c == z.back:
                        s = jnp.where(key_id <= query_id, s, -jnp.inf)
                    s_all[c] = s
                    here = jnp.max(s, axis=0, keepdims=True)
                    if c < z.back:
                        here = jnp.where(first + b + c >= z.back, here, -jnp.inf)
                    top = here if top is None else jnp.maximum(top, here)
                norm = jnp.zeros((1, z.wide), jnp.float32)
                for c in range(z.span):
                    base = top
                    if c < z.back:
                        base = jnp.where(first + b + c >= z.back, top, jnp.inf)
                    e = jnp.exp2((s_all[c] - base) * factor)
                    norm = norm + jnp.sum(e, axis=0, keepdims=True)
                    e_ref[head, b, c] = e.astype(jnp.bfloat16)
                inverse_ref[head, b] = 1.0 / norm

    outs = [
        jax.ShapeDtypeStruct((z.heads, z.group, z.span, z.tokens, z.wide), jnp.bfloat16),
        jax.ShapeDtypeStruct((z.heads, z.group, 1, z.wide), jnp.float32),
    ]
    scratch = [
        pltpu.VMEM((z.total, z.tokens, HEAD_SIZE), jnp.bfloat16),
        pltpu.VMEM((z.span, z.tokens, z.wide), jnp.float32),
    ]
    return call(body, outs, scratch, flops=2 * z.entries * HEAD_SIZE, exps=z.entries)(
        kv_own, *kv_earlier, qt
    )


def value_terms(z, e, inverse, grads):
    def body(e_ref, inverse_ref, *refs):
        g_refs, (g_ref, own_ref), earlier_refs = (
            refs[: z.group],
            refs[z.group : z.group + 2],
            refs[z.group + 2 : z.group + 2 + z.steps],
        )
        dv_all = refs[-1]
        place = spot(z.group)[0]
        for head in range(z.heads):
            at = slice(head * HEAD_SIZE, (head + 1) * HEAD_SIZE)
            for r in range(z.group):
                for j in range(z.per_head):
                    lower = (head * z.per_head + j) * HEAD_SIZE
                    g_ref[head, place ^ hop(z.group, r), :, j * z.tokens : (j + 1) * z.tokens] = g_refs[r][
                        lower : lower + HEAD_SIZE, :
                    ]
            dv_all[...] = jnp.zeros_like(dv_all)

            @pl.loop(0, z.group)
            def _(b):
                g = (g_ref[head, b].astype(jnp.float32) * inverse_ref[head, b]).astype(jnp.bfloat16)
                for c in range(z.span):
                    dv_all[b + c] += lax.dot_general(
                        e_ref[head, b, c], g, NT, preferred_element_type=jnp.float32
                    )

            for number in range(z.total):
                part = dv_all[number]
                z.block(own_ref, earlier_refs, number)[:, at] = part.astype(own_ref.dtype if number >= z.back else jnp.bfloat16)

    outs = [
        jax.ShapeDtypeStruct((z.heads, z.group, HEAD_SIZE, z.wide), jnp.bfloat16),
        jax.ShapeDtypeStruct((z.group, z.tokens, z.kv_width), jnp.float32),
    ]
    outs += [jax.ShapeDtypeStruct((z.group, z.tokens, z.kv_width), jnp.bfloat16)] * z.steps
    scratch = [pltpu.VMEM((z.total, z.tokens, HEAD_SIZE), jnp.float32)]
    results = call(body, outs, scratch, flops=2 * z.entries * HEAD_SIZE)(e, inverse, *grads)
    return results[0], results[1], results[2:]


def key_terms(z, e, inverse, qt, g, kv_own, kv_earlier):
    def body(e_ref, inverse_ref, qt_ref, g_ref, own_ref, *refs):
        earlier_refs, ds_ref = refs[: z.steps], refs[z.steps]
        dk_own, dk_earlier = refs[z.steps + 1], refs[z.steps + 2 : 2 * z.steps + 2]
        v_all, dk_all, dp_all = refs[2 * z.steps + 2 :]
        for head in range(z.heads):
            at = slice(head * HEAD_SIZE, (head + 1) * HEAD_SIZE)
            at_v = slice(z.kv_width + head * HEAD_SIZE, z.kv_width + (head + 1) * HEAD_SIZE)
            for number in range(z.total):
                v_all[number] = z.block(own_ref, earlier_refs, number)[:, at_v]
            dk_all[...] = jnp.zeros_like(dk_all)

            @pl.loop(0, z.group)
            def _(b):
                g = g_ref[head, b]
                inverse = inverse_ref[head, b]
                delta = jnp.zeros((1, z.wide), jnp.float32)
                for c in range(z.span):
                    dp = lax.dot_general(v_all[b + c], g, NN, preferred_element_type=jnp.float32)
                    delta = delta + jnp.sum(e_ref[head, b, c].astype(jnp.float32) * dp, axis=0, keepdims=True)
                    dp_all[c] = dp
                delta = delta * inverse
                q = (qt_ref[head, b].astype(jnp.float32) * inverse).astype(jnp.bfloat16)
                for c in range(z.span):
                    ds = e_ref[head, b, c] * (dp_all[c] - delta).astype(jnp.bfloat16)
                    ds_ref[head, b, c] = ds
                    dk_all[b + c] += lax.dot_general(ds, q, NT, preferred_element_type=jnp.float32)

            for number in range(z.total):
                part = dk_all[number] * score_scale
                z.block(dk_own, dk_earlier, number)[:, at] = part.astype(
                    dk_own.dtype if number >= z.back else jnp.bfloat16
                )

    outs = [jax.ShapeDtypeStruct(e.shape, jnp.bfloat16)]
    outs += [jax.ShapeDtypeStruct((z.group, z.tokens, z.kv_width), jnp.float32)]
    outs += [jax.ShapeDtypeStruct((z.group, z.tokens, z.kv_width), jnp.bfloat16)] * z.steps
    scratch = [
        pltpu.VMEM((z.total, z.tokens, HEAD_SIZE), jnp.bfloat16),
        pltpu.VMEM((z.total, z.tokens, HEAD_SIZE), jnp.float32),
        pltpu.VMEM((z.span, z.tokens, z.wide), jnp.float32),
    ]
    results = call(body, outs, scratch, flops=4 * z.entries * HEAD_SIZE)(
        e, inverse, qt, g, kv_own, *kv_earlier
    )
    return results[0], results[1], results[2:]


def query_terms(z, ds, inverse, kv_own, kv_earlier, dv_terms):
    def body(ds_ref, inverse_ref, own_ref, *refs):
        earlier_refs, term_refs = refs[: z.steps], refs[z.steps : 2 * z.steps + 1]
        out_refs = refs[2 * z.steps + 1 : 2 * z.steps + 1 + z.group]
        kt_all, dq_all = refs[2 * z.steps + 1 + z.group :]
        for head in range(z.heads):
            at = slice(head * HEAD_SIZE, (head + 1) * HEAD_SIZE)
            for number in range(z.total):
                kt_all[number] = z.block(own_ref, earlier_refs, number)[:, at].T

            @pl.loop(0, z.group)
            def _(b):
                dqt = jnp.zeros((HEAD_SIZE, z.wide), jnp.float32)
                for c in range(z.span):
                    dqt = dqt + lax.dot_general(
                        kt_all[b + c], ds_ref[head, b, c], NN, preferred_element_type=jnp.float32
                    )
                dqt = dqt * (inverse_ref[head, b] * score_scale)
                for j in range(z.per_head):
                    lower = (head * z.per_head + j) * HEAD_SIZE
                    dq_all[b, :, lower : lower + HEAD_SIZE] = (
                        dqt[:, j * z.tokens : (j + 1) * z.tokens].T.astype(jnp.bfloat16)
                    )

        for r in range(z.group):
            member = spot(z.group)[0] ^ hop(z.group, r)
            dv = term_refs[0][member]
            for term in term_refs[1:]:
                dv = dv + term[member].astype(jnp.float32)
            out_refs[r][:, : z.width] = dq_all[member]
            out_refs[r][:, z.width :] = dv.astype(jnp.bfloat16)

    outs = [jax.ShapeDtypeStruct((z.tokens, z.width + z.kv_width), jnp.bfloat16)] * z.group
    scratch = [
        pltpu.VMEM((z.total, HEAD_SIZE, z.tokens), jnp.bfloat16),
        pltpu.VMEM((z.group, z.tokens, z.width), jnp.bfloat16),
    ]
    return call(body, outs, scratch, flops=2 * z.entries * HEAD_SIZE)(
        ds, inverse, kv_own, *kv_earlier, *dv_terms
    )


def pack_terms(group, sums):
    tokens, width = sums[0][0].shape[1:]
    flat = [term for terms in sums for term in terms]

    def body(*refs):
        for r in range(group):
            member = spot(group)[0] ^ hop(group, r)
            number = 0
            for column, terms in enumerate(sums):
                total = refs[number][member].astype(jnp.float32)
                for term in refs[number + 1 : number + len(terms)]:
                    total = total + term[member].astype(jnp.float32)
                refs[len(flat) + r][:, column * width : (column + 1) * width] = total.astype(jnp.bfloat16)
                number += len(terms)

    outs = [jax.ShapeDtypeStruct((tokens, len(sums) * width), jnp.bfloat16)] * group
    return call(body, outs)(*flat)


def unpack(group, pieces, widths, before):
    tokens = pieces[0].shape[0]

    def body(*refs):
        for r in range(group):
            lower = 0
            for number, width in enumerate(widths):
                there = lanes(spot(group)[0] ^ hop(group, r), width)
                refs[group + 1 + number][:, there] = refs[r][:, lower : lower + width]
                lower += width

    outs = [jax.ShapeDtypeStruct((tokens, group * width), jnp.bfloat16) for width in widths]
    return call(body, outs, specs=[VMEM] * group + [ANY])(*pieces, before)


def local(layer_cotangent, out_weight, queries, keys, values):
    tokens = queries.shape[0]
    kv_heads = keys.shape[1] // HEAD_SIZE
    per_head = queries.shape[1] // keys.shape[1]
    count, tp_count = lax.axis_size("ctx"), lax.axis_size("tp")
    group = 1
    while (
        kv_heads % (2 * group) == 0
        and count % (2 * group) == 0
        and WINDOW_LENGTH % (2 * group * tokens) == 0
    ):
        group *= 2
    heads = kv_heads // group
    kv_width = heads * HEAD_SIZE
    back_groups = WINDOW_LENGTH // (group * tokens)

    def trade(sent):
        return [sent[0]] + [swapped(sent[r], "ctx", hop(group, r)) for r in range(1, group)]

    def returned(earlier):
        return [
            shifted(earlier[number], "ctx", -group * (back_groups - number)) for number in range(back_groups)
        ]

    sent = pack_kv(group, keys, values, begin())
    kv_pieces = trade(sent)
    z = Shape(group, back_groups, heads, per_head, tokens)
    query_sent = pack_queries(group, queries, sent[0])
    qt = turn_queries(z, trade(query_sent))
    if tp_count == 2:
        other = head_product(2, 1, out_weight, layer_cotangent, [query_sent[0]])
        terms = [head_product(2, 0, out_weight, layer_cotangent, [other]), swapped(other, "tp", 1)]
    else:
        other = head_product(1, 0, out_weight, layer_cotangent, [query_sent[0]])
        terms = [lax.psum_scatter(other, "tp", scatter_dimension=0, tiled=True)]
    kv_own = order_pieces(group, kv_pieces, terms[0])
    kv_earlier = [shifted(kv_own, "ctx", group * step) for step in range(back_groups, 0, -1)]
    grads = trade(pack_grads(group, terms, kv_own))
    e, inverse = softmax(z, kv_own, kv_earlier, qt)
    g, dv_own, dv_earlier = value_terms(z, e, inverse, grads)
    dv_terms = [dv_own] + returned(dv_earlier)
    ds, dk_own, dk_earlier = key_terms(z, e, inverse, qt, g, kv_own, kv_earlier)
    dk_terms = [dk_own] + returned(dk_earlier)
    pieces = trade(query_terms(z, ds, inverse, kv_own, kv_earlier, dv_terms))
    query_grads, value_gradients = unpack(group, pieces, [z.width, kv_width], ds)
    pieces = trade(pack_terms(group, [dk_terms]))
    (key_gradients,) = unpack(group, pieces, [kv_width], value_gradients)
    return (query_grads, key_gradients, value_gradients)


def solution(mesh):
    in_specs = (P("ctx", "tp"), P(None, "tp"), P("ctx", "tp"), P("ctx", "tp"), P("ctx", "tp"))
    out_specs = (P("ctx", "tp"), P("ctx", "tp"), P("ctx", "tp"))
    return jax.shard_map(local, mesh=mesh, in_specs=in_specs, out_specs=out_specs, check_vma=False)
```

```python
import functools

import jax
import jax.numpy as jnp
from jax import lax
from jax.experimental import pallas as pl
from jax.experimental.pallas import tpu as pltpu
from jax.sharding import PartitionSpec as P

HEAD_SIZE = 128
WINDOW_LENGTH = 1024
LOG2_E = 1.4426950408889634
AHEAD = 10**10

score_scale = 168.0 ** (-0.5)

VMEM = pl.BlockSpec(memory_space=pltpu.VMEM)
ANY = pl.BlockSpec(memory_space=pl.ANY)
SMEM = pl.BlockSpec(memory_space=pltpu.SMEM)
NT = (((1,), (1,)), ((), ()))
NN = (((1,), (0,)), ((), ()))


def shifted(value, axis, steps):
    count = lax.axis_size(axis)
    leading, last = (max(0, -steps), min(count, count - steps))
    return lax.ppermute(value, axis, [(source, source + steps) for source in range(leading, last)])


def swapped(value, axis, bits):
    count = lax.axis_size(axis)
    return lax.ppermute(value, axis, [(source, source ^ bits) for source in range(count)])


def exchanged(value, axis, group):
    if group == 1:
        return value
    count = lax.axis_size(axis)
    groups = [list(range(first, first + group)) for first in range(0, count, group)]
    return lax.all_to_all(value, axis, 0, 0, axis_index_groups=groups, tiled=True)


def call(body, outs, scratch=(), flops=0, exps=0, specs=None, vmem=32):
    def run(*args):
        moved = sum(a.size * a.dtype.itemsize for a in args)
        moved += sum(o.size * o.dtype.itemsize for o in outs)
        return pl.pallas_call(
            body,
            out_shape=tuple(outs),
            in_specs=specs or [SMEM if a.dtype == jnp.int32 else VMEM for a in args],
            out_specs=tuple(VMEM for _ in outs),
            scratch_shapes=list(scratch),
            compiler_params=pltpu.CompilerParams(vmem_limit_bytes=vmem * 1024 * 1024),
            cost_estimate=pl.CostEstimate(flops=flops, bytes_accessed=moved, transcendentals=exps),
        )(*args)

    return run


def spot(group):
    index = lax.axis_index("ctx")
    place = lax.rem(index, group)
    return place, index - place


def hop(group, r):
    return group - r if r else 0


def lanes(index, width):
    return pl.ds(pl.multiple_of(index * width, width), width)


def begin():
    def body(out_ref):
        out_ref[...] = jnp.zeros_like(out_ref)

    return call(body, [jax.ShapeDtypeStruct((8, 128), jnp.float32)], flops=AHEAD)()[0]


def pack_kv(group, keys, values, before):
    tokens, width = keys.shape[0], keys.shape[1] // group

    def body(k_ref, v_ref, before_ref, *refs):
        for r in range(group):
            member = spot(group)[0] ^ hop(group, r)
            refs[r][:, :width] = k_ref[:, lanes(member, width)]
            refs[r][:, width:] = v_ref[:, lanes(member, width)]

    outs = [jax.ShapeDtypeStruct((tokens, 2 * width), jnp.bfloat16)] * group
    return call(body, outs, flops=AHEAD, specs=[VMEM, VMEM, ANY])(keys, values, before)


def split_queries(group, queries, before):
    tokens, width = queries.shape[0], queries.shape[1] // group

    def body(q_ref, before_ref, out_ref):
        for member in range(group):
            out_ref[member] = q_ref[:, member * width : (member + 1) * width]

    outs = [jax.ShapeDtypeStruct((group, tokens, width), jnp.bfloat16)]
    return call(body, outs, specs=[VMEM, ANY])(queries, before)[0]


def order_pieces(group, pieces, before):
    def body(*refs):
        for r in range(group):
            refs[-1][spot(group)[0] ^ hop(group, r)] = refs[r][...]

    outs = [jax.ShapeDtypeStruct((group,) + pieces[0].shape, jnp.bfloat16)]
    return call(body, outs, flops=AHEAD, specs=[VMEM] * group + [ANY])(*pieces, before)[0]


def head_product(parts, part, out_weight, layer_cotangent, before):
    tokens, depth = layer_cotangent.shape
    rows = out_weight.shape[0] // parts
    tile = min(rows, 512)

    def body(w_ref, c_ref, *refs):
        first = (lax.axis_index("tp") ^ part) * rows if parts > 1 else 0

        @pl.loop(0, rows // tile)
        def _(i):
            here = pl.ds(pl.multiple_of(i * tile, tile), tile)
            there = pl.ds(pl.multiple_of(first + i * tile, tile), tile)
            refs[-1][here, :] = lax.dot_general(
                w_ref[there, :], c_ref[...], NT, preferred_element_type=jnp.float32
            ).astype(jnp.bfloat16)

    outs = [jax.ShapeDtypeStruct((rows, tokens), jnp.bfloat16)]
    specs = [VMEM, VMEM] + [ANY] * len(before)
    return call(body, outs, flops=2 * rows * tokens * depth, specs=specs, vmem=16)(
        out_weight, layer_cotangent, *before
    )[0]


def pack_grads(group, terms, before):
    rows, tokens = terms[0].shape
    rows //= group

    def body(*refs):
        for r in range(group):
            there = lanes(spot(group)[0] ^ hop(group, r), rows)
            total = refs[0][there, :]
            if len(terms) > 1:
                total = total.astype(jnp.float32)
                for term in refs[1 : len(terms)]:
                    total = total + term[there, :].astype(jnp.float32)
            refs[len(terms) + 1 + r][...] = total.astype(jnp.bfloat16)

    outs = [jax.ShapeDtypeStruct((rows, tokens), jnp.bfloat16)] * group
    return call(body, outs, specs=[VMEM] * len(terms) + [ANY])(*terms, before)


class Shape:
    def __init__(self, group, steps, heads, per_head, tokens):
        self.group, self.steps, self.heads, self.per_head, self.tokens = group, steps, heads, per_head, tokens
        self.back = steps * group
        self.span = self.back + 1
        self.total = self.back + group
        self.wide = per_head * tokens
        self.width = heads * per_head * HEAD_SIZE
        self.kv_width = heads * HEAD_SIZE
        self.entries = group * heads * self.wide * self.span * tokens

    def block(self, own_ref, earlier_refs, number):
        if number < self.back:
            return earlier_refs[number // self.group].at[number % self.group]
        return own_ref.at[number - self.back]


def turn_queries(z, queries):
    def body(in_ref, out_ref):
        for head in range(z.heads):
            for member in range(z.group):
                for j in range(z.per_head):
                    lower = (head * z.per_head + j) * HEAD_SIZE
                    out_ref[head, member, :, j * z.tokens : (j + 1) * z.tokens] = in_ref[
                        member, :, lower : lower + HEAD_SIZE
                    ].T

    outs = [jax.ShapeDtypeStruct((z.heads, z.group, HEAD_SIZE, z.wide), jnp.bfloat16)]
    return call(body, outs)(queries)[0]


def softmax(z, kv_own, kv_earlier, qt):
    factor = score_scale * LOG2_E

    def body(*refs):
        own_ref, earlier_refs = refs[0], refs[1 : 1 + z.steps]
        qt_ref, e_ref, inverse_ref, k_all, s_all = refs[1 + z.steps :]
        first = spot(z.group)[1]
        key_id = lax.broadcasted_iota(jnp.int32, (z.tokens, z.wide), 0)
        query_id = lax.broadcasted_iota(jnp.int32, (z.tokens, z.wide), 1) & (z.tokens - 1)
        for head in range(z.heads):
            at_k = slice(head * HEAD_SIZE, (head + 1) * HEAD_SIZE)
            for number in range(z.total):
                k_all[number] = z.block(own_ref, earlier_refs, number)[:, at_k]

            @pl.loop(0, z.group)
            def _(b):
                qt = qt_ref[head, b]
                top = None
                for c in range(z.span):
                    s = lax.dot_general(k_all[b + c], qt, NN, preferred_element_type=jnp.float32)
                    if c == 0:
                        s = jnp.where(key_id > query_id, s, -jnp.inf)
                    if c == z.back:
                        s = jnp.where(key_id <= query_id, s, -jnp.inf)
                    s_all[c] = s
                    here = jnp.max(s, axis=0, keepdims=True)
                    if c < z.back:
                        here = jnp.where(first + b + c >= z.back, here, -jnp.inf)
                    top = here if top is None else jnp.maximum(top, here)
                norm = jnp.zeros((1, z.wide), jnp.float32)
                for c in range(z.span):
                    base = top
                    if c < z.back:
                        base = jnp.where(first + b + c >= z.back, top, jnp.inf)
                    e = jnp.exp2((s_all[c] - base) * factor)
                    norm = norm + jnp.sum(e, axis=0, keepdims=True)
                    e_ref[head, b, c] = e.astype(jnp.bfloat16)
                inverse_ref[head, b] = 1.0 / norm

    outs = [
        jax.ShapeDtypeStruct((z.heads, z.group, z.span, z.tokens, z.wide), jnp.bfloat16),
        jax.ShapeDtypeStruct((z.heads, z.group, 1, z.wide), jnp.float32),
    ]
    scratch = [
        pltpu.VMEM((z.total, z.tokens, HEAD_SIZE), jnp.bfloat16),
        pltpu.VMEM((z.span, z.tokens, z.wide), jnp.float32),
    ]
    return call(body, outs, scratch, flops=2 * z.entries * HEAD_SIZE, exps=z.entries)(
        kv_own, *kv_earlier, qt
    )


def value_terms(z, e, inverse, grads):
    def body(e_ref, inverse_ref, *refs):
        g_refs, (g_ref, own_ref), earlier_refs = (
            refs[: z.group],
            refs[z.group : z.group + 2],
            refs[z.group + 2 : z.group + 2 + z.steps],
        )
        dv_all = refs[-1]
        place = spot(z.group)[0]
        for head in range(z.heads):
            at = slice(head * HEAD_SIZE, (head + 1) * HEAD_SIZE)
            for r in range(z.group):
                for j in range(z.per_head):
                    lower = (head * z.per_head + j) * HEAD_SIZE
                    g_ref[head, place ^ hop(z.group, r), :, j * z.tokens : (j + 1) * z.tokens] = g_refs[r][
                        lower : lower + HEAD_SIZE, :
                    ]
            dv_all[...] = jnp.zeros_like(dv_all)

            @pl.loop(0, z.group)
            def _(b):
                g = (g_ref[head, b].astype(jnp.float32) * inverse_ref[head, b]).astype(jnp.bfloat16)
                for c in range(z.span):
                    dv_all[b + c] += lax.dot_general(
                        e_ref[head, b, c], g, NT, preferred_element_type=jnp.float32
                    )

            for number in range(z.total):
                part = dv_all[number]
                z.block(own_ref, earlier_refs, number)[:, at] = part.astype(own_ref.dtype if number >= z.back else jnp.bfloat16)

    outs = [
        jax.ShapeDtypeStruct((z.heads, z.group, HEAD_SIZE, z.wide), jnp.bfloat16),
        jax.ShapeDtypeStruct((z.group, z.tokens, z.kv_width), jnp.float32),
    ]
    outs += [jax.ShapeDtypeStruct((z.group, z.tokens, z.kv_width), jnp.bfloat16)] * z.steps
    scratch = [pltpu.VMEM((z.total, z.tokens, HEAD_SIZE), jnp.float32)]
    results = call(body, outs, scratch, flops=2 * z.entries * HEAD_SIZE)(e, inverse, *grads)
    return results[0], results[1], results[2:]


def key_terms(z, e, inverse, qt, g, kv_own, kv_earlier):
    def body(e_ref, inverse_ref, qt_ref, g_ref, own_ref, *refs):
        earlier_refs, ds_ref = refs[: z.steps], refs[z.steps]
        dk_own, dk_earlier = refs[z.steps + 1], refs[z.steps + 2 : 2 * z.steps + 2]
        v_all, dk_all, dp_all = refs[2 * z.steps + 2 :]
        for head in range(z.heads):
            at = slice(head * HEAD_SIZE, (head + 1) * HEAD_SIZE)
            at_v = slice(z.kv_width + head * HEAD_SIZE, z.kv_width + (head + 1) * HEAD_SIZE)
            for number in range(z.total):
                v_all[number] = z.block(own_ref, earlier_refs, number)[:, at_v]
            dk_all[...] = jnp.zeros_like(dk_all)

            @pl.loop(0, z.group)
            def _(b):
                g = g_ref[head, b]
                inverse = inverse_ref[head, b]
                delta = jnp.zeros((1, z.wide), jnp.float32)
                for c in range(z.span):
                    dp = lax.dot_general(v_all[b + c], g, NN, preferred_element_type=jnp.float32)
                    delta = delta + jnp.sum(e_ref[head, b, c].astype(jnp.float32) * dp, axis=0, keepdims=True)
                    dp_all[c] = dp
                delta = delta * inverse
                q = (qt_ref[head, b].astype(jnp.float32) * inverse).astype(jnp.bfloat16)
                for c in range(z.span):
                    ds = e_ref[head, b, c] * (dp_all[c] - delta).astype(jnp.bfloat16)
                    ds_ref[head, b, c] = ds
                    dk_all[b + c] += lax.dot_general(ds, q, NT, preferred_element_type=jnp.float32)

            for number in range(z.total):
                part = dk_all[number] * score_scale
                z.block(dk_own, dk_earlier, number)[:, at] = part.astype(
                    dk_own.dtype if number >= z.back else jnp.bfloat16
                )

    outs = [jax.ShapeDtypeStruct(e.shape, jnp.bfloat16)]
    outs += [jax.ShapeDtypeStruct((z.group, z.tokens, z.kv_width), jnp.float32)]
    outs += [jax.ShapeDtypeStruct((z.group, z.tokens, z.kv_width), jnp.bfloat16)] * z.steps
    scratch = [
        pltpu.VMEM((z.total, z.tokens, HEAD_SIZE), jnp.bfloat16),
        pltpu.VMEM((z.total, z.tokens, HEAD_SIZE), jnp.float32),
        pltpu.VMEM((z.span, z.tokens, z.wide), jnp.float32),
    ]
    results = call(body, outs, scratch, flops=4 * z.entries * HEAD_SIZE)(
        e, inverse, qt, g, kv_own, *kv_earlier
    )
    return results[0], results[1], results[2:]


def query_terms(z, ds, inverse, kv_own, kv_earlier, dv_terms):
    def body(ds_ref, inverse_ref, own_ref, *refs):
        earlier_refs, term_refs = refs[: z.steps], refs[z.steps : 2 * z.steps + 1]
        out_refs = refs[2 * z.steps + 1 : 2 * z.steps + 1 + z.group]
        kt_all, dq_all = refs[2 * z.steps + 1 + z.group :]
        for head in range(z.heads):
            at = slice(head * HEAD_SIZE, (head + 1) * HEAD_SIZE)
            for number in range(z.total):
                kt_all[number] = z.block(own_ref, earlier_refs, number)[:, at].T

            @pl.loop(0, z.group)
            def _(b):
                dqt = jnp.zeros((HEAD_SIZE, z.wide), jnp.float32)
                for c in range(z.span):
                    dqt = dqt + lax.dot_general(
                        kt_all[b + c], ds_ref[head, b, c], NN, preferred_element_type=jnp.float32
                    )
                dqt = dqt * (inverse_ref[head, b] * score_scale)
                for j in range(z.per_head):
                    lower = (head * z.per_head + j) * HEAD_SIZE
                    dq_all[b, :, lower : lower + HEAD_SIZE] = (
                        dqt[:, j * z.tokens : (j + 1) * z.tokens].T.astype(jnp.bfloat16)
                    )

        for r in range(z.group):
            member = spot(z.group)[0] ^ hop(z.group, r)
            dv = term_refs[0][member]
            for term in term_refs[1:]:
                dv = dv + term[member].astype(jnp.float32)
            out_refs[r][:, : z.width] = dq_all[member]
            out_refs[r][:, z.width :] = dv.astype(jnp.bfloat16)

    outs = [jax.ShapeDtypeStruct((z.tokens, z.width + z.kv_width), jnp.bfloat16)] * z.group
    scratch = [
        pltpu.VMEM((z.total, HEAD_SIZE, z.tokens), jnp.bfloat16),
        pltpu.VMEM((z.group, z.tokens, z.width), jnp.bfloat16),
    ]
    return call(body, outs, scratch, flops=2 * z.entries * HEAD_SIZE)(
        ds, inverse, kv_own, *kv_earlier, *dv_terms
    )


def pack_terms(group, sums):
    tokens, width = sums[0][0].shape[1:]
    flat = [term for terms in sums for term in terms]

    def body(*refs):
        for r in range(group):
            member = spot(group)[0] ^ hop(group, r)
            number = 0
            for column, terms in enumerate(sums):
                total = refs[number][member].astype(jnp.float32)
                for term in refs[number + 1 : number + len(terms)]:
                    total = total + term[member].astype(jnp.float32)
                refs[len(flat) + r][:, column * width : (column + 1) * width] = total.astype(jnp.bfloat16)
                number += len(terms)

    outs = [jax.ShapeDtypeStruct((tokens, len(sums) * width), jnp.bfloat16)] * group
    return call(body, outs)(*flat)


def unpack(group, pieces, widths):
    tokens = pieces[0].shape[0]

    def body(*refs):
        for r in range(group):
            lower = 0
            for number, width in enumerate(widths):
                there = lanes(spot(group)[0] ^ hop(group, r), width)
                refs[group + number][:, there] = refs[r][:, lower : lower + width]
                lower += width

    outs = [jax.ShapeDtypeStruct((tokens, group * width), jnp.bfloat16) for width in widths]
    return call(body, outs)(*pieces)


def local(layer_cotangent, out_weight, queries, keys, values):
    tokens = queries.shape[0]
    kv_heads = keys.shape[1] // HEAD_SIZE
    per_head = queries.shape[1] // keys.shape[1]
    count, tp_count = lax.axis_size("ctx"), lax.axis_size("tp")
    group = 1
    while (
        kv_heads % (2 * group) == 0
        and count % (2 * group) == 0
        and WINDOW_LENGTH % (2 * group * tokens) == 0
    ):
        group *= 2
    heads = kv_heads // group
    kv_width = heads * HEAD_SIZE
    back_groups = WINDOW_LENGTH // (group * tokens)

    def trade(sent):
        return [sent[0]] + [swapped(sent[r], "ctx", hop(group, r)) for r in range(1, group)]

    def returned(earlier):
        return [
            shifted(earlier[number], "ctx", -group * (back_groups - number)) for number in range(back_groups)
        ]

    sent = pack_kv(group, keys, values, begin())
    kv_pieces = trade(sent)
    z = Shape(group, back_groups, heads, per_head, tokens)
    query_sent = split_queries(group, queries, sent[0])
    qt = turn_queries(z, exchanged(query_sent, "ctx", group))
    if tp_count == 2:
        other = head_product(2, 1, out_weight, layer_cotangent, [query_sent])
        terms = [head_product(2, 0, out_weight, layer_cotangent, [other]), swapped(other, "tp", 1)]
    else:
        other = head_product(1, 0, out_weight, layer_cotangent, [query_sent])
        terms = [lax.psum_scatter(other, "tp", scatter_dimension=0, tiled=True)]
    kv_own = order_pieces(group, kv_pieces, terms[0])
    kv_earlier = [shifted(kv_own, "ctx", group * step) for step in range(back_groups, 0, -1)]
    grads = trade(pack_grads(group, terms, kv_own))
    e, inverse = softmax(z, kv_own, kv_earlier, qt)
    g, dv_own, dv_earlier = value_terms(z, e, inverse, grads)
    dv_terms = [dv_own] + returned(dv_earlier)
    ds, dk_own, dk_earlier = key_terms(z, e, inverse, qt, g, kv_own, kv_earlier)
    dk_terms = [dk_own] + returned(dk_earlier)
    pieces = trade(query_terms(z, ds, inverse, kv_own, kv_earlier, dv_terms))
    query_grads, value_gradients = unpack(group, pieces, [z.width, kv_width])
    pieces = trade(pack_terms(group, [dk_terms]))
    (key_gradients,) = unpack(group, pieces, [kv_width])
    return (query_grads, key_gradients, value_gradients)


def solution(mesh):
    in_specs = (P("ctx", "tp"), P(None, "tp"), P("ctx", "tp"), P("ctx", "tp"), P("ctx", "tp"))
    out_specs = (P("ctx", "tp"), P("ctx", "tp"), P("ctx", "tp"))
    return jax.shard_map(local, mesh=mesh, in_specs=in_specs, out_specs=out_specs, check_vma=False)
```

```python
import functools

import jax
import jax.numpy as jnp
from jax import lax
from jax.experimental import pallas as pl
from jax.experimental.pallas import tpu as pltpu
from jax.sharding import PartitionSpec as P

HEAD_SIZE = 128
WINDOW_LENGTH = 1024
LOG2_E = 1.4426950408889634
AHEAD = 10**10

score_scale = 168.0 ** (-0.5)

VMEM = pl.BlockSpec(memory_space=pltpu.VMEM)
ANY = pl.BlockSpec(memory_space=pl.ANY)
SMEM = pl.BlockSpec(memory_space=pltpu.SMEM)
NT = (((1,), (1,)), ((), ()))
NN = (((1,), (0,)), ((), ()))


def shifted(value, axis, steps):
    count = lax.axis_size(axis)
    leading, last = (max(0, -steps), min(count, count - steps))
    return lax.ppermute(value, axis, [(source, source + steps) for source in range(leading, last)])


def swapped(value, axis, bits):
    count = lax.axis_size(axis)
    return lax.ppermute(value, axis, [(source, source ^ bits) for source in range(count)])


def call(body, outs, scratch=(), flops=0, exps=0, specs=None, vmem=32):
    def run(*args):
        moved = sum(a.size * a.dtype.itemsize for a in args)
        moved += sum(o.size * o.dtype.itemsize for o in outs)
        return pl.pallas_call(
            body,
            out_shape=tuple(outs),
            in_specs=specs or [SMEM if a.dtype == jnp.int32 else VMEM for a in args],
            out_specs=tuple(VMEM for _ in outs),
            scratch_shapes=list(scratch),
            compiler_params=pltpu.CompilerParams(vmem_limit_bytes=vmem * 1024 * 1024),
            cost_estimate=pl.CostEstimate(flops=flops, bytes_accessed=moved, transcendentals=exps),
        )(*args)

    return run


def spot(group):
    index = lax.axis_index("ctx")
    place = lax.rem(index, group)
    return place, index - place


def hop(group, r, near=False):
    return r if near or r == 0 else group - r


def lanes(index, width):
    return pl.ds(pl.multiple_of(index * width, width), width)


def begin():
    def body(out_ref):
        out_ref[...] = jnp.zeros_like(out_ref)

    return call(body, [jax.ShapeDtypeStruct((8, 128), jnp.float32)], flops=AHEAD)()[0]


def pack_kv(group, keys, values, before):
    tokens, width = keys.shape[0], keys.shape[1] // group

    def body(k_ref, v_ref, before_ref, *refs):
        for r in range(group):
            member = spot(group)[0] ^ hop(group, r)
            refs[r][:, :width] = k_ref[:, lanes(member, width)]
            refs[r][:, width:] = v_ref[:, lanes(member, width)]

    outs = [jax.ShapeDtypeStruct((tokens, 2 * width), jnp.bfloat16)] * group
    return call(body, outs, flops=AHEAD, specs=[VMEM, VMEM, ANY])(keys, values, before)


def pack_queries(group, queries, before):
    tokens, width = queries.shape[0], queries.shape[1] // group

    def body(q_ref, before_ref, *out_refs):
        for r in range(group):
            out_refs[r][...] = q_ref[:, lanes(spot(group)[0] ^ hop(group, r), width)]

    outs = [jax.ShapeDtypeStruct((tokens, width), jnp.bfloat16)] * group
    return call(body, outs, specs=[VMEM, ANY])(queries, before)


def order_pieces(group, pieces, before):
    def body(*refs):
        for r in range(group):
            refs[-1][spot(group)[0] ^ hop(group, r)] = refs[r][...]

    outs = [jax.ShapeDtypeStruct((group,) + pieces[0].shape, jnp.bfloat16)]
    return call(body, outs, specs=[VMEM] * group + [ANY])(*pieces, before)[0]


def head_product(parts, part, out_weight, layer_cotangent, before):
    tokens, depth = layer_cotangent.shape
    rows = out_weight.shape[0] // parts
    tile = min(rows, 512)

    def body(w_ref, c_ref, *refs):
        first = (lax.axis_index("tp") ^ part) * rows if parts > 1 else 0

        @pl.loop(0, rows // tile)
        def _(i):
            here = pl.ds(pl.multiple_of(i * tile, tile), tile)
            there = pl.ds(pl.multiple_of(first + i * tile, tile), tile)
            refs[-1][here, :] = lax.dot_general(
                w_ref[there, :], c_ref[...], NT, preferred_element_type=jnp.float32
            ).astype(jnp.bfloat16)

    outs = [jax.ShapeDtypeStruct((rows, tokens), jnp.bfloat16)]
    specs = [VMEM, VMEM] + [ANY] * len(before)
    return call(body, outs, flops=2 * rows * tokens * depth, specs=specs, vmem=16)(
        out_weight, layer_cotangent, *before
    )[0]


def pack_grads(group, terms, before):
    rows, tokens = terms[0].shape
    rows //= group

    def body(*refs):
        for r in range(group):
            there = lanes(spot(group)[0] ^ hop(group, r), rows)
            total = refs[0][there, :]
            if len(terms) > 1:
                total = total.astype(jnp.float32)
                for term in refs[1 : len(terms)]:
                    total = total + term[there, :].astype(jnp.float32)
            refs[len(terms) + 1 + r][...] = total.astype(jnp.bfloat16)

    outs = [jax.ShapeDtypeStruct((rows, tokens), jnp.bfloat16)] * group
    return call(body, outs, specs=[VMEM] * len(terms) + [ANY])(*terms, before)


class Shape:
    def __init__(self, group, steps, heads, per_head, tokens):
        self.group, self.steps, self.heads, self.per_head, self.tokens = group, steps, heads, per_head, tokens
        self.back = steps * group
        self.span = self.back + 1
        self.total = self.back + group
        self.wide = per_head * tokens
        self.width = heads * per_head * HEAD_SIZE
        self.kv_width = heads * HEAD_SIZE
        self.entries = group * heads * self.wide * self.span * tokens

    def block(self, own_ref, earlier_refs, number):
        if number < self.back:
            return earlier_refs[number // self.group].at[number % self.group]
        return own_ref.at[number - self.back]


def turn_queries(z, pieces):
    def body(*refs):
        for head in range(z.heads):
            for r in range(z.group):
                for j in range(z.per_head):
                    lower = (head * z.per_head + j) * HEAD_SIZE
                    refs[z.group][head, spot(z.group)[0] ^ hop(z.group, r), :, j * z.tokens : (j + 1) * z.tokens] = refs[r][
                        :, lower : lower + HEAD_SIZE
                    ].T

    outs = [jax.ShapeDtypeStruct((z.heads, z.group, HEAD_SIZE, z.wide), jnp.bfloat16)]
    return call(body, outs)(*pieces)[0]


def softmax(z, kv_own, kv_earlier, qt):
    factor = score_scale * LOG2_E

    def body(*refs):
        own_ref, earlier_refs = refs[0], refs[1 : 1 + z.steps]
        qt_ref, e_ref, inverse_ref, k_all, s_all = refs[1 + z.steps :]
        first = spot(z.group)[1]
        key_id = lax.broadcasted_iota(jnp.int32, (z.tokens, z.wide), 0)
        query_id = lax.broadcasted_iota(jnp.int32, (z.tokens, z.wide), 1) & (z.tokens - 1)
        for head in range(z.heads):
            at_k = slice(head * HEAD_SIZE, (head + 1) * HEAD_SIZE)
            for number in range(z.total):
                k_all[number] = z.block(own_ref, earlier_refs, number)[:, at_k]

            @pl.loop(0, z.group)
            def _(b):
                qt = qt_ref[head, b]
                top = None
                for c in range(z.span):
                    s = lax.dot_general(k_all[b + c], qt, NN, preferred_element_type=jnp.float32)
                    if c == 0:
                        s = jnp.where(key_id > query_id, s, -jnp.inf)
                    if c == z.back:
                        s = jnp.where(key_id <= query_id, s, -jnp.inf)
                    s_all[c] = s
                    here = jnp.max(s, axis=0, keepdims=True)
                    if c < z.back:
                        here = jnp.where(first + b + c >= z.back, here, -jnp.inf)
                    top = here if top is None else jnp.maximum(top, here)
                norm = jnp.zeros((1, z.wide), jnp.float32)
                for c in range(z.span):
                    base = top
                    if c < z.back:
                        base = jnp.where(first + b + c >= z.back, top, jnp.inf)
                    e = jnp.exp2((s_all[c] - base) * factor)
                    norm = norm + jnp.sum(e, axis=0, keepdims=True)
                    e_ref[head, b, c] = e.astype(jnp.bfloat16)
                inverse_ref[head, b] = 1.0 / norm

    outs = [
        jax.ShapeDtypeStruct((z.heads, z.group, z.span, z.tokens, z.wide), jnp.bfloat16),
        jax.ShapeDtypeStruct((z.heads, z.group, 1, z.wide), jnp.float32),
    ]
    scratch = [
        pltpu.VMEM((z.total, z.tokens, HEAD_SIZE), jnp.bfloat16),
        pltpu.VMEM((z.span, z.tokens, z.wide), jnp.float32),
    ]
    return call(body, outs, scratch, flops=2 * z.entries * HEAD_SIZE, exps=z.entries)(
        kv_own, *kv_earlier, qt
    )


def value_terms(z, e, inverse, grads):
    def body(e_ref, inverse_ref, *refs):
        g_refs, (g_ref, own_ref), earlier_refs = (
            refs[: z.group],
            refs[z.group : z.group + 2],
            refs[z.group + 2 : z.group + 2 + z.steps],
        )
        dv_all = refs[-1]
        place = spot(z.group)[0]
        for head in range(z.heads):
            at = slice(head * HEAD_SIZE, (head + 1) * HEAD_SIZE)
            for r in range(z.group):
                for j in range(z.per_head):
                    lower = (head * z.per_head + j) * HEAD_SIZE
                    g_ref[head, place ^ hop(z.group, r), :, j * z.tokens : (j + 1) * z.tokens] = g_refs[r][
                        lower : lower + HEAD_SIZE, :
                    ]
            dv_all[...] = jnp.zeros_like(dv_all)

            @pl.loop(0, z.group)
            def _(b):
                g = (g_ref[head, b].astype(jnp.float32) * inverse_ref[head, b]).astype(jnp.bfloat16)
                for c in range(z.span):
                    dv_all[b + c] += lax.dot_general(
                        e_ref[head, b, c], g, NT, preferred_element_type=jnp.float32
                    )

            for number in range(z.total):
                part = dv_all[number]
                z.block(own_ref, earlier_refs, number)[:, at] = part.astype(own_ref.dtype if number >= z.back else jnp.bfloat16)

    outs = [
        jax.ShapeDtypeStruct((z.heads, z.group, HEAD_SIZE, z.wide), jnp.bfloat16),
        jax.ShapeDtypeStruct((z.group, z.tokens, z.kv_width), jnp.float32),
    ]
    outs += [jax.ShapeDtypeStruct((z.group, z.tokens, z.kv_width), jnp.bfloat16)] * z.steps
    scratch = [pltpu.VMEM((z.total, z.tokens, HEAD_SIZE), jnp.float32)]
    results = call(body, outs, scratch, flops=2 * z.entries * HEAD_SIZE)(e, inverse, *grads)
    return results[0], results[1], results[2:]


def key_terms(z, e, inverse, qt, g, kv_own, kv_earlier):
    def body(e_ref, inverse_ref, qt_ref, g_ref, own_ref, *refs):
        earlier_refs, ds_ref = refs[: z.steps], refs[z.steps]
        dk_own, dk_earlier = refs[z.steps + 1], refs[z.steps + 2 : 2 * z.steps + 2]
        v_all, dk_all, dp_all = refs[2 * z.steps + 2 :]
        for head in range(z.heads):
            at = slice(head * HEAD_SIZE, (head + 1) * HEAD_SIZE)
            at_v = slice(z.kv_width + head * HEAD_SIZE, z.kv_width + (head + 1) * HEAD_SIZE)
            for number in range(z.total):
                v_all[number] = z.block(own_ref, earlier_refs, number)[:, at_v]
            dk_all[...] = jnp.zeros_like(dk_all)

            @pl.loop(0, z.group)
            def _(b):
                g = g_ref[head, b]
                inverse = inverse_ref[head, b]
                delta = jnp.zeros((1, z.wide), jnp.float32)
                for c in range(z.span):
                    dp = lax.dot_general(v_all[b + c], g, NN, preferred_element_type=jnp.float32)
                    delta = delta + jnp.sum(e_ref[head, b, c].astype(jnp.float32) * dp, axis=0, keepdims=True)
                    dp_all[c] = dp
                delta = delta * inverse
                q = (qt_ref[head, b].astype(jnp.float32) * inverse).astype(jnp.bfloat16)
                for c in range(z.span):
                    ds = e_ref[head, b, c] * (dp_all[c] - delta).astype(jnp.bfloat16)
                    ds_ref[head, b, c] = ds
                    dk_all[b + c] += lax.dot_general(ds, q, NT, preferred_element_type=jnp.float32)

            for number in range(z.total):
                part = dk_all[number] * score_scale
                z.block(dk_own, dk_earlier, number)[:, at] = part.astype(
                    dk_own.dtype if number >= z.back else jnp.bfloat16
                )

    outs = [jax.ShapeDtypeStruct(e.shape, jnp.bfloat16)]
    outs += [jax.ShapeDtypeStruct((z.group, z.tokens, z.kv_width), jnp.float32)]
    outs += [jax.ShapeDtypeStruct((z.group, z.tokens, z.kv_width), jnp.bfloat16)] * z.steps
    scratch = [
        pltpu.VMEM((z.total, z.tokens, HEAD_SIZE), jnp.bfloat16),
        pltpu.VMEM((z.total, z.tokens, HEAD_SIZE), jnp.float32),
        pltpu.VMEM((z.span, z.tokens, z.wide), jnp.float32),
    ]
    results = call(body, outs, scratch, flops=4 * z.entries * HEAD_SIZE)(
        e, inverse, qt, g, kv_own, *kv_earlier
    )
    return results[0], results[1], results[2:]


def query_terms(z, ds, inverse, kv_own, kv_earlier, dv_terms):
    def body(ds_ref, inverse_ref, own_ref, *refs):
        earlier_refs, term_refs = refs[: z.steps], refs[z.steps : 2 * z.steps + 1]
        out_refs = refs[2 * z.steps + 1 : 2 * z.steps + 1 + z.group]
        kt_all, dq_all = refs[2 * z.steps + 1 + z.group :]
        for head in range(z.heads):
            at = slice(head * HEAD_SIZE, (head + 1) * HEAD_SIZE)
            for number in range(z.total):
                kt_all[number] = z.block(own_ref, earlier_refs, number)[:, at].T

            @pl.loop(0, z.group)
            def _(b):
                dqt = jnp.zeros((HEAD_SIZE, z.wide), jnp.float32)
                for c in range(z.span):
                    dqt = dqt + lax.dot_general(
                        kt_all[b + c], ds_ref[head, b, c], NN, preferred_element_type=jnp.float32
                    )
                dqt = dqt * (inverse_ref[head, b] * score_scale)
                for j in range(z.per_head):
                    lower = (head * z.per_head + j) * HEAD_SIZE
                    dq_all[b, :, lower : lower + HEAD_SIZE] = (
                        dqt[:, j * z.tokens : (j + 1) * z.tokens].T.astype(jnp.bfloat16)
                    )

        for r in range(z.group):
            member = spot(z.group)[0] ^ hop(z.group, r, near=True)
            dv = term_refs[0][member]
            for term in term_refs[1:]:
                dv = dv + term[member].astype(jnp.float32)
            out_refs[r][:, : z.width] = dq_all[member]
            out_refs[r][:, z.width :] = dv.astype(jnp.bfloat16)

    outs = [jax.ShapeDtypeStruct((z.tokens, z.width + z.kv_width), jnp.bfloat16)] * z.group
    scratch = [
        pltpu.VMEM((z.total, HEAD_SIZE, z.tokens), jnp.bfloat16),
        pltpu.VMEM((z.group, z.tokens, z.width), jnp.bfloat16),
    ]
    return call(body, outs, scratch, flops=2 * z.entries * HEAD_SIZE)(
        ds, inverse, kv_own, *kv_earlier, *dv_terms
    )


def pack_terms(group, sums):
    tokens, width = sums[0][0].shape[1:]
    flat = [term for terms in sums for term in terms]

    def body(*refs):
        for r in range(group):
            member = spot(group)[0] ^ hop(group, r)
            number = 0
            for column, terms in enumerate(sums):
                total = refs[number][member].astype(jnp.float32)
                for term in refs[number + 1 : number + len(terms)]:
                    total = total + term[member].astype(jnp.float32)
                refs[len(flat) + r][:, column * width : (column + 1) * width] = total.astype(jnp.bfloat16)
                number += len(terms)

    outs = [jax.ShapeDtypeStruct((tokens, len(sums) * width), jnp.bfloat16)] * group
    return call(body, outs)(*flat)


def unpack(group, pieces, widths, before=(), near=False):
    tokens = pieces[0].shape[0]

    def body(*refs):
        out_refs = refs[group + len(before) :]
        for r in range(group):
            lower = 0
            for number, width in enumerate(widths):
                there = lanes(spot(group)[0] ^ hop(group, r, near), width)
                out_refs[number][:, there] = refs[r][:, lower : lower + width]
                lower += width
        out_refs[-1][...] = jnp.zeros_like(out_refs[-1])

    outs = [jax.ShapeDtypeStruct((tokens, group * width), jnp.bfloat16) for width in widths]
    outs += [jax.ShapeDtypeStruct((8, 128), jnp.float32)]
    return call(body, outs, specs=[VMEM] * group + [ANY] * len(before))(*pieces, *before)


def local(layer_cotangent, out_weight, queries, keys, values):
    tokens = queries.shape[0]
    kv_heads = keys.shape[1] // HEAD_SIZE
    per_head = queries.shape[1] // keys.shape[1]
    count, tp_count = lax.axis_size("ctx"), lax.axis_size("tp")
    group = 1
    while (
        kv_heads % (2 * group) == 0
        and count % (2 * group) == 0
        and WINDOW_LENGTH % (2 * group * tokens) == 0
    ):
        group *= 2
    heads = kv_heads // group
    kv_width = heads * HEAD_SIZE
    back_groups = WINDOW_LENGTH // (group * tokens)

    def trade(sent, near=False):
        return [sent[0]] + [swapped(sent[r], "ctx", hop(group, r, near)) for r in range(1, group)]

    def returned(earlier):
        return [
            shifted(earlier[number], "ctx", -group * (back_groups - number)) for number in range(back_groups)
        ]

    sent = pack_kv(group, keys, values, begin())
    kv_pieces = trade(sent)
    z = Shape(group, back_groups, heads, per_head, tokens)
    query_sent = pack_queries(group, queries, sent[0])
    if tp_count == 2:
        other = head_product(2, 1, out_weight, layer_cotangent, [query_sent[0]])
    else:
        other = head_product(1, 0, out_weight, layer_cotangent, [query_sent[0]])
    kv_own = order_pieces(group, kv_pieces, other)
    kv_earlier = [shifted(kv_own, "ctx", group * step) for step in range(back_groups, 0, -1)]
    if tp_count == 2:
        terms = [head_product(2, 0, out_weight, layer_cotangent, [kv_own, other]), swapped(other, "tp", 1)]
    else:
        terms = [lax.psum_scatter(other, "tp", scatter_dimension=0, tiled=True)]
    qt = turn_queries(z, trade(query_sent))
    grads = trade(pack_grads(group, terms, kv_own))
    e, inverse = softmax(z, kv_own, kv_earlier, qt)
    g, dv_own, dv_earlier = value_terms(z, e, inverse, grads)
    dv_terms = [dv_own] + returned(dv_earlier)
    ds, dk_own, dk_earlier = key_terms(z, e, inverse, qt, g, kv_own, kv_earlier)
    dk_terms = [dk_own] + returned(dk_earlier)
    pieces = trade(query_terms(z, ds, inverse, kv_own, kv_earlier, dv_terms), near=True)
    query_grads, value_gradients, done = unpack(group, pieces, [z.width, kv_width], near=True)
    key_gradients, _ = unpack(group, trade(pack_terms(group, [dk_terms])), [kv_width], [done])
    return (query_grads, key_gradients, value_gradients)


def solution(mesh):
    in_specs = (P("ctx", "tp"), P(None, "tp"), P("ctx", "tp"), P("ctx", "tp"), P("ctx", "tp"))
    out_specs = (P("ctx", "tp"), P("ctx", "tp"), P("ctx", "tp"))
    return jax.shard_map(local, mesh=mesh, in_specs=in_specs, out_specs=out_specs, check_vma=False)
```

```python
import functools

import jax
import jax.numpy as jnp
from jax import lax
from jax.experimental import pallas as pl
from jax.experimental.pallas import tpu as pltpu
from jax.sharding import PartitionSpec as P

HEAD_SIZE = 128
WINDOW_LENGTH = 1024
LOG2_E = 1.4426950408889634
AHEAD = 10**10

score_scale = 168.0 ** (-0.5)

VMEM = pl.BlockSpec(memory_space=pltpu.VMEM)
ANY = pl.BlockSpec(memory_space=pl.ANY)
SMEM = pl.BlockSpec(memory_space=pltpu.SMEM)
NT = (((1,), (1,)), ((), ()))
NN = (((1,), (0,)), ((), ()))


def shifted(value, axis, steps):
    count = lax.axis_size(axis)
    leading, last = (max(0, -steps), min(count, count - steps))
    return lax.ppermute(value, axis, [(source, source + steps) for source in range(leading, last)])


def swapped(value, axis, bits):
    count = lax.axis_size(axis)
    return lax.ppermute(value, axis, [(source, source ^ bits) for source in range(count)])


def call(body, outs, scratch=(), flops=0, exps=0, specs=None, vmem=32):
    def run(*args):
        moved = sum(a.size * a.dtype.itemsize for a in args)
        moved += sum(o.size * o.dtype.itemsize for o in outs)
        return pl.pallas_call(
            body,
            out_shape=tuple(outs),
            in_specs=specs or [SMEM if a.dtype == jnp.int32 else VMEM for a in args],
            out_specs=tuple(VMEM for _ in outs),
            scratch_shapes=list(scratch),
            compiler_params=pltpu.CompilerParams(vmem_limit_bytes=vmem * 1024 * 1024),
            cost_estimate=pl.CostEstimate(flops=flops, bytes_accessed=moved, transcendentals=exps),
        )(*args)

    return run


def spot(group):
    index = lax.axis_index("ctx")
    place = lax.rem(index, group)
    return place, index - place


def lanes(index, width):
    return pl.ds(pl.multiple_of(index * width, width), width)


def begin():
    def body(out_ref):
        out_ref[...] = jnp.zeros_like(out_ref)

    return call(body, [jax.ShapeDtypeStruct((8, 128), jnp.float32)], flops=AHEAD)()[0]


def pack_kv(group, keys, values, before):
    tokens, width = keys.shape[0], keys.shape[1] // group

    def body(k_ref, v_ref, before_ref, *refs):
        for r in range(group):
            member = spot(group)[0] ^ r
            refs[r][:, :width] = k_ref[:, lanes(member, width)]
            refs[r][:, width:] = v_ref[:, lanes(member, width)]

    outs = [jax.ShapeDtypeStruct((tokens, 2 * width), jnp.bfloat16)] * group
    return call(body, outs, flops=AHEAD, specs=[VMEM, VMEM, ANY])(keys, values, before)


def pack_queries(group, queries, before):
    tokens, width = queries.shape[0], queries.shape[1] // group

    def body(q_ref, before_ref, *out_refs):
        for r in range(group):
            out_refs[r][...] = q_ref[:, lanes(spot(group)[0] ^ r, width)]

    outs = [jax.ShapeDtypeStruct((tokens, width), jnp.bfloat16)] * group
    return call(body, outs, specs=[VMEM, ANY])(queries, before)


def order_pieces(group, pieces, before):
    def body(*refs):
        for r in range(group):
            refs[-1][spot(group)[0] ^ r] = refs[r][...]

    outs = [jax.ShapeDtypeStruct((group,) + pieces[0].shape, jnp.bfloat16)]
    return call(body, outs, specs=[VMEM] * group + [ANY])(*pieces, before)[0]


def head_product(parts, part, out_weight, layer_cotangent, before):
    tokens, depth = layer_cotangent.shape
    rows = out_weight.shape[0] // parts
    tile = min(rows, 512)

    def body(w_ref, c_ref, *refs):
        first = (lax.axis_index("tp") ^ part) * rows if parts > 1 else 0

        @pl.loop(0, rows // tile)
        def _(i):
            here = pl.ds(pl.multiple_of(i * tile, tile), tile)
            there = pl.ds(pl.multiple_of(first + i * tile, tile), tile)
            refs[-1][here, :] = lax.dot_general(
                w_ref[there, :], c_ref[...], NT, preferred_element_type=jnp.float32
            ).astype(jnp.bfloat16)

    outs = [jax.ShapeDtypeStruct((rows, tokens), jnp.bfloat16)]
    specs = [VMEM, VMEM] + [ANY] * len(before)
    return call(body, outs, flops=2 * rows * tokens * depth, specs=specs, vmem=16)(
        out_weight, layer_cotangent, *before
    )[0]


def pack_grads(group, terms, before):
    rows, tokens = terms[0].shape
    rows //= group

    def body(*refs):
        for r in range(group):
            there = lanes(spot(group)[0] ^ r, rows)
            total = refs[0][there, :]
            if len(terms) > 1:
                total = total.astype(jnp.float32)
                for term in refs[1 : len(terms)]:
                    total = total + term[there, :].astype(jnp.float32)
            refs[len(terms) + 1 + r][...] = total.astype(jnp.bfloat16)

    outs = [jax.ShapeDtypeStruct((rows, tokens), jnp.bfloat16)] * group
    return call(body, outs, specs=[VMEM] * len(terms) + [ANY])(*terms, before)


class Shape:
    def __init__(self, group, steps, heads, per_head, tokens):
        self.group, self.steps, self.heads, self.per_head, self.tokens = group, steps, heads, per_head, tokens
        self.back = steps * group
        self.span = self.back + 1
        self.total = self.back + group
        self.wide = per_head * tokens
        self.width = heads * per_head * HEAD_SIZE
        self.kv_width = heads * HEAD_SIZE
        self.entries = group * heads * self.wide * self.span * tokens

    def block(self, own_ref, earlier_refs, number):
        if number < self.back:
            return earlier_refs[number // self.group].at[number % self.group]
        return own_ref.at[number - self.back]


def turn_queries(z, pieces):
    def body(*refs):
        for head in range(z.heads):
            for r in range(z.group):
                for j in range(z.per_head):
                    lower = (head * z.per_head + j) * HEAD_SIZE
                    refs[z.group][head, spot(z.group)[0] ^ r, :, j * z.tokens : (j + 1) * z.tokens] = refs[r][
                        :, lower : lower + HEAD_SIZE
                    ].T

    outs = [jax.ShapeDtypeStruct((z.heads, z.group, HEAD_SIZE, z.wide), jnp.bfloat16)]
    return call(body, outs)(*pieces)[0]


def softmax(z, kv_own, kv_earlier, qt):
    factor = score_scale * LOG2_E

    def body(*refs):
        own_ref, earlier_refs = refs[0], refs[1 : 1 + z.steps]
        qt_ref, e_ref, inverse_ref, k_all, s_all = refs[1 + z.steps :]
        first = spot(z.group)[1]
        key_id = lax.broadcasted_iota(jnp.int32, (z.tokens, z.wide), 0)
        query_id = lax.broadcasted_iota(jnp.int32, (z.tokens, z.wide), 1) & (z.tokens - 1)
        for head in range(z.heads):
            at_k = slice(head * HEAD_SIZE, (head + 1) * HEAD_SIZE)
            for number in range(z.total):
                k_all[number] = z.block(own_ref, earlier_refs, number)[:, at_k]

            @pl.loop(0, z.group)
            def _(b):
                qt = qt_ref[head, b]
                top = None
                for c in range(z.span):
                    s = lax.dot_general(k_all[b + c], qt, NN, preferred_element_type=jnp.float32)
                    if c == 0:
                        s = jnp.where(key_id > query_id, s, -jnp.inf)
                    if c == z.back:
                        s = jnp.where(key_id <= query_id, s, -jnp.inf)
                    s_all[c] = s
                    here = jnp.max(s, axis=0, keepdims=True)
                    if c < z.back:
                        here = jnp.where(first + b + c >= z.back, here, -jnp.inf)
                    top = here if top is None else jnp.maximum(top, here)
                norm = jnp.zeros((1, z.wide), jnp.float32)
                for c in range(z.span):
                    base = top
                    if c < z.back:
                        base = jnp.where(first + b + c >= z.back, top, jnp.inf)
                    e = jnp.exp2((s_all[c] - base) * factor)
                    norm = norm + jnp.sum(e, axis=0, keepdims=True)
                    e_ref[head, b, c] = e.astype(jnp.bfloat16)
                inverse_ref[head, b] = 1.0 / norm

    outs = [
        jax.ShapeDtypeStruct((z.heads, z.group, z.span, z.tokens, z.wide), jnp.bfloat16),
        jax.ShapeDtypeStruct((z.heads, z.group, 1, z.wide), jnp.float32),
    ]
    scratch = [
        pltpu.VMEM((z.total, z.tokens, HEAD_SIZE), jnp.bfloat16),
        pltpu.VMEM((z.span, z.tokens, z.wide), jnp.float32),
    ]
    return call(body, outs, scratch, flops=2 * z.entries * HEAD_SIZE, exps=z.entries)(
        kv_own, *kv_earlier, qt
    )


def value_terms(z, e, inverse, grads):
    def body(e_ref, inverse_ref, *refs):
        g_refs, (g_ref, own_ref), earlier_refs = (
            refs[: z.group],
            refs[z.group : z.group + 2],
            refs[z.group + 2 : z.group + 2 + z.steps],
        )
        dv_all = refs[-1]
        place = spot(z.group)[0]
        for head in range(z.heads):
            at = slice(head * HEAD_SIZE, (head + 1) * HEAD_SIZE)
            for r in range(z.group):
                for j in range(z.per_head):
                    lower = (head * z.per_head + j) * HEAD_SIZE
                    g_ref[head, place ^ r, :, j * z.tokens : (j + 1) * z.tokens] = g_refs[r][
                        lower : lower + HEAD_SIZE, :
                    ]
            dv_all[...] = jnp.zeros_like(dv_all)

            @pl.loop(0, z.group)
            def _(b):
                g = (g_ref[head, b].astype(jnp.float32) * inverse_ref[head, b]).astype(jnp.bfloat16)
                for c in range(z.span):
                    dv_all[b + c] += lax.dot_general(
                        e_ref[head, b, c], g, NT, preferred_element_type=jnp.float32
                    )

            for number in range(z.total):
                part = dv_all[number]
                z.block(own_ref, earlier_refs, number)[:, at] = part.astype(own_ref.dtype if number >= z.back else jnp.bfloat16)

    outs = [
        jax.ShapeDtypeStruct((z.heads, z.group, HEAD_SIZE, z.wide), jnp.bfloat16),
        jax.ShapeDtypeStruct((z.group, z.tokens, z.kv_width), jnp.float32),
    ]
    outs += [jax.ShapeDtypeStruct((z.group, z.tokens, z.kv_width), jnp.bfloat16)] * z.steps
    scratch = [pltpu.VMEM((z.total, z.tokens, HEAD_SIZE), jnp.float32)]
    results = call(body, outs, scratch, flops=2 * z.entries * HEAD_SIZE)(e, inverse, *grads)
    return results[0], results[1], results[2:]


def key_terms(z, e, inverse, qt, g, kv_own, kv_earlier):
    def body(e_ref, inverse_ref, qt_ref, g_ref, own_ref, *refs):
        earlier_refs, ds_ref = refs[: z.steps], refs[z.steps]
        dk_own, dk_earlier = refs[z.steps + 1], refs[z.steps + 2 : 2 * z.steps + 2]
        v_all, dk_all, dp_all = refs[2 * z.steps + 2 :]
        for head in range(z.heads):
            at = slice(head * HEAD_SIZE, (head + 1) * HEAD_SIZE)
            at_v = slice(z.kv_width + head * HEAD_SIZE, z.kv_width + (head + 1) * HEAD_SIZE)
            for number in range(z.total):
                v_all[number] = z.block(own_ref, earlier_refs, number)[:, at_v]
            dk_all[...] = jnp.zeros_like(dk_all)

            @pl.loop(0, z.group)
            def _(b):
                g = g_ref[head, b]
                inverse = inverse_ref[head, b]
                delta = jnp.zeros((1, z.wide), jnp.float32)
                for c in range(z.span):
                    dp = lax.dot_general(v_all[b + c], g, NN, preferred_element_type=jnp.float32)
                    delta = delta + jnp.sum(e_ref[head, b, c].astype(jnp.float32) * dp, axis=0, keepdims=True)
                    dp_all[c] = dp
                delta = delta * inverse
                q = (qt_ref[head, b].astype(jnp.float32) * inverse).astype(jnp.bfloat16)
                for c in range(z.span):
                    ds = e_ref[head, b, c] * (dp_all[c] - delta).astype(jnp.bfloat16)
                    ds_ref[head, b, c] = ds
                    dk_all[b + c] += lax.dot_general(ds, q, NT, preferred_element_type=jnp.float32)

            for number in range(z.total):
                part = dk_all[number] * score_scale
                z.block(dk_own, dk_earlier, number)[:, at] = part.astype(
                    dk_own.dtype if number >= z.back else jnp.bfloat16
                )

    outs = [jax.ShapeDtypeStruct(e.shape, jnp.bfloat16)]
    outs += [jax.ShapeDtypeStruct((z.group, z.tokens, z.kv_width), jnp.float32)]
    outs += [jax.ShapeDtypeStruct((z.group, z.tokens, z.kv_width), jnp.bfloat16)] * z.steps
    scratch = [
        pltpu.VMEM((z.total, z.tokens, HEAD_SIZE), jnp.bfloat16),
        pltpu.VMEM((z.total, z.tokens, HEAD_SIZE), jnp.float32),
        pltpu.VMEM((z.span, z.tokens, z.wide), jnp.float32),
    ]
    results = call(body, outs, scratch, flops=4 * z.entries * HEAD_SIZE)(
        e, inverse, qt, g, kv_own, *kv_earlier
    )
    return results[0], results[1], results[2:]


def query_terms(z, ds, inverse, kv_own, kv_earlier, dv_terms):
    def body(ds_ref, inverse_ref, own_ref, *refs):
        earlier_refs, term_refs = refs[: z.steps], refs[z.steps : 2 * z.steps + 1]
        out_refs = refs[2 * z.steps + 1 : 2 * z.steps + 1 + z.group]
        kt_all, dq_all = refs[2 * z.steps + 1 + z.group :]
        for head in range(z.heads):
            at = slice(head * HEAD_SIZE, (head + 1) * HEAD_SIZE)
            for number in range(z.total):
                kt_all[number] = z.block(own_ref, earlier_refs, number)[:, at].T

            @pl.loop(0, z.group)
            def _(b):
                dqt = jnp.zeros((HEAD_SIZE, z.wide), jnp.float32)
                for c in range(z.span):
                    dqt = dqt + lax.dot_general(
                        kt_all[b + c], ds_ref[head, b, c], NN, preferred_element_type=jnp.float32
                    )
                dqt = dqt * (inverse_ref[head, b] * score_scale)
                for j in range(z.per_head):
                    lower = (head * z.per_head + j) * HEAD_SIZE
                    dq_all[b, :, lower : lower + HEAD_SIZE] = (
                        dqt[:, j * z.tokens : (j + 1) * z.tokens].T.astype(jnp.bfloat16)
                    )

        for r in range(z.group):
            member = spot(z.group)[0] ^ r
            dv = term_refs[0][member]
            for term in term_refs[1:]:
                dv = dv + term[member].astype(jnp.float32)
            out_refs[r][:, : z.width] = dq_all[member]
            out_refs[r][:, z.width :] = dv.astype(jnp.bfloat16)

    outs = [jax.ShapeDtypeStruct((z.tokens, z.width + z.kv_width), jnp.bfloat16)] * z.group
    scratch = [
        pltpu.VMEM((z.total, HEAD_SIZE, z.tokens), jnp.bfloat16),
        pltpu.VMEM((z.group, z.tokens, z.width), jnp.bfloat16),
    ]
    return call(body, outs, scratch, flops=2 * z.entries * HEAD_SIZE)(
        ds, inverse, kv_own, *kv_earlier, *dv_terms
    )


def pack_terms(group, sums):
    tokens, width = sums[0][0].shape[1:]
    flat = [term for terms in sums for term in terms]

    def body(*refs):
        for r in range(group):
            member = spot(group)[0] ^ r
            number = 0
            for column, terms in enumerate(sums):
                total = refs[number][member].astype(jnp.float32)
                for term in refs[number + 1 : number + len(terms)]:
                    total = total + term[member].astype(jnp.float32)
                refs[len(flat) + r][:, column * width : (column + 1) * width] = total.astype(jnp.bfloat16)
                number += len(terms)

    outs = [jax.ShapeDtypeStruct((tokens, len(sums) * width), jnp.bfloat16)] * group
    return call(body, outs)(*flat)


def unpack(group, pieces, widths, before=()):
    tokens = pieces[0].shape[0]

    def body(*refs):
        out_refs = refs[group + len(before) :]
        for r in range(group):
            lower = 0
            for number, width in enumerate(widths):
                there = lanes(spot(group)[0] ^ r, width)
                out_refs[number][:, there] = refs[r][:, lower : lower + width]
                lower += width
        out_refs[-1][...] = jnp.zeros_like(out_refs[-1])

    outs = [jax.ShapeDtypeStruct((tokens, group * width), jnp.bfloat16) for width in widths]
    outs += [jax.ShapeDtypeStruct((8, 128), jnp.float32)]
    return call(body, outs, specs=[VMEM] * group + [ANY] * len(before))(*pieces, *before)


def local(layer_cotangent, out_weight, queries, keys, values):
    tokens = queries.shape[0]
    kv_heads = keys.shape[1] // HEAD_SIZE
    per_head = queries.shape[1] // keys.shape[1]
    count, tp_count = lax.axis_size("ctx"), lax.axis_size("tp")
    group = 1
    while (
        kv_heads % (2 * group) == 0
        and count % (2 * group) == 0
        and WINDOW_LENGTH % (2 * group * tokens) == 0
    ):
        group *= 2
    heads = kv_heads // group
    kv_width = heads * HEAD_SIZE
    back_groups = WINDOW_LENGTH // (group * tokens)

    def trade(sent):
        return [sent[0]] + [swapped(sent[r], "ctx", r) for r in range(1, group)]

    def returned(earlier):
        return [
            shifted(earlier[number], "ctx", -group * (back_groups - number)) for number in range(back_groups)
        ]

    sent = pack_kv(group, keys, values, begin())
    kv_pieces = trade(sent)
    z = Shape(group, back_groups, heads, per_head, tokens)
    query_sent = pack_queries(group, queries, sent[0])
    if tp_count == 2:
        other = head_product(2, 1, out_weight, layer_cotangent, [query_sent[0]])
    else:
        other = head_product(1, 0, out_weight, layer_cotangent, [query_sent[0]])
    kv_own = order_pieces(group, kv_pieces, other)
    kv_earlier = [shifted(kv_own, "ctx", group * step) for step in range(back_groups, 0, -1)]
    if tp_count == 2:
        terms = [head_product(2, 0, out_weight, layer_cotangent, [kv_own, other]), swapped(other, "tp", 1)]
    else:
        terms = [lax.psum_scatter(other, "tp", scatter_dimension=0, tiled=True)]
    qt = turn_queries(z, trade(query_sent))
    grads = trade(pack_grads(group, terms, kv_own))
    e, inverse = softmax(z, kv_own, kv_earlier, qt)
    g, dv_own, dv_earlier = value_terms(z, e, inverse, grads)
    dv_terms = [dv_own] + returned(dv_earlier)
    ds, dk_own, dk_earlier = key_terms(z, e, inverse, qt, g, kv_own, kv_earlier)
    dk_terms = [dk_own] + returned(dk_earlier)
    pieces = trade(query_terms(z, ds, inverse, kv_own, kv_earlier, dv_terms))
    query_grads, value_gradients, done = unpack(group, pieces, [z.width, kv_width])
    key_gradients, _ = unpack(group, trade(pack_terms(group, [dk_terms])), [kv_width], [done])
    return (query_grads, key_gradients, value_gradients)


def solution(mesh):
    in_specs = (P("ctx", "tp"), P(None, "tp"), P("ctx", "tp"), P("ctx", "tp"), P("ctx", "tp"))
    out_specs = (P("ctx", "tp"), P("ctx", "tp"), P("ctx", "tp"))
    return jax.shard_map(local, mesh=mesh, in_specs=in_specs, out_specs=out_specs, check_vma=False)
```

```python
import functools

import jax
import jax.numpy as jnp
from jax import lax
from jax.experimental import pallas as pl
from jax.experimental.pallas import tpu as pltpu
from jax.sharding import PartitionSpec as P

HEAD_SIZE = 128
WINDOW_LENGTH = 1024
LOG2_E = 1.4426950408889634
AHEAD = 10**10

score_scale = 168.0 ** (-0.5)

VMEM = pl.BlockSpec(memory_space=pltpu.VMEM)
ANY = pl.BlockSpec(memory_space=pl.ANY)
SMEM = pl.BlockSpec(memory_space=pltpu.SMEM)
NT = (((1,), (1,)), ((), ()))
NN = (((1,), (0,)), ((), ()))


def shifted(value, axis, steps):
    count = lax.axis_size(axis)
    leading, last = (max(0, -steps), min(count, count - steps))
    return lax.ppermute(value, axis, [(source, source + steps) for source in range(leading, last)])


def swapped(value, axis, bits):
    count = lax.axis_size(axis)
    return lax.ppermute(value, axis, [(source, source ^ bits) for source in range(count)])


def call(body, outs, scratch=(), flops=0, exps=0, specs=None, vmem=32):
    def run(*args):
        moved = sum(a.size * a.dtype.itemsize for a in args)
        moved += sum(o.size * o.dtype.itemsize for o in outs)
        return pl.pallas_call(
            body,
            out_shape=tuple(outs),
            in_specs=specs or [SMEM if a.dtype == jnp.int32 else VMEM for a in args],
            out_specs=tuple(VMEM for _ in outs),
            scratch_shapes=list(scratch),
            compiler_params=pltpu.CompilerParams(vmem_limit_bytes=vmem * 1024 * 1024),
            cost_estimate=pl.CostEstimate(flops=flops, bytes_accessed=moved, transcendentals=exps),
        )(*args)

    return run


def spot(group):
    index = lax.axis_index("ctx")
    place = lax.rem(index, group)
    return place, index - place


def hop(group, r):
    turned, bit = 0, 1
    while bit < group:
        turned, r, bit = 2 * turned + r % 2, r // 2, 2 * bit
    return turned


def lanes(index, width):
    return pl.ds(pl.multiple_of(index * width, width), width)


def begin():
    def body(out_ref):
        out_ref[...] = jnp.zeros_like(out_ref)

    return call(body, [jax.ShapeDtypeStruct((8, 128), jnp.float32)], flops=AHEAD)()[0]


def pack_kv(group, keys, values, before):
    tokens, width = keys.shape[0], keys.shape[1] // group

    def body(k_ref, v_ref, before_ref, *refs):
        for r in range(group):
            member = spot(group)[0] ^ hop(group, r)
            refs[r][:, :width] = k_ref[:, lanes(member, width)]
            refs[r][:, width:] = v_ref[:, lanes(member, width)]

    outs = [jax.ShapeDtypeStruct((tokens, 2 * width), jnp.bfloat16)] * group
    return call(body, outs, flops=AHEAD, specs=[VMEM, VMEM, ANY])(keys, values, before)


def pack_queries(group, queries, before):
    tokens, width = queries.shape[0], queries.shape[1] // group

    def body(q_ref, before_ref, *out_refs):
        for r in range(group):
            out_refs[r][...] = q_ref[:, lanes(spot(group)[0] ^ hop(group, r), width)]

    outs = [jax.ShapeDtypeStruct((tokens, width), jnp.bfloat16)] * group
    return call(body, outs, specs=[VMEM, ANY])(queries, before)


def order_pieces(group, pieces, before):
    def body(*refs):
        for r in range(group):
            refs[-1][spot(group)[0] ^ hop(group, r)] = refs[r][...]

    outs = [jax.ShapeDtypeStruct((group,) + pieces[0].shape, jnp.bfloat16)]
    return call(body, outs, specs=[VMEM] * group + [ANY])(*pieces, before)[0]


def head_product(parts, part, out_weight, layer_cotangent, before):
    tokens, depth = layer_cotangent.shape
    rows = out_weight.shape[0] // parts
    tile = min(rows, 512)

    def body(w_ref, c_ref, *refs):
        first = (lax.axis_index("tp") ^ part) * rows if parts > 1 else 0

        @pl.loop(0, rows // tile)
        def _(i):
            here = pl.ds(pl.multiple_of(i * tile, tile), tile)
            there = pl.ds(pl.multiple_of(first + i * tile, tile), tile)
            refs[-1][here, :] = lax.dot_general(
                w_ref[there, :], c_ref[...], NT, preferred_element_type=jnp.float32
            ).astype(jnp.bfloat16)

    outs = [jax.ShapeDtypeStruct((rows, tokens), jnp.bfloat16)]
    specs = [VMEM, VMEM] + [ANY] * len(before)
    return call(body, outs, flops=2 * rows * tokens * depth, specs=specs, vmem=16)(
        out_weight, layer_cotangent, *before
    )[0]


def pack_grads(group, terms, before):
    rows, tokens = terms[0].shape
    rows //= group

    def body(*refs):
        for r in range(group):
            there = lanes(spot(group)[0] ^ hop(group, r), rows)
            total = refs[0][there, :]
            if len(terms) > 1:
                total = total.astype(jnp.float32)
                for term in refs[1 : len(terms)]:
                    total = total + term[there, :].astype(jnp.float32)
            refs[len(terms) + 1 + r][...] = total.astype(jnp.bfloat16)

    outs = [jax.ShapeDtypeStruct((rows, tokens), jnp.bfloat16)] * group
    return call(body, outs, specs=[VMEM] * len(terms) + [ANY])(*terms, before)


class Shape:
    def __init__(self, group, steps, heads, per_head, tokens):
        self.group, self.steps, self.heads, self.per_head, self.tokens = group, steps, heads, per_head, tokens
        self.back = steps * group
        self.span = self.back + 1
        self.total = self.back + group
        self.wide = per_head * tokens
        self.width = heads * per_head * HEAD_SIZE
        self.kv_width = heads * HEAD_SIZE
        self.entries = group * heads * self.wide * self.span * tokens

    def block(self, own_ref, earlier_refs, number):
        if number < self.back:
            return earlier_refs[number // self.group].at[number % self.group]
        return own_ref.at[number - self.back]


def turn_queries(z, pieces):
    def body(*refs):
        for head in range(z.heads):
            for r in range(z.group):
                for j in range(z.per_head):
                    lower = (head * z.per_head + j) * HEAD_SIZE
                    refs[z.group][head, spot(z.group)[0] ^ hop(z.group, r), :, j * z.tokens : (j + 1) * z.tokens] = refs[r][
                        :, lower : lower + HEAD_SIZE
                    ].T

    outs = [jax.ShapeDtypeStruct((z.heads, z.group, HEAD_SIZE, z.wide), jnp.bfloat16)]
    return call(body, outs)(*pieces)[0]


def softmax(z, kv_own, kv_earlier, qt):
    factor = score_scale * LOG2_E

    def body(*refs):
        own_ref, earlier_refs = refs[0], refs[1 : 1 + z.steps]
        qt_ref, e_ref, inverse_ref, k_all, s_all = refs[1 + z.steps :]
        first = spot(z.group)[1]
        key_id = lax.broadcasted_iota(jnp.int32, (z.tokens, z.wide), 0)
        query_id = lax.broadcasted_iota(jnp.int32, (z.tokens, z.wide), 1) & (z.tokens - 1)
        for head in range(z.heads):
            at_k = slice(head * HEAD_SIZE, (head + 1) * HEAD_SIZE)
            for number in range(z.total):
                k_all[number] = z.block(own_ref, earlier_refs, number)[:, at_k]

            @pl.loop(0, z.group)
            def _(b):
                qt = qt_ref[head, b]
                top = None
                for c in range(z.span):
                    s = lax.dot_general(k_all[b + c], qt, NN, preferred_element_type=jnp.float32)
                    if c == 0:
                        s = jnp.where(key_id > query_id, s, -jnp.inf)
                    if c == z.back:
                        s = jnp.where(key_id <= query_id, s, -jnp.inf)
                    s_all[c] = s
                    here = jnp.max(s, axis=0, keepdims=True)
                    if c < z.back:
                        here = jnp.where(first + b + c >= z.back, here, -jnp.inf)
                    top = here if top is None else jnp.maximum(top, here)
                norm = jnp.zeros((1, z.wide), jnp.float32)
                for c in range(z.span):
                    base = top
                    if c < z.back:
                        base = jnp.where(first + b + c >= z.back, top, jnp.inf)
                    e = jnp.exp2((s_all[c] - base) * factor)
                    norm = norm + jnp.sum(e, axis=0, keepdims=True)
                    e_ref[head, b, c] = e.astype(jnp.bfloat16)
                inverse_ref[head, b] = 1.0 / norm

    outs = [
        jax.ShapeDtypeStruct((z.heads, z.group, z.span, z.tokens, z.wide), jnp.bfloat16),
        jax.ShapeDtypeStruct((z.heads, z.group, 1, z.wide), jnp.float32),
    ]
    scratch = [
        pltpu.VMEM((z.total, z.tokens, HEAD_SIZE), jnp.bfloat16),
        pltpu.VMEM((z.span, z.tokens, z.wide), jnp.float32),
    ]
    return call(body, outs, scratch, flops=2 * z.entries * HEAD_SIZE, exps=z.entries)(
        kv_own, *kv_earlier, qt
    )


def value_terms(z, e, inverse, grads):
    def body(e_ref, inverse_ref, *refs):
        g_refs, (g_ref, own_ref), earlier_refs = (
            refs[: z.group],
            refs[z.group : z.group + 2],
            refs[z.group + 2 : z.group + 2 + z.steps],
        )
        dv_all = refs[-1]
        place = spot(z.group)[0]
        for head in range(z.heads):
            at = slice(head * HEAD_SIZE, (head + 1) * HEAD_SIZE)
            for r in range(z.group):
                for j in range(z.per_head):
                    lower = (head * z.per_head + j) * HEAD_SIZE
                    g_ref[head, place ^ hop(z.group, r), :, j * z.tokens : (j + 1) * z.tokens] = g_refs[r][
                        lower : lower + HEAD_SIZE, :
                    ]
            dv_all[...] = jnp.zeros_like(dv_all)

            @pl.loop(0, z.group)
            def _(b):
                g = (g_ref[head, b].astype(jnp.float32) * inverse_ref[head, b]).astype(jnp.bfloat16)
                for c in range(z.span):
                    dv_all[b + c] += lax.dot_general(
                        e_ref[head, b, c], g, NT, preferred_element_type=jnp.float32
                    )

            for number in range(z.total):
                part = dv_all[number]
                z.block(own_ref, earlier_refs, number)[:, at] = part.astype(own_ref.dtype if number >= z.back else jnp.bfloat16)

    outs = [
        jax.ShapeDtypeStruct((z.heads, z.group, HEAD_SIZE, z.wide), jnp.bfloat16),
        jax.ShapeDtypeStruct((z.group, z.tokens, z.kv_width), jnp.float32),
    ]
    outs += [jax.ShapeDtypeStruct((z.group, z.tokens, z.kv_width), jnp.bfloat16)] * z.steps
    scratch = [pltpu.VMEM((z.total, z.tokens, HEAD_SIZE), jnp.float32)]
    results = call(body, outs, scratch, flops=2 * z.entries * HEAD_SIZE)(e, inverse, *grads)
    return results[0], results[1], results[2:]


def key_terms(z, e, inverse, qt, g, kv_own, kv_earlier):
    def body(e_ref, inverse_ref, qt_ref, g_ref, own_ref, *refs):
        earlier_refs, ds_ref = refs[: z.steps], refs[z.steps]
        dk_own, dk_earlier = refs[z.steps + 1], refs[z.steps + 2 : 2 * z.steps + 2]
        v_all, dk_all, dp_all = refs[2 * z.steps + 2 :]
        for head in range(z.heads):
            at = slice(head * HEAD_SIZE, (head + 1) * HEAD_SIZE)
            at_v = slice(z.kv_width + head * HEAD_SIZE, z.kv_width + (head + 1) * HEAD_SIZE)
            for number in range(z.total):
                v_all[number] = z.block(own_ref, earlier_refs, number)[:, at_v]
            dk_all[...] = jnp.zeros_like(dk_all)

            @pl.loop(0, z.group)
            def _(b):
                g = g_ref[head, b]
                inverse = inverse_ref[head, b]
                delta = jnp.zeros((1, z.wide), jnp.float32)
                for c in range(z.span):
                    dp = lax.dot_general(v_all[b + c], g, NN, preferred_element_type=jnp.float32)
                    delta = delta + jnp.sum(e_ref[head, b, c].astype(jnp.float32) * dp, axis=0, keepdims=True)
                    dp_all[c] = dp
                delta = delta * inverse
                q = (qt_ref[head, b].astype(jnp.float32) * inverse).astype(jnp.bfloat16)
                for c in range(z.span):
                    ds = e_ref[head, b, c] * (dp_all[c] - delta).astype(jnp.bfloat16)
                    ds_ref[head, b, c] = ds
                    dk_all[b + c] += lax.dot_general(ds, q, NT, preferred_element_type=jnp.float32)

            for number in range(z.total):
                part = dk_all[number] * score_scale
                z.block(dk_own, dk_earlier, number)[:, at] = part.astype(
                    dk_own.dtype if number >= z.back else jnp.bfloat16
                )

    outs = [jax.ShapeDtypeStruct(e.shape, jnp.bfloat16)]
    outs += [jax.ShapeDtypeStruct((z.group, z.tokens, z.kv_width), jnp.float32)]
    outs += [jax.ShapeDtypeStruct((z.group, z.tokens, z.kv_width), jnp.bfloat16)] * z.steps
    scratch = [
        pltpu.VMEM((z.total, z.tokens, HEAD_SIZE), jnp.bfloat16),
        pltpu.VMEM((z.total, z.tokens, HEAD_SIZE), jnp.float32),
        pltpu.VMEM((z.span, z.tokens, z.wide), jnp.float32),
    ]
    results = call(body, outs, scratch, flops=4 * z.entries * HEAD_SIZE)(
        e, inverse, qt, g, kv_own, *kv_earlier
    )
    return results[0], results[1], results[2:]


def query_terms(z, ds, inverse, kv_own, kv_earlier, dv_terms):
    def body(ds_ref, inverse_ref, own_ref, *refs):
        earlier_refs, term_refs = refs[: z.steps], refs[z.steps : 2 * z.steps + 1]
        out_refs = refs[2 * z.steps + 1 : 2 * z.steps + 1 + z.group]
        kt_all, dq_all = refs[2 * z.steps + 1 + z.group :]
        for head in range(z.heads):
            at = slice(head * HEAD_SIZE, (head + 1) * HEAD_SIZE)
            for number in range(z.total):
                kt_all[number] = z.block(own_ref, earlier_refs, number)[:, at].T

            @pl.loop(0, z.group)
            def _(b):
                dqt = jnp.zeros((HEAD_SIZE, z.wide), jnp.float32)
                for c in range(z.span):
                    dqt = dqt + lax.dot_general(
                        kt_all[b + c], ds_ref[head, b, c], NN, preferred_element_type=jnp.float32
                    )
                dqt = dqt * (inverse_ref[head, b] * score_scale)
                for j in range(z.per_head):
                    lower = (head * z.per_head + j) * HEAD_SIZE
                    dq_all[b, :, lower : lower + HEAD_SIZE] = (
                        dqt[:, j * z.tokens : (j + 1) * z.tokens].T.astype(jnp.bfloat16)
                    )

        for r in range(z.group):
            member = spot(z.group)[0] ^ hop(z.group, r)
            dv = term_refs[0][member]
            for term in term_refs[1:]:
                dv = dv + term[member].astype(jnp.float32)
            out_refs[r][:, : z.width] = dq_all[member]
            out_refs[r][:, z.width :] = dv.astype(jnp.bfloat16)

    outs = [jax.ShapeDtypeStruct((z.tokens, z.width + z.kv_width), jnp.bfloat16)] * z.group
    scratch = [
        pltpu.VMEM((z.total, HEAD_SIZE, z.tokens), jnp.bfloat16),
        pltpu.VMEM((z.group, z.tokens, z.width), jnp.bfloat16),
    ]
    return call(body, outs, scratch, flops=2 * z.entries * HEAD_SIZE)(
        ds, inverse, kv_own, *kv_earlier, *dv_terms
    )


def pack_terms(group, sums):
    tokens, width = sums[0][0].shape[1:]
    flat = [term for terms in sums for term in terms]

    def body(*refs):
        for r in range(group):
            member = spot(group)[0] ^ hop(group, r)
            number = 0
            for column, terms in enumerate(sums):
                total = refs[number][member].astype(jnp.float32)
                for term in refs[number + 1 : number + len(terms)]:
                    total = total + term[member].astype(jnp.float32)
                refs[len(flat) + r][:, column * width : (column + 1) * width] = total.astype(jnp.bfloat16)
                number += len(terms)

    outs = [jax.ShapeDtypeStruct((tokens, len(sums) * width), jnp.bfloat16)] * group
    return call(body, outs)(*flat)


def unpack(group, pieces, widths, before=()):
    tokens = pieces[0].shape[0]

    def body(*refs):
        out_refs = refs[group + len(before) :]
        for r in range(group):
            lower = 0
            for number, width in enumerate(widths):
                there = lanes(spot(group)[0] ^ hop(group, r), width)
                out_refs[number][:, there] = refs[r][:, lower : lower + width]
                lower += width
        out_refs[-1][...] = jnp.zeros_like(out_refs[-1])

    outs = [jax.ShapeDtypeStruct((tokens, group * width), jnp.bfloat16) for width in widths]
    outs += [jax.ShapeDtypeStruct((8, 128), jnp.float32)]
    return call(body, outs, specs=[VMEM] * group + [ANY] * len(before))(*pieces, *before)


def local(layer_cotangent, out_weight, queries, keys, values):
    tokens = queries.shape[0]
    kv_heads = keys.shape[1] // HEAD_SIZE
    per_head = queries.shape[1] // keys.shape[1]
    count, tp_count = lax.axis_size("ctx"), lax.axis_size("tp")
    group = 1
    while (
        kv_heads % (2 * group) == 0
        and count % (2 * group) == 0
        and WINDOW_LENGTH % (2 * group * tokens) == 0
    ):
        group *= 2
    heads = kv_heads // group
    kv_width = heads * HEAD_SIZE
    back_groups = WINDOW_LENGTH // (group * tokens)

    def trade(sent):
        return [sent[0]] + [swapped(sent[r], "ctx", hop(group, r)) for r in range(1, group)]

    def returned(earlier):
        return [
            shifted(earlier[number], "ctx", -group * (back_groups - number)) for number in range(back_groups)
        ]

    sent = pack_kv(group, keys, values, begin())
    kv_pieces = trade(sent)
    z = Shape(group, back_groups, heads, per_head, tokens)
    query_sent = pack_queries(group, queries, sent[0])
    if tp_count == 2:
        other = head_product(2, 1, out_weight, layer_cotangent, [query_sent[0]])
    else:
        other = head_product(1, 0, out_weight, layer_cotangent, [query_sent[0]])
    kv_own = order_pieces(group, kv_pieces, other)
    kv_earlier = [shifted(kv_own, "ctx", group * step) for step in range(back_groups, 0, -1)]
    if tp_count == 2:
        terms = [head_product(2, 0, out_weight, layer_cotangent, [kv_own, other]), swapped(other, "tp", 1)]
    else:
        terms = [lax.psum_scatter(other, "tp", scatter_dimension=0, tiled=True)]
    qt = turn_queries(z, trade(query_sent))
    grads = trade(pack_grads(group, terms, kv_own))
    e, inverse = softmax(z, kv_own, kv_earlier, qt)
    g, dv_own, dv_earlier = value_terms(z, e, inverse, grads)
    dv_terms = [dv_own] + returned(dv_earlier)
    ds, dk_own, dk_earlier = key_terms(z, e, inverse, qt, g, kv_own, kv_earlier)
    dk_terms = [dk_own] + returned(dk_earlier)
    pieces = trade(query_terms(z, ds, inverse, kv_own, kv_earlier, dv_terms))
    query_grads, value_gradients, done = unpack(group, pieces, [z.width, kv_width])
    key_gradients, _ = unpack(group, trade(pack_terms(group, [dk_terms])), [kv_width], [done])
    return (query_grads, key_gradients, value_gradients)


def solution(mesh):
    in_specs = (P("ctx", "tp"), P(None, "tp"), P("ctx", "tp"), P("ctx", "tp"), P("ctx", "tp"))
    out_specs = (P("ctx", "tp"), P("ctx", "tp"), P("ctx", "tp"))
    return jax.shard_map(local, mesh=mesh, in_specs=in_specs, out_specs=out_specs, check_vma=False)
```

```python
import functools

import jax
import jax.numpy as jnp
from jax import lax
from jax.experimental import pallas as pl
from jax.experimental.pallas import tpu as pltpu
from jax.sharding import PartitionSpec as P

HEAD_SIZE = 128
WINDOW_LENGTH = 1024
LOG2_E = 1.4426950408889634
AHEAD = 10**10

score_scale = 168.0 ** (-0.5)

VMEM = pl.BlockSpec(memory_space=pltpu.VMEM)
ANY = pl.BlockSpec(memory_space=pl.ANY)
SMEM = pl.BlockSpec(memory_space=pltpu.SMEM)
NT = (((1,), (1,)), ((), ()))
NN = (((1,), (0,)), ((), ()))


def shifted(value, axis, steps):
    count = lax.axis_size(axis)
    leading, last = (max(0, -steps), min(count, count - steps))
    return lax.ppermute(value, axis, [(source, source + steps) for source in range(leading, last)])


def swapped(value, axis, bits):
    count = lax.axis_size(axis)
    return lax.ppermute(value, axis, [(source, source ^ bits) for source in range(count)])


def call(body, outs, scratch=(), flops=0, exps=0, specs=None, vmem=32):
    def run(*args):
        moved = sum(a.size * a.dtype.itemsize for a in args)
        moved += sum(o.size * o.dtype.itemsize for o in outs)
        return pl.pallas_call(
            body,
            out_shape=tuple(outs),
            in_specs=specs or [SMEM if a.dtype == jnp.int32 else VMEM for a in args],
            out_specs=tuple(VMEM for _ in outs),
            scratch_shapes=list(scratch),
            compiler_params=pltpu.CompilerParams(vmem_limit_bytes=vmem * 1024 * 1024),
            cost_estimate=pl.CostEstimate(flops=flops, bytes_accessed=moved, transcendentals=exps),
        )(*args)

    return run


def spot(group):
    index = lax.axis_index("ctx")
    place = lax.rem(index, group)
    return place, index - place


def lanes(index, width):
    return pl.ds(pl.multiple_of(index * width, width), width)


def begin():
    def body(out_ref):
        out_ref[...] = jnp.zeros_like(out_ref)

    return call(body, [jax.ShapeDtypeStruct((8, 128), jnp.float32)], flops=AHEAD)()[0]


def pack_heads(group, arrays, before, flops):
    tokens = arrays[0].shape[0]
    widths = [array.shape[1] // group for array in arrays]

    def body(*refs):
        for r in range(group):
            lower = 0
            for ref, width in zip(refs, widths):
                refs[len(arrays) + 1 + r][:, lower : lower + width] = ref[:, lanes(spot(group)[0] ^ r, width)]
                lower += width

    outs = [jax.ShapeDtypeStruct((tokens, sum(widths)), jnp.bfloat16)] * group
    return call(body, outs, flops=flops, specs=[VMEM] * len(arrays) + [ANY])(*arrays, before)


def order_pieces(group, pieces, width, before, flops):
    tokens = pieces[0].shape[0]

    def body(*refs):
        for r in range(group):
            refs[-1][spot(group)[0] ^ r] = refs[r][:, :width]

    outs = [jax.ShapeDtypeStruct((group, tokens, width), jnp.bfloat16)]
    return call(body, outs, flops=flops, specs=[VMEM] * group + [ANY])(*pieces, before)[0]


def head_product(parts, part, out_weight, layer_cotangent, before):
    tokens, depth = layer_cotangent.shape
    rows = out_weight.shape[0] // parts
    tile = min(rows, 512)

    def body(w_ref, c_ref, *refs):
        first = (lax.axis_index("tp") ^ part) * rows if parts > 1 else 0

        @pl.loop(0, rows // tile)
        def _(i):
            here = pl.ds(pl.multiple_of(i * tile, tile), tile)
            there = pl.ds(pl.multiple_of(first + i * tile, tile), tile)
            refs[-1][here, :] = lax.dot_general(
                w_ref[there, :], c_ref[...], NT, preferred_element_type=jnp.float32
            ).astype(jnp.bfloat16)

    outs = [jax.ShapeDtypeStruct((rows, tokens), jnp.bfloat16)]
    specs = [VMEM, VMEM] + [ANY] * len(before)
    return call(body, outs, flops=2 * rows * tokens * depth, specs=specs, vmem=16)(
        out_weight, layer_cotangent, *before
    )[0]


def pack_grads(group, terms, before):
    rows, tokens = terms[0].shape
    rows //= group

    def body(*refs):
        for r in range(group):
            there = lanes(spot(group)[0] ^ r, rows)
            total = refs[0][there, :]
            if len(terms) > 1:
                total = total.astype(jnp.float32)
                for term in refs[1 : len(terms)]:
                    total = total + term[there, :].astype(jnp.float32)
            refs[len(terms) + 1 + r][...] = total.astype(jnp.bfloat16)

    outs = [jax.ShapeDtypeStruct((rows, tokens), jnp.bfloat16)] * group
    return call(body, outs, specs=[VMEM] * len(terms) + [ANY])(*terms, before)


class Shape:
    def __init__(self, group, steps, heads, per_head, tokens):
        self.group, self.steps, self.heads, self.per_head, self.tokens = group, steps, heads, per_head, tokens
        self.back = steps * group
        self.span = self.back + 1
        self.total = self.back + group
        self.wide = per_head * tokens
        self.width = heads * per_head * HEAD_SIZE
        self.kv_width = heads * HEAD_SIZE
        self.entries = group * heads * self.wide * self.span * tokens

    def block(self, own_ref, earlier_refs, number):
        if number < self.back:
            return earlier_refs[number // self.group].at[number % self.group]
        return own_ref.at[number - self.back]


def turn_queries(z, pieces):
    def body(*refs):
        for head in range(z.heads):
            for r in range(z.group):
                for j in range(z.per_head):
                    lower = z.kv_width + (head * z.per_head + j) * HEAD_SIZE
                    refs[z.group][head, spot(z.group)[0] ^ r, :, j * z.tokens : (j + 1) * z.tokens] = refs[r][
                        :, lower : lower + HEAD_SIZE
                    ].T

    outs = [jax.ShapeDtypeStruct((z.heads, z.group, HEAD_SIZE, z.wide), jnp.bfloat16)]
    return call(body, outs)(*pieces)[0]


def softmax(z, k_own, k_earlier, qt):
    factor = score_scale * LOG2_E

    def body(own_ref, *refs):
        earlier_refs = refs[: z.steps]
        qt_ref, e_ref, inverse_ref, k_all, s_all = refs[z.steps :]
        first = spot(z.group)[1]
        key_id = lax.broadcasted_iota(jnp.int32, (z.tokens, z.wide), 0)
        query_id = lax.broadcasted_iota(jnp.int32, (z.tokens, z.wide), 1) & (z.tokens - 1)
        for head in range(z.heads):
            at = slice(head * HEAD_SIZE, (head + 1) * HEAD_SIZE)
            for number in range(z.total):
                k_all[number] = z.block(own_ref, earlier_refs, number)[:, at]

            @pl.loop(0, z.group)
            def _(b):
                qt = qt_ref[head, b]
                top = None
                for c in range(z.span):
                    s = lax.dot_general(k_all[b + c], qt, NN, preferred_element_type=jnp.float32)
                    if c == 0:
                        s = jnp.where(key_id > query_id, s, -jnp.inf)
                    if c == z.back:
                        s = jnp.where(key_id <= query_id, s, -jnp.inf)
                    s_all[c] = s
                    here = jnp.max(s, axis=0, keepdims=True)
                    if c < z.back:
                        here = jnp.where(first + b + c >= z.back, here, -jnp.inf)
                    top = here if top is None else jnp.maximum(top, here)
                norm = jnp.zeros((1, z.wide), jnp.float32)
                for c in range(z.span):
                    base = top
                    if c < z.back:
                        base = jnp.where(first + b + c >= z.back, top, jnp.inf)
                    e = jnp.exp2((s_all[c] - base) * factor)
                    norm = norm + jnp.sum(e, axis=0, keepdims=True)
                    e_ref[head, b, c] = e.astype(jnp.bfloat16)
                inverse_ref[head, b] = 1.0 / norm

    outs = [
        jax.ShapeDtypeStruct((z.heads, z.group, z.span, z.tokens, z.wide), jnp.bfloat16),
        jax.ShapeDtypeStruct((z.heads, z.group, 1, z.wide), jnp.float32),
    ]
    scratch = [
        pltpu.VMEM((z.total, z.tokens, HEAD_SIZE), jnp.bfloat16),
        pltpu.VMEM((z.span, z.tokens, z.wide), jnp.float32),
    ]
    return call(body, outs, scratch, flops=2 * z.entries * HEAD_SIZE, exps=z.entries)(
        k_own, *k_earlier, qt
    )


def value_terms(z, e, inverse, grads):
    def body(e_ref, inverse_ref, *refs):
        g_refs, (g_ref, own_ref), earlier_refs = (
            refs[: z.group],
            refs[z.group : z.group + 2],
            refs[z.group + 2 : z.group + 2 + z.steps],
        )
        dv_all = refs[-1]
        place = spot(z.group)[0]
        for head in range(z.heads):
            at = slice(head * HEAD_SIZE, (head + 1) * HEAD_SIZE)
            for r in range(z.group):
                for j in range(z.per_head):
                    lower = (head * z.per_head + j) * HEAD_SIZE
                    g_ref[head, place ^ r, :, j * z.tokens : (j + 1) * z.tokens] = g_refs[r][
                        lower : lower + HEAD_SIZE, :
                    ]
            dv_all[...] = jnp.zeros_like(dv_all)

            @pl.loop(0, z.group)
            def _(b):
                g = (g_ref[head, b].astype(jnp.float32) * inverse_ref[head, b]).astype(jnp.bfloat16)
                for c in range(z.span):
                    dv_all[b + c] += lax.dot_general(
                        e_ref[head, b, c], g, NT, preferred_element_type=jnp.float32
                    )

            for number in range(z.total):
                z.block(own_ref, earlier_refs, number)[:, at] = dv_all[number].astype(
                    own_ref.dtype if number >= z.back else jnp.bfloat16
                )

    outs = [
        jax.ShapeDtypeStruct((z.heads, z.group, HEAD_SIZE, z.wide), jnp.bfloat16),
        jax.ShapeDtypeStruct((z.group, z.tokens, z.kv_width), jnp.float32),
    ]
    outs += [jax.ShapeDtypeStruct((z.group, z.tokens, z.kv_width), jnp.bfloat16)] * z.steps
    scratch = [pltpu.VMEM((z.total, z.tokens, HEAD_SIZE), jnp.float32)]
    results = call(body, outs, scratch, flops=2 * z.entries * HEAD_SIZE)(e, inverse, *grads)
    return results[0], results[1], results[2:]


def key_terms(z, e, inverse, qt, g, v_own, v_earlier):
    def body(e_ref, inverse_ref, qt_ref, g_ref, own_ref, *refs):
        earlier_refs, ds_ref = refs[: z.steps], refs[z.steps]
        dk_own, dk_earlier = refs[z.steps + 1], refs[z.steps + 2 : 2 * z.steps + 2]
        v_all, dk_all, dp_all = refs[2 * z.steps + 2 :]
        for head in range(z.heads):
            at = slice(head * HEAD_SIZE, (head + 1) * HEAD_SIZE)
            for number in range(z.total):
                v_all[number] = z.block(own_ref, earlier_refs, number)[:, at]
            dk_all[...] = jnp.zeros_like(dk_all)

            @pl.loop(0, z.group)
            def _(b):
                g = g_ref[head, b]
                inverse = inverse_ref[head, b]
                delta = jnp.zeros((1, z.wide), jnp.float32)
                for c in range(z.span):
                    dp = lax.dot_general(v_all[b + c], g, NN, preferred_element_type=jnp.float32)
                    delta = delta + jnp.sum(e_ref[head, b, c].astype(jnp.float32) * dp, axis=0, keepdims=True)
                    dp_all[c] = dp
                delta = delta * inverse
                q = (qt_ref[head, b].astype(jnp.float32) * inverse).astype(jnp.bfloat16)
                for c in range(z.span):
                    ds = e_ref[head, b, c] * (dp_all[c] - delta).astype(jnp.bfloat16)
                    ds_ref[head, b, c] = ds
                    dk_all[b + c] += lax.dot_general(ds, q, NT, preferred_element_type=jnp.float32)

            for number in range(z.total):
                part = dk_all[number] * score_scale
                z.block(dk_own, dk_earlier, number)[:, at] = part.astype(
                    dk_own.dtype if number >= z.back else jnp.bfloat16
                )

    outs = [jax.ShapeDtypeStruct(e.shape, jnp.bfloat16)]
    outs += [jax.ShapeDtypeStruct((z.group, z.tokens, z.kv_width), jnp.float32)]
    outs += [jax.ShapeDtypeStruct((z.group, z.tokens, z.kv_width), jnp.bfloat16)] * z.steps
    scratch = [
        pltpu.VMEM((z.total, z.tokens, HEAD_SIZE), jnp.bfloat16),
        pltpu.VMEM((z.total, z.tokens, HEAD_SIZE), jnp.float32),
        pltpu.VMEM((z.span, z.tokens, z.wide), jnp.float32),
    ]
    results = call(body, outs, scratch, flops=4 * z.entries * HEAD_SIZE)(
        e, inverse, qt, g, v_own, *v_earlier
    )
    return results[0], results[1], results[2:]


def query_terms(z, ds, inverse, k_own, k_earlier, dv_terms):
    def body(ds_ref, inverse_ref, own_ref, *refs):
        earlier_refs, term_refs = refs[: z.steps], refs[z.steps : 2 * z.steps + 1]
        out_refs = refs[2 * z.steps + 1 : 2 * z.steps + 1 + z.group]
        kt_all, dq_all = refs[2 * z.steps + 1 + z.group :]
        for head in range(z.heads):
            at = slice(head * HEAD_SIZE, (head + 1) * HEAD_SIZE)
            for number in range(z.total):
                kt_all[number] = z.block(own_ref, earlier_refs, number)[:, at].T

            @pl.loop(0, z.group)
            def _(b):
                dqt = jnp.zeros((HEAD_SIZE, z.wide), jnp.float32)
                for c in range(z.span):
                    dqt = dqt + lax.dot_general(
                        kt_all[b + c], ds_ref[head, b, c], NN, preferred_element_type=jnp.float32
                    )
                dqt = dqt * (inverse_ref[head, b] * score_scale)
                for j in range(z.per_head):
                    lower = (head * z.per_head + j) * HEAD_SIZE
                    dq_all[b, :, lower : lower + HEAD_SIZE] = (
                        dqt[:, j * z.tokens : (j + 1) * z.tokens].T.astype(jnp.bfloat16)
                    )

        for r in range(z.group):
            member = spot(z.group)[0] ^ r
            dv = term_refs[0][member]
            for term in term_refs[1:]:
                dv = dv + term[member].astype(jnp.float32)
            out_refs[r][:, : z.width] = dq_all[member]
            out_refs[r][:, z.width :] = dv.astype(jnp.bfloat16)

    outs = [jax.ShapeDtypeStruct((z.tokens, z.width + z.kv_width), jnp.bfloat16)] * z.group
    scratch = [
        pltpu.VMEM((z.total, HEAD_SIZE, z.tokens), jnp.bfloat16),
        pltpu.VMEM((z.group, z.tokens, z.width), jnp.bfloat16),
    ]
    return call(body, outs, scratch, flops=2 * z.entries * HEAD_SIZE)(
        ds, inverse, k_own, *k_earlier, *dv_terms
    )


def pack_terms(group, sums):
    tokens, width = sums[0][0].shape[1:]
    flat = [term for terms in sums for term in terms]

    def body(*refs):
        for r in range(group):
            member = spot(group)[0] ^ r
            number = 0
            for column, terms in enumerate(sums):
                total = refs[number][member].astype(jnp.float32)
                for term in refs[number + 1 : number + len(terms)]:
                    total = total + term[member].astype(jnp.float32)
                refs[len(flat) + r][:, column * width : (column + 1) * width] = total.astype(jnp.bfloat16)
                number += len(terms)

    outs = [jax.ShapeDtypeStruct((tokens, len(sums) * width), jnp.bfloat16)] * group
    return call(body, outs)(*flat)


def unpack(group, pieces, widths, before=()):
    tokens = pieces[0].shape[0]

    def body(*refs):
        out_refs = refs[group + len(before) :]
        for r in range(group):
            lower = 0
            for number, width in enumerate(widths):
                there = lanes(spot(group)[0] ^ r, width)
                out_refs[number][:, there] = refs[r][:, lower : lower + width]
                lower += width
        out_refs[-1][...] = jnp.zeros_like(out_refs[-1])

    outs = [jax.ShapeDtypeStruct((tokens, group * width), jnp.bfloat16) for width in widths]
    outs += [jax.ShapeDtypeStruct((8, 128), jnp.float32)]
    return call(body, outs, specs=[VMEM] * group + [ANY] * len(before))(*pieces, *before)


def local(layer_cotangent, out_weight, queries, keys, values):
    tokens = queries.shape[0]
    kv_heads = keys.shape[1] // HEAD_SIZE
    per_head = queries.shape[1] // keys.shape[1]
    count, tp_count = lax.axis_size("ctx"), lax.axis_size("tp")
    group = 1
    while (
        kv_heads % (2 * group) == 0
        and count % (2 * group) == 0
        and WINDOW_LENGTH % (2 * group * tokens) == 0
    ):
        group *= 2
    heads = kv_heads // group
    kv_width = heads * HEAD_SIZE
    back_groups = WINDOW_LENGTH // (group * tokens)
    def trade(sent):
        return [sent[0]] + [swapped(sent[r], "ctx", r) for r in range(1, group)]

    def returned(earlier):
        return [
            shifted(earlier[number], "ctx", -group * (back_groups - number)) for number in range(back_groups)
        ]

    z = Shape(group, back_groups, heads, per_head, tokens)
    key_sent = pack_heads(group, [keys], begin(), AHEAD)
    sent = pack_heads(group, [values, queries], key_sent[0], 0)
    if tp_count == 2:
        other = head_product(2, 1, out_weight, layer_cotangent, [sent[0]])
    else:
        other = head_product(1, 0, out_weight, layer_cotangent, [sent[0]])
    k_own = order_pieces(group, trade(key_sent), kv_width, other, AHEAD)
    if tp_count == 2:
        terms = [head_product(2, 0, out_weight, layer_cotangent, [other, k_own]), swapped(other, "tp", 1)]
    else:
        terms = [lax.psum_scatter(other, "tp", scatter_dimension=0, tiled=True)]
    pieces = trade(sent)
    v_own = order_pieces(group, pieces, kv_width, terms[0], 0)
    k_earlier, v_earlier = (
        [shifted(own, "ctx", group * step) for step in range(back_groups, 0, -1)] for own in (k_own, v_own)
    )
    qt = turn_queries(z, pieces)
    grads = trade(pack_grads(group, terms, k_own))
    e, inverse = softmax(z, k_own, k_earlier, qt)
    g, dv_own, dv_earlier = value_terms(z, e, inverse, grads)
    dv_terms = [dv_own] + returned(dv_earlier)
    ds, dk_own, dk_earlier = key_terms(z, e, inverse, qt, g, v_own, v_earlier)
    dk_terms = [dk_own] + returned(dk_earlier)
    pieces = trade(query_terms(z, ds, inverse, k_own, k_earlier, dv_terms))
    query_grads, value_gradients, done = unpack(group, pieces, [z.width, kv_width])
    key_gradients, _ = unpack(group, trade(pack_terms(group, [dk_terms])), [kv_width], [done])
    return (query_grads, key_gradients, value_gradients)


def solution(mesh):
    in_specs = (P("ctx", "tp"), P(None, "tp"), P("ctx", "tp"), P("ctx", "tp"), P("ctx", "tp"))
    out_specs = (P("ctx", "tp"), P("ctx", "tp"), P("ctx", "tp"))
    return jax.shard_map(local, mesh=mesh, in_specs=in_specs, out_specs=out_specs, check_vma=False)
```

```python
import functools

import jax
import jax.numpy as jnp
from jax import lax
from jax.experimental import pallas as pl
from jax.experimental.pallas import tpu as pltpu
from jax.sharding import PartitionSpec as P

HEAD_SIZE = 128
WINDOW_LENGTH = 1024
LOG2_E = 1.4426950408889634
AHEAD = 10**10

score_scale = 168.0 ** (-0.5)

VMEM = pl.BlockSpec(memory_space=pltpu.VMEM)
ANY = pl.BlockSpec(memory_space=pl.ANY)
SMEM = pl.BlockSpec(memory_space=pltpu.SMEM)
NT = (((1,), (1,)), ((), ()))
NN = (((1,), (0,)), ((), ()))


def shifted(value, axis, steps):
    count = lax.axis_size(axis)
    leading, last = (max(0, -steps), min(count, count - steps))
    return lax.ppermute(value, axis, [(source, source + steps) for source in range(leading, last)])


def swapped(value, axis, bits):
    count = lax.axis_size(axis)
    return lax.ppermute(value, axis, [(source, source ^ bits) for source in range(count)])


def call(body, outs, scratch=(), flops=0, exps=0, specs=None, vmem=32):
    def run(*args):
        moved = sum(a.size * a.dtype.itemsize for a in args)
        moved += sum(o.size * o.dtype.itemsize for o in outs)
        return pl.pallas_call(
            body,
            out_shape=tuple(outs),
            in_specs=specs or [SMEM if a.dtype == jnp.int32 else VMEM for a in args],
            out_specs=tuple(VMEM for _ in outs),
            scratch_shapes=list(scratch),
            compiler_params=pltpu.CompilerParams(vmem_limit_bytes=vmem * 1024 * 1024),
            cost_estimate=pl.CostEstimate(flops=flops, bytes_accessed=moved, transcendentals=exps),
        )(*args)

    return run


def spot(group):
    index = lax.axis_index("ctx")
    place = lax.rem(index, group)
    return place, index - place


def lanes(index, width):
    return pl.ds(pl.multiple_of(index * width, width), width)


def begin():
    def body(out_ref):
        out_ref[...] = jnp.zeros_like(out_ref)

    return call(body, [jax.ShapeDtypeStruct((8, 128), jnp.float32)], flops=AHEAD)()[0]


def pack_kv(group, keys, values, before):
    tokens, width = keys.shape[0], keys.shape[1] // group

    def body(k_ref, v_ref, before_ref, *refs):
        for r in range(group):
            member = spot(group)[0] ^ r
            refs[r][:, :width] = k_ref[:, lanes(member, width)]
            refs[r][:, width:] = v_ref[:, lanes(member, width)]

    outs = [jax.ShapeDtypeStruct((tokens, 2 * width), jnp.bfloat16)] * group
    return call(body, outs, flops=AHEAD, specs=[VMEM, VMEM, ANY])(keys, values, before)


def pack_queries(group, queries, before):
    tokens, width = queries.shape[0], queries.shape[1] // group

    def body(q_ref, before_ref, *out_refs):
        for r in range(group):
            out_refs[r][...] = q_ref[:, lanes(spot(group)[0] ^ r, width)]

    outs = [jax.ShapeDtypeStruct((tokens, width), jnp.bfloat16)] * group
    return call(body, outs, specs=[VMEM, ANY])(queries, before)


def order_pieces(group, pieces, before):
    def body(*refs):
        for r in range(group):
            refs[-1][spot(group)[0] ^ r] = refs[r][...]

    outs = [jax.ShapeDtypeStruct((group,) + pieces[0].shape, jnp.bfloat16)]
    return call(body, outs, specs=[VMEM] * group + [ANY])(*pieces, before)[0]


def head_product(parts, part, out_weight, layer_cotangent, before):
    tokens, depth = layer_cotangent.shape
    rows = out_weight.shape[0] // parts
    tile = min(rows, 512)

    def body(w_ref, c_ref, *refs):
        first = (lax.axis_index("tp") ^ part) * rows if parts > 1 else 0

        @pl.loop(0, rows // tile)
        def _(i):
            here = pl.ds(pl.multiple_of(i * tile, tile), tile)
            there = pl.ds(pl.multiple_of(first + i * tile, tile), tile)
            refs[-1][here, :] = lax.dot_general(
                w_ref[there, :], c_ref[...], NT, preferred_element_type=jnp.float32
            ).astype(jnp.bfloat16)

    outs = [jax.ShapeDtypeStruct((rows, tokens), jnp.bfloat16)]
    specs = [VMEM, VMEM] + [ANY] * len(before)
    return call(body, outs, flops=2 * rows * tokens * depth, specs=specs, vmem=16)(
        out_weight, layer_cotangent, *before
    )[0]


def pack_grads(group, terms, before):
    rows, tokens = terms[0].shape
    rows //= group

    def body(*refs):
        for r in range(group):
            there = lanes(spot(group)[0] ^ r, rows)
            total = refs[0][there, :]
            if len(terms) > 1:
                total = total.astype(jnp.float32)
                for term in refs[1 : len(terms)]:
                    total = total + term[there, :].astype(jnp.float32)
            refs[len(terms) + 1 + r][...] = total.astype(jnp.bfloat16)

    outs = [jax.ShapeDtypeStruct((rows, tokens), jnp.bfloat16)] * group
    return call(body, outs, specs=[VMEM] * len(terms) + [ANY])(*terms, before)


class Shape:
    def __init__(self, group, steps, heads, per_head, tokens):
        self.group, self.steps, self.heads, self.per_head, self.tokens = group, steps, heads, per_head, tokens
        self.back = steps * group
        self.span = self.back + 1
        self.total = self.back + group
        self.wide = per_head * tokens
        self.width = heads * per_head * HEAD_SIZE
        self.kv_width = heads * HEAD_SIZE
        self.entries = group * heads * self.wide * self.span * tokens

    def block(self, own_ref, earlier_refs, number):
        if number < self.back:
            return earlier_refs[number // self.group].at[number % self.group]
        return own_ref.at[number - self.back]


def turn_queries(z, pieces):
    def body(*refs):
        for head in range(z.heads):
            for r in range(z.group):
                for j in range(z.per_head):
                    lower = (head * z.per_head + j) * HEAD_SIZE
                    refs[z.group][head, spot(z.group)[0] ^ r, :, j * z.tokens : (j + 1) * z.tokens] = refs[r][
                        :, lower : lower + HEAD_SIZE
                    ].T

    outs = [jax.ShapeDtypeStruct((z.heads, z.group, HEAD_SIZE, z.wide), jnp.bfloat16)]
    return call(body, outs)(*pieces)[0]


def softmax(z, kv_own, kv_earlier, qt):
    factor = score_scale * LOG2_E

    def body(*refs):
        own_ref, earlier_refs = refs[0], refs[1 : 1 + z.steps]
        qt_ref, e_ref, inverse_ref, k_all, s_all = refs[1 + z.steps :]
        first = spot(z.group)[1]
        key_id = lax.broadcasted_iota(jnp.int32, (z.tokens, z.wide), 0)
        query_id = lax.broadcasted_iota(jnp.int32, (z.tokens, z.wide), 1) & (z.tokens - 1)
        for head in range(z.heads):
            at_k = slice(head * HEAD_SIZE, (head + 1) * HEAD_SIZE)
            for number in range(z.total):
                k_all[number] = z.block(own_ref, earlier_refs, number)[:, at_k]

            @pl.loop(0, z.group)
            def _(b):
                qt = qt_ref[head, b]
                last = lax.dot_general(k_all[b + z.back], qt, NN, preferred_element_type=jnp.float32)
                top = None
                for c in range(z.back):
                    s = lax.dot_general(k_all[b + c], qt, NN, preferred_element_type=jnp.float32)
                    there = first + b + c >= z.back
                    if c == 0:
                        s = jnp.where(key_id > query_id, s + jnp.where(there, 0.0, -jnp.inf), last)
                    s_all[c] = s
                    here = jnp.max(s, axis=0, keepdims=True)
                    if c > 0:
                        here = jnp.where(there, here, -jnp.inf)
                    top = here if top is None else jnp.maximum(top, here)
                norm = jnp.zeros((1, z.wide), jnp.float32)
                for c in range(z.back):
                    base = top
                    if c > 0:
                        base = jnp.where(first + b + c >= z.back, top, jnp.inf)
                    e = jnp.exp2((s_all[c] - base) * factor)
                    norm = norm + jnp.sum(e, axis=0, keepdims=True)
                    if c == 0:
                        e_ref[head, b, 0] = jnp.where(key_id > query_id, e, 0.0).astype(jnp.bfloat16)
                        e_ref[head, b, z.back] = jnp.where(key_id > query_id, 0.0, e).astype(jnp.bfloat16)
                    else:
                        e_ref[head, b, c] = e.astype(jnp.bfloat16)
                inverse_ref[head, b] = 1.0 / norm

    outs = [
        jax.ShapeDtypeStruct((z.heads, z.group, z.span, z.tokens, z.wide), jnp.bfloat16),
        jax.ShapeDtypeStruct((z.heads, z.group, 1, z.wide), jnp.float32),
    ]
    scratch = [
        pltpu.VMEM((z.total, z.tokens, HEAD_SIZE), jnp.bfloat16),
        pltpu.VMEM((z.span, z.tokens, z.wide), jnp.float32),
    ]
    return call(body, outs, scratch, flops=2 * z.entries * HEAD_SIZE, exps=z.entries)(
        kv_own, *kv_earlier, qt
    )


def value_terms(z, e, inverse, grads):
    def body(e_ref, inverse_ref, *refs):
        g_refs, (g_ref, own_ref), earlier_refs = (
            refs[: z.group],
            refs[z.group : z.group + 2],
            refs[z.group + 2 : z.group + 2 + z.steps],
        )
        dv_all = refs[-1]
        place = spot(z.group)[0]
        for head in range(z.heads):
            at = slice(head * HEAD_SIZE, (head + 1) * HEAD_SIZE)
            for r in range(z.group):
                for j in range(z.per_head):
                    lower = (head * z.per_head + j) * HEAD_SIZE
                    g_ref[head, place ^ r, :, j * z.tokens : (j + 1) * z.tokens] = g_refs[r][
                        lower : lower + HEAD_SIZE, :
                    ]
            dv_all[...] = jnp.zeros_like(dv_all)

            @pl.loop(0, z.group)
            def _(b):
                g = (g_ref[head, b].astype(jnp.float32) * inverse_ref[head, b]).astype(jnp.bfloat16)
                for c in range(z.span):
                    dv_all[b + c] += lax.dot_general(
                        e_ref[head, b, c], g, NT, preferred_element_type=jnp.float32
                    )

            for number in range(z.total):
                part = dv_all[number]
                z.block(own_ref, earlier_refs, number)[:, at] = part.astype(own_ref.dtype if number >= z.back else jnp.bfloat16)

    outs = [
        jax.ShapeDtypeStruct((z.heads, z.group, HEAD_SIZE, z.wide), jnp.bfloat16),
        jax.ShapeDtypeStruct((z.group, z.tokens, z.kv_width), jnp.float32),
    ]
    outs += [jax.ShapeDtypeStruct((z.group, z.tokens, z.kv_width), jnp.bfloat16)] * z.steps
    scratch = [pltpu.VMEM((z.total, z.tokens, HEAD_SIZE), jnp.float32)]
    results = call(body, outs, scratch, flops=2 * z.entries * HEAD_SIZE)(e, inverse, *grads)
    return results[0], results[1], results[2:]


def key_terms(z, e, inverse, qt, g, kv_own, kv_earlier):
    def body(e_ref, inverse_ref, qt_ref, g_ref, own_ref, *refs):
        earlier_refs, ds_ref = refs[: z.steps], refs[z.steps]
        dk_own, dk_earlier = refs[z.steps + 1], refs[z.steps + 2 : 2 * z.steps + 2]
        v_all, dk_all, dp_all = refs[2 * z.steps + 2 :]
        for head in range(z.heads):
            at = slice(head * HEAD_SIZE, (head + 1) * HEAD_SIZE)
            at_v = slice(z.kv_width + head * HEAD_SIZE, z.kv_width + (head + 1) * HEAD_SIZE)
            for number in range(z.total):
                v_all[number] = z.block(own_ref, earlier_refs, number)[:, at_v]
            dk_all[...] = jnp.zeros_like(dk_all)

            @pl.loop(0, z.group)
            def _(b):
                g = g_ref[head, b]
                inverse = inverse_ref[head, b]
                delta = jnp.zeros((1, z.wide), jnp.float32)
                for c in range(z.span):
                    dp = lax.dot_general(v_all[b + c], g, NN, preferred_element_type=jnp.float32)
                    delta = delta + jnp.sum(e_ref[head, b, c].astype(jnp.float32) * dp, axis=0, keepdims=True)
                    dp_all[c] = dp
                delta = delta * inverse
                q = (qt_ref[head, b].astype(jnp.float32) * inverse).astype(jnp.bfloat16)
                for c in range(z.span):
                    ds = e_ref[head, b, c] * (dp_all[c] - delta).astype(jnp.bfloat16)
                    ds_ref[head, b, c] = ds
                    dk_all[b + c] += lax.dot_general(ds, q, NT, preferred_element_type=jnp.float32)

            for number in range(z.total):
                part = dk_all[number] * score_scale
                z.block(dk_own, dk_earlier, number)[:, at] = part.astype(
                    dk_own.dtype if number >= z.back else jnp.bfloat16
                )

    outs = [jax.ShapeDtypeStruct(e.shape, jnp.bfloat16)]
    outs += [jax.ShapeDtypeStruct((z.group, z.tokens, z.kv_width), jnp.float32)]
    outs += [jax.ShapeDtypeStruct((z.group, z.tokens, z.kv_width), jnp.bfloat16)] * z.steps
    scratch = [
        pltpu.VMEM((z.total, z.tokens, HEAD_SIZE), jnp.bfloat16),
        pltpu.VMEM((z.total, z.tokens, HEAD_SIZE), jnp.float32),
        pltpu.VMEM((z.span, z.tokens, z.wide), jnp.float32),
    ]
    results = call(body, outs, scratch, flops=4 * z.entries * HEAD_SIZE)(
        e, inverse, qt, g, kv_own, *kv_earlier
    )
    return results[0], results[1], results[2:]


def query_terms(z, ds, inverse, kv_own, kv_earlier, dv_terms):
    def body(ds_ref, inverse_ref, own_ref, *refs):
        earlier_refs, term_refs = refs[: z.steps], refs[z.steps : 2 * z.steps + 1]
        out_refs = refs[2 * z.steps + 1 : 2 * z.steps + 1 + z.group]
        kt_all, dq_all = refs[2 * z.steps + 1 + z.group :]
        for head in range(z.heads):
            at = slice(head * HEAD_SIZE, (head + 1) * HEAD_SIZE)
            for number in range(z.total):
                kt_all[number] = z.block(own_ref, earlier_refs, number)[:, at].T

            @pl.loop(0, z.group)
            def _(b):
                dqt = jnp.zeros((HEAD_SIZE, z.wide), jnp.float32)
                for c in range(z.span):
                    dqt = dqt + lax.dot_general(
                        kt_all[b + c], ds_ref[head, b, c], NN, preferred_element_type=jnp.float32
                    )
                dqt = dqt * (inverse_ref[head, b] * score_scale)
                for j in range(z.per_head):
                    lower = (head * z.per_head + j) * HEAD_SIZE
                    dq_all[b, :, lower : lower + HEAD_SIZE] = (
                        dqt[:, j * z.tokens : (j + 1) * z.tokens].T.astype(jnp.bfloat16)
                    )

        for r in range(z.group):
            member = spot(z.group)[0] ^ r
            dv = term_refs[0][member]
            for term in term_refs[1:]:
                dv = dv + term[member].astype(jnp.float32)
            out_refs[r][:, : z.width] = dq_all[member]
            out_refs[r][:, z.width :] = dv.astype(jnp.bfloat16)

    outs = [jax.ShapeDtypeStruct((z.tokens, z.width + z.kv_width), jnp.bfloat16)] * z.group
    scratch = [
        pltpu.VMEM((z.total, HEAD_SIZE, z.tokens), jnp.bfloat16),
        pltpu.VMEM((z.group, z.tokens, z.width), jnp.bfloat16),
    ]
    return call(body, outs, scratch, flops=2 * z.entries * HEAD_SIZE)(
        ds, inverse, kv_own, *kv_earlier, *dv_terms
    )


def pack_terms(group, sums):
    tokens, width = sums[0][0].shape[1:]
    flat = [term for terms in sums for term in terms]

    def body(*refs):
        for r in range(group):
            member = spot(group)[0] ^ r
            number = 0
            for column, terms in enumerate(sums):
                total = refs[number][member].astype(jnp.float32)
                for term in refs[number + 1 : number + len(terms)]:
                    total = total + term[member].astype(jnp.float32)
                refs[len(flat) + r][:, column * width : (column + 1) * width] = total.astype(jnp.bfloat16)
                number += len(terms)

    outs = [jax.ShapeDtypeStruct((tokens, len(sums) * width), jnp.bfloat16)] * group
    return call(body, outs)(*flat)


def unpack(group, pieces, widths, before=()):
    tokens = pieces[0].shape[0]

    def body(*refs):
        out_refs = refs[group + len(before) :]
        for r in range(group):
            lower = 0
            for number, width in enumerate(widths):
                there = lanes(spot(group)[0] ^ r, width)
                out_refs[number][:, there] = refs[r][:, lower : lower + width]
                lower += width
        out_refs[-1][...] = jnp.zeros_like(out_refs[-1])

    outs = [jax.ShapeDtypeStruct((tokens, group * width), jnp.bfloat16) for width in widths]
    outs += [jax.ShapeDtypeStruct((8, 128), jnp.float32)]
    return call(body, outs, specs=[VMEM] * group + [ANY] * len(before))(*pieces, *before)


def local(layer_cotangent, out_weight, queries, keys, values):
    tokens = queries.shape[0]
    kv_heads = keys.shape[1] // HEAD_SIZE
    per_head = queries.shape[1] // keys.shape[1]
    count, tp_count = lax.axis_size("ctx"), lax.axis_size("tp")
    group = 1
    while (
        kv_heads % (2 * group) == 0
        and count % (2 * group) == 0
        and WINDOW_LENGTH % (2 * group * tokens) == 0
    ):
        group *= 2
    heads = kv_heads // group
    kv_width = heads * HEAD_SIZE
    back_groups = WINDOW_LENGTH // (group * tokens)

    def trade(sent):
        return [sent[0]] + [swapped(sent[r], "ctx", r) for r in range(1, group)]

    def returned(earlier):
        return [
            shifted(earlier[number], "ctx", -group * (back_groups - number)) for number in range(back_groups)
        ]

    sent = pack_kv(group, keys, values, begin())
    kv_pieces = trade(sent)
    z = Shape(group, back_groups, heads, per_head, tokens)
    query_sent = pack_queries(group, queries, sent[0])
    if tp_count == 2:
        other = head_product(2, 1, out_weight, layer_cotangent, [query_sent[0]])
    else:
        other = head_product(1, 0, out_weight, layer_cotangent, [query_sent[0]])
    kv_own = order_pieces(group, kv_pieces, other)
    kv_earlier = [shifted(kv_own, "ctx", group * step) for step in range(back_groups, 0, -1)]
    if tp_count == 2:
        terms = [head_product(2, 0, out_weight, layer_cotangent, [kv_own, other]), swapped(other, "tp", 1)]
    else:
        terms = [lax.psum_scatter(other, "tp", scatter_dimension=0, tiled=True)]
    qt = turn_queries(z, trade(query_sent))
    grads = trade(pack_grads(group, terms, kv_own))
    e, inverse = softmax(z, kv_own, kv_earlier, qt)
    g, dv_own, dv_earlier = value_terms(z, e, inverse, grads)
    dv_terms = [dv_own] + returned(dv_earlier)
    ds, dk_own, dk_earlier = key_terms(z, e, inverse, qt, g, kv_own, kv_earlier)
    dk_terms = [dk_own] + returned(dk_earlier)
    pieces = trade(query_terms(z, ds, inverse, kv_own, kv_earlier, dv_terms))
    query_grads, value_gradients, done = unpack(group, pieces, [z.width, kv_width])
    key_gradients, _ = unpack(group, trade(pack_terms(group, [dk_terms])), [kv_width], [done])
    return (query_grads, key_gradients, value_gradients)


def solution(mesh):
    in_specs = (P("ctx", "tp"), P(None, "tp"), P("ctx", "tp"), P("ctx", "tp"), P("ctx", "tp"))
    out_specs = (P("ctx", "tp"), P("ctx", "tp"), P("ctx", "tp"))
    return jax.shard_map(local, mesh=mesh, in_specs=in_specs, out_specs=out_specs, check_vma=False)
```

```python
import functools

import jax
import jax.numpy as jnp
from jax import lax
from jax.experimental import pallas as pl
from jax.experimental.pallas import tpu as pltpu
from jax.sharding import PartitionSpec as P

HEAD_SIZE = 128
WINDOW_LENGTH = 1024
LOG2_E = 1.4426950408889634
AHEAD = 10**10

score_scale = 168.0 ** (-0.5)

VMEM = pl.BlockSpec(memory_space=pltpu.VMEM)
ANY = pl.BlockSpec(memory_space=pl.ANY)
SMEM = pl.BlockSpec(memory_space=pltpu.SMEM)
NT = (((1,), (1,)), ((), ()))
NN = (((1,), (0,)), ((), ()))


def shifted(value, axis, steps):
    count = lax.axis_size(axis)
    leading, last = (max(0, -steps), min(count, count - steps))
    return lax.ppermute(value, axis, [(source, source + steps) for source in range(leading, last)])


def swapped(value, axis, bits):
    count = lax.axis_size(axis)
    return lax.ppermute(value, axis, [(source, source ^ bits) for source in range(count)])


def call(body, outs, scratch=(), flops=0, exps=0, specs=None, vmem=32):
    def run(*args):
        moved = sum(a.size * a.dtype.itemsize for a in args)
        moved += sum(o.size * o.dtype.itemsize for o in outs)
        return pl.pallas_call(
            body,
            out_shape=tuple(outs),
            in_specs=specs or [SMEM if a.dtype == jnp.int32 else VMEM for a in args],
            out_specs=tuple(VMEM for _ in outs),
            scratch_shapes=list(scratch),
            compiler_params=pltpu.CompilerParams(vmem_limit_bytes=vmem * 1024 * 1024),
            cost_estimate=pl.CostEstimate(flops=flops, bytes_accessed=moved, transcendentals=exps),
        )(*args)

    return run


def spot(group):
    index = lax.axis_index("ctx")
    place = lax.rem(index, group)
    return place, index - place


def lanes(index, width):
    return pl.ds(pl.multiple_of(index * width, width), width)


def begin():
    def body(out_ref):
        out_ref[...] = jnp.zeros_like(out_ref)

    return call(body, [jax.ShapeDtypeStruct((8, 128), jnp.float32)], flops=AHEAD)()[0]


def pack_kv(group, keys, values, before):
    tokens, width = keys.shape[0], keys.shape[1] // group

    def body(k_ref, v_ref, before_ref, *refs):
        for r in range(group):
            member = spot(group)[0] ^ r
            refs[r][:, :width] = k_ref[:, lanes(member, width)]
            refs[r][:, width:] = v_ref[:, lanes(member, width)]

    outs = [jax.ShapeDtypeStruct((tokens, 2 * width), jnp.bfloat16)] * group
    return call(body, outs, flops=AHEAD, specs=[VMEM, VMEM, ANY])(keys, values, before)


def pack_queries(group, queries, before):
    tokens, width = queries.shape[0], queries.shape[1] // group

    def body(q_ref, before_ref, *out_refs):
        for r in range(group):
            out_refs[r][...] = q_ref[:, lanes(spot(group)[0] ^ r, width)]

    outs = [jax.ShapeDtypeStruct((tokens, width), jnp.bfloat16)] * group
    return call(body, outs, specs=[VMEM, ANY])(queries, before)


def order_pieces(group, pieces, before):
    def body(*refs):
        for r in range(group):
            refs[-1][spot(group)[0] ^ r] = refs[r][...]

    outs = [jax.ShapeDtypeStruct((group,) + pieces[0].shape, jnp.bfloat16)]
    return call(body, outs, specs=[VMEM] * group + [ANY])(*pieces, before)[0]


def head_product(parts, part, out_weight, layer_cotangent, before):
    tokens, depth = layer_cotangent.shape
    rows = out_weight.shape[0] // parts
    tile = min(rows, 1024)

    def body(w_ref, c_ref, *refs):
        first = (lax.axis_index("tp") ^ part) * rows if parts > 1 else 0

        @pl.loop(0, rows // tile)
        def _(i):
            here = pl.ds(pl.multiple_of(i * tile, tile), tile)
            there = pl.ds(pl.multiple_of(first + i * tile, tile), tile)
            refs[-1][here, :] = lax.dot_general(
                w_ref[there, :], c_ref[...], NT, preferred_element_type=jnp.float32
            ).astype(jnp.bfloat16)

    outs = [jax.ShapeDtypeStruct((rows, tokens), jnp.bfloat16)]
    specs = [VMEM, VMEM] + [ANY] * len(before)
    return call(body, outs, flops=2 * rows * tokens * depth, specs=specs, vmem=16)(
        out_weight, layer_cotangent, *before
    )[0]


def pack_grads(group, terms, before):
    rows, tokens = terms[0].shape
    rows //= group

    def body(*refs):
        for r in range(group):
            there = lanes(spot(group)[0] ^ r, rows)
            total = refs[0][there, :]
            if len(terms) > 1:
                total = total.astype(jnp.float32)
                for term in refs[1 : len(terms)]:
                    total = total + term[there, :].astype(jnp.float32)
            refs[len(terms) + 1 + r][...] = total.astype(jnp.bfloat16)

    outs = [jax.ShapeDtypeStruct((rows, tokens), jnp.bfloat16)] * group
    return call(body, outs, specs=[VMEM] * len(terms) + [ANY])(*terms, before)


class Shape:
    def __init__(self, group, steps, heads, per_head, tokens):
        self.group, self.steps, self.heads, self.per_head, self.tokens = group, steps, heads, per_head, tokens
        self.back = steps * group
        self.span = self.back + 1
        self.total = self.back + group
        self.wide = per_head * tokens
        self.width = heads * per_head * HEAD_SIZE
        self.kv_width = heads * HEAD_SIZE
        self.entries = group * heads * self.wide * self.span * tokens

    def block(self, own_ref, earlier_refs, number):
        if number < self.back:
            return earlier_refs[number // self.group].at[number % self.group]
        return own_ref.at[number - self.back]


def turn_queries(z, pieces):
    def body(*refs):
        for head in range(z.heads):
            for r in range(z.group):
                for j in range(z.per_head):
                    lower = (head * z.per_head + j) * HEAD_SIZE
                    refs[z.group][head, spot(z.group)[0] ^ r, :, j * z.tokens : (j + 1) * z.tokens] = refs[r][
                        :, lower : lower + HEAD_SIZE
                    ].T

    outs = [jax.ShapeDtypeStruct((z.heads, z.group, HEAD_SIZE, z.wide), jnp.bfloat16)]
    return call(body, outs)(*pieces)[0]


def softmax(z, kv_own, kv_earlier, qt):
    factor = score_scale * LOG2_E

    def body(*refs):
        own_ref, earlier_refs = refs[0], refs[1 : 1 + z.steps]
        qt_ref, e_ref, inverse_ref, k_all, s_all = refs[1 + z.steps :]
        first = spot(z.group)[1]
        key_id = lax.broadcasted_iota(jnp.int32, (z.tokens, z.wide), 0)
        query_id = lax.broadcasted_iota(jnp.int32, (z.tokens, z.wide), 1) & (z.tokens - 1)
        for head in range(z.heads):
            at_k = slice(head * HEAD_SIZE, (head + 1) * HEAD_SIZE)
            for number in range(z.total):
                k_all[number] = z.block(own_ref, earlier_refs, number)[:, at_k]

            @pl.loop(0, z.group)
            def _(b):
                qt = qt_ref[head, b]
                top = None
                for c in range(z.span):
                    s = lax.dot_general(k_all[b + c], qt, NN, preferred_element_type=jnp.float32)
                    if c == 0:
                        s = jnp.where(key_id > query_id, s, -jnp.inf)
                    if c == z.back:
                        s = jnp.where(key_id <= query_id, s, -jnp.inf)
                    s_all[c] = s
                    here = jnp.max(s, axis=0, keepdims=True)
                    if c < z.back:
                        here = jnp.where(first + b + c >= z.back, here, -jnp.inf)
                    top = here if top is None else jnp.maximum(top, here)
                norm = jnp.zeros((1, z.wide), jnp.float32)
                for c in range(z.span):
                    base = top
                    if c < z.back:
                        base = jnp.where(first + b + c >= z.back, top, jnp.inf)
                    e = jnp.exp2((s_all[c] - base) * factor)
                    norm = norm + jnp.sum(e, axis=0, keepdims=True)
                    e_ref[head, b, c] = e.astype(jnp.bfloat16)
                inverse_ref[head, b] = 1.0 / norm

    outs = [
        jax.ShapeDtypeStruct((z.heads, z.group, z.span, z.tokens, z.wide), jnp.bfloat16),
        jax.ShapeDtypeStruct((z.heads, z.group, 1, z.wide), jnp.float32),
    ]
    scratch = [
        pltpu.VMEM((z.total, z.tokens, HEAD_SIZE), jnp.bfloat16),
        pltpu.VMEM((z.span, z.tokens, z.wide), jnp.float32),
    ]
    return call(body, outs, scratch, flops=2 * z.entries * HEAD_SIZE, exps=z.entries)(
        kv_own, *kv_earlier, qt
    )


def value_terms(z, e, inverse, grads):
    def body(e_ref, inverse_ref, *refs):
        g_refs, (g_ref, own_ref), earlier_refs = (
            refs[: z.group],
            refs[z.group : z.group + 2],
            refs[z.group + 2 : z.group + 2 + z.steps],
        )
        dv_all = refs[-1]
        place = spot(z.group)[0]
        for head in range(z.heads):
            at = slice(head * HEAD_SIZE, (head + 1) * HEAD_SIZE)
            for r in range(z.group):
                for j in range(z.per_head):
                    lower = (head * z.per_head + j) * HEAD_SIZE
                    g_ref[head, place ^ r, :, j * z.tokens : (j + 1) * z.tokens] = g_refs[r][
                        lower : lower + HEAD_SIZE, :
                    ]
            dv_all[...] = jnp.zeros_like(dv_all)

            @pl.loop(0, z.group)
            def _(b):
                g = (g_ref[head, b].astype(jnp.float32) * inverse_ref[head, b]).astype(jnp.bfloat16)
                for c in range(z.span):
                    dv_all[b + c] += lax.dot_general(
                        e_ref[head, b, c], g, NT, preferred_element_type=jnp.float32
                    )

            for number in range(z.total):
                part = dv_all[number]
                z.block(own_ref, earlier_refs, number)[:, at] = part.astype(own_ref.dtype if number >= z.back else jnp.bfloat16)

    outs = [
        jax.ShapeDtypeStruct((z.heads, z.group, HEAD_SIZE, z.wide), jnp.bfloat16),
        jax.ShapeDtypeStruct((z.group, z.tokens, z.kv_width), jnp.float32),
    ]
    outs += [jax.ShapeDtypeStruct((z.group, z.tokens, z.kv_width), jnp.bfloat16)] * z.steps
    scratch = [pltpu.VMEM((z.total, z.tokens, HEAD_SIZE), jnp.float32)]
    results = call(body, outs, scratch, flops=2 * z.entries * HEAD_SIZE)(e, inverse, *grads)
    return results[0], results[1], results[2:]


def key_terms(z, e, inverse, qt, g, kv_own, kv_earlier):
    def body(e_ref, inverse_ref, qt_ref, g_ref, own_ref, *refs):
        earlier_refs, ds_ref = refs[: z.steps], refs[z.steps]
        dk_own, dk_earlier = refs[z.steps + 1], refs[z.steps + 2 : 2 * z.steps + 2]
        v_all, dk_all, dp_all = refs[2 * z.steps + 2 :]
        for head in range(z.heads):
            at = slice(head * HEAD_SIZE, (head + 1) * HEAD_SIZE)
            at_v = slice(z.kv_width + head * HEAD_SIZE, z.kv_width + (head + 1) * HEAD_SIZE)
            for number in range(z.total):
                v_all[number] = z.block(own_ref, earlier_refs, number)[:, at_v]
            dk_all[...] = jnp.zeros_like(dk_all)

            @pl.loop(0, z.group)
            def _(b):
                g = g_ref[head, b]
                inverse = inverse_ref[head, b]
                delta = jnp.zeros((1, z.wide), jnp.float32)
                for c in range(z.span):
                    dp = lax.dot_general(v_all[b + c], g, NN, preferred_element_type=jnp.float32)
                    delta = delta + jnp.sum(e_ref[head, b, c].astype(jnp.float32) * dp, axis=0, keepdims=True)
                    dp_all[c] = dp
                delta = delta * inverse
                q = (qt_ref[head, b].astype(jnp.float32) * inverse).astype(jnp.bfloat16)
                for c in range(z.span):
                    ds = e_ref[head, b, c] * (dp_all[c] - delta).astype(jnp.bfloat16)
                    ds_ref[head, b, c] = ds
                    dk_all[b + c] += lax.dot_general(ds, q, NT, preferred_element_type=jnp.float32)

            for number in range(z.total):
                part = dk_all[number] * score_scale
                z.block(dk_own, dk_earlier, number)[:, at] = part.astype(
                    dk_own.dtype if number >= z.back else jnp.bfloat16
                )

    outs = [jax.ShapeDtypeStruct(e.shape, jnp.bfloat16)]
    outs += [jax.ShapeDtypeStruct((z.group, z.tokens, z.kv_width), jnp.float32)]
    outs += [jax.ShapeDtypeStruct((z.group, z.tokens, z.kv_width), jnp.bfloat16)] * z.steps
    scratch = [
        pltpu.VMEM((z.total, z.tokens, HEAD_SIZE), jnp.bfloat16),
        pltpu.VMEM((z.total, z.tokens, HEAD_SIZE), jnp.float32),
        pltpu.VMEM((z.span, z.tokens, z.wide), jnp.float32),
    ]
    results = call(body, outs, scratch, flops=4 * z.entries * HEAD_SIZE)(
        e, inverse, qt, g, kv_own, *kv_earlier
    )
    return results[0], results[1], results[2:]


def query_terms(z, ds, inverse, kv_own, kv_earlier, dv_terms):
    def body(ds_ref, inverse_ref, own_ref, *refs):
        earlier_refs, term_refs = refs[: z.steps], refs[z.steps : 2 * z.steps + 1]
        out_refs = refs[2 * z.steps + 1 : 2 * z.steps + 1 + z.group]
        kt_all, dq_all = refs[2 * z.steps + 1 + z.group :]
        for head in range(z.heads):
            at = slice(head * HEAD_SIZE, (head + 1) * HEAD_SIZE)
            for number in range(z.total):
                kt_all[number] = z.block(own_ref, earlier_refs, number)[:, at].T

            @pl.loop(0, z.group)
            def _(b):
                dqt = jnp.zeros((HEAD_SIZE, z.wide), jnp.float32)
                for c in range(z.span):
                    dqt = dqt + lax.dot_general(
                        kt_all[b + c], ds_ref[head, b, c], NN, preferred_element_type=jnp.float32
                    )
                dqt = dqt * (inverse_ref[head, b] * score_scale)
                for j in range(z.per_head):
                    lower = (head * z.per_head + j) * HEAD_SIZE
                    dq_all[b, :, lower : lower + HEAD_SIZE] = (
                        dqt[:, j * z.tokens : (j + 1) * z.tokens].T.astype(jnp.bfloat16)
                    )

        for r in range(z.group):
            member = spot(z.group)[0] ^ r
            dv = term_refs[0][member]
            for term in term_refs[1:]:
                dv = dv + term[member].astype(jnp.float32)
            out_refs[r][:, : z.width] = dq_all[member]
            out_refs[r][:, z.width :] = dv.astype(jnp.bfloat16)

    outs = [jax.ShapeDtypeStruct((z.tokens, z.width + z.kv_width), jnp.bfloat16)] * z.group
    scratch = [
        pltpu.VMEM((z.total, HEAD_SIZE, z.tokens), jnp.bfloat16),
        pltpu.VMEM((z.group, z.tokens, z.width), jnp.bfloat16),
    ]
    return call(body, outs, scratch, flops=2 * z.entries * HEAD_SIZE)(
        ds, inverse, kv_own, *kv_earlier, *dv_terms
    )


def pack_terms(group, sums):
    tokens, width = sums[0][0].shape[1:]
    flat = [term for terms in sums for term in terms]

    def body(*refs):
        for r in range(group):
            member = spot(group)[0] ^ r
            number = 0
            for column, terms in enumerate(sums):
                total = refs[number][member].astype(jnp.float32)
                for term in refs[number + 1 : number + len(terms)]:
                    total = total + term[member].astype(jnp.float32)
                refs[len(flat) + r][:, column * width : (column + 1) * width] = total.astype(jnp.bfloat16)
                number += len(terms)

    outs = [jax.ShapeDtypeStruct((tokens, len(sums) * width), jnp.bfloat16)] * group
    return call(body, outs)(*flat)


def unpack(group, pieces, widths, before=()):
    tokens = pieces[0].shape[0]

    def body(*refs):
        out_refs = refs[group + len(before) :]
        for r in range(group):
            lower = 0
            for number, width in enumerate(widths):
                there = lanes(spot(group)[0] ^ r, width)
                out_refs[number][:, there] = refs[r][:, lower : lower + width]
                lower += width
        out_refs[-1][...] = jnp.zeros_like(out_refs[-1])

    outs = [jax.ShapeDtypeStruct((tokens, group * width), jnp.bfloat16) for width in widths]
    outs += [jax.ShapeDtypeStruct((8, 128), jnp.float32)]
    return call(body, outs, specs=[VMEM] * group + [ANY] * len(before))(*pieces, *before)


def local(layer_cotangent, out_weight, queries, keys, values):
    tokens = queries.shape[0]
    kv_heads = keys.shape[1] // HEAD_SIZE
    per_head = queries.shape[1] // keys.shape[1]
    count, tp_count = lax.axis_size("ctx"), lax.axis_size("tp")
    group = 1
    while (
        kv_heads % (2 * group) == 0
        and count % (2 * group) == 0
        and WINDOW_LENGTH % (2 * group * tokens) == 0
    ):
        group *= 2
    heads = kv_heads // group
    kv_width = heads * HEAD_SIZE
    back_groups = WINDOW_LENGTH // (group * tokens)

    def trade(sent):
        return [sent[0]] + [swapped(sent[r], "ctx", r) for r in range(1, group)]

    def returned(earlier):
        return [
            shifted(earlier[number], "ctx", -group * (back_groups - number)) for number in range(back_groups)
        ]

    sent = pack_kv(group, keys, values, begin())
    kv_pieces = trade(sent)
    z = Shape(group, back_groups, heads, per_head, tokens)
    query_sent = pack_queries(group, queries, sent[0])
    if tp_count == 2:
        other = head_product(2, 1, out_weight, layer_cotangent, [query_sent[0]])
    else:
        other = head_product(1, 0, out_weight, layer_cotangent, [query_sent[0]])
    kv_own = order_pieces(group, kv_pieces, other)
    kv_earlier = [shifted(kv_own, "ctx", group * step) for step in range(back_groups, 0, -1)]
    if tp_count == 2:
        terms = [head_product(2, 0, out_weight, layer_cotangent, [kv_own, other]), swapped(other, "tp", 1)]
    else:
        terms = [lax.psum_scatter(other, "tp", scatter_dimension=0, tiled=True)]
    qt = turn_queries(z, trade(query_sent))
    grads = trade(pack_grads(group, terms, kv_own))
    e, inverse = softmax(z, kv_own, kv_earlier, qt)
    g, dv_own, dv_earlier = value_terms(z, e, inverse, grads)
    dv_terms = [dv_own] + returned(dv_earlier)
    ds, dk_own, dk_earlier = key_terms(z, e, inverse, qt, g, kv_own, kv_earlier)
    dk_terms = [dk_own] + returned(dk_earlier)
    pieces = trade(query_terms(z, ds, inverse, kv_own, kv_earlier, dv_terms))
    query_grads, value_gradients, done = unpack(group, pieces, [z.width, kv_width])
    key_gradients, _ = unpack(group, trade(pack_terms(group, [dk_terms])), [kv_width], [done])
    return (query_grads, key_gradients, value_gradients)


def solution(mesh):
    in_specs = (P("ctx", "tp"), P(None, "tp"), P("ctx", "tp"), P("ctx", "tp"), P("ctx", "tp"))
    out_specs = (P("ctx", "tp"), P("ctx", "tp"), P("ctx", "tp"))
    return jax.shard_map(local, mesh=mesh, in_specs=in_specs, out_specs=out_specs, check_vma=False)
```
